256 devices in a mesh: dp: 32 (over z, y_lo, core), seq: 8 (over y_hi, x).
Axes of the slice: x: 4, y: 4 (y_hi: 2, y_lo: 2; y = y_hi * 2 + y_lo), z: 8, core: 2. Of those that a mesh axis runs over, the one named last changes fastest.
Arguments:
- tokens: bfloat16 [65536, 1024], P(('dp', 'seq')), may hold values from -40 to 40
- lengths: int32 [32, 4], P('dp'), may hold values from 1 to 1024, 2048 in all within a row
- in_weight: bfloat16 [1024, 4096], P(('dp', 'seq')), may hold values from -0.1875 to 0.1875
- out_weight: bfloat16 [1024, 1024], P(('dp', 'seq')), may hold values from -0.1875 to 0.1875
- cotangent: bfloat16 [65536, 1024], P(('dp', 'seq')), may hold values from -6 to 6
Outputs:
- layer_out: bfloat16 [65536, 1024], P(('dp', 'seq'))
- tokens_grad: bfloat16 [65536, 1024], P(('dp', 'seq'))
- in_weight_grad: float32 [1024, 4096], P(('dp', 'seq'))
- out_weight_grad: float32 [1024, 1024], P(('dp', 'seq'))
The draws below stay inside these ranges and needn't reach their ends.
Inputs may be any that keep to these rules, and one draw needn't show every extreme that they name: Row g holds the lengths of the 4 histories of group g, which fill its 2048 positions; the longest of every row is exactly 1024.
All inputs are finite; a program needn't handle non-finite values.
Results may differ from the reference program's by a relative error of at most 0.034.
Values may be sent and summed in bfloat16 or wider, within the bound.
A program may use at most 128 MiB of HBM per device.

```python
import math
import jax
import jax.numpy as jnp
import numpy as np
from jax import lax

D = 1024
H = 8
HD = 128
TOK_DEV = 256
SEQS = 4
S_GRP = 2048
MOST = 1024
TOKENS = 65536
N_DP = 32
N_SEQ = 8


def draw_tokens(key, part):
    key = jax.random.fold_in(key, 7)
    key_rows, key_cols, key_values = jax.random.split(key, 3)
    row_scale = jnp.exp(jax.random.uniform(key_rows, (TOKENS, 1), jnp.float32, -1.15, 1.15))
    col_scale = jnp.exp(jax.random.uniform(key_cols, (1, D), jnp.float32, -1.15, 1.15))
    values = jnp.clip(jax.random.normal(key_values, (TOKENS, D), jnp.float32), -4.0, 4.0)
    return (values * row_scale * col_scale).astype(jnp.bfloat16)


def block_levels(rng, shape, shards, least, high):
    factor_of, own = 1.0, jax.random.fold_in(rng, 6)
    for dim, blocks in shards:
        heights = jnp.exp(jax.random.uniform(jax.random.fold_in(own, dim), (blocks,), jnp.float32, least / len(shards), high / len(shards)))
        factor_of = factor_of * jnp.repeat(heights, shape[dim] // blocks).reshape([-1 if axis == dim else 1 for axis in range(len(shape))])
    return factor_of


def length_profile(number_of, total, reach, lean):
    portions = [(1 << 20) // math.isqrt(rank ** lean) + 1 for rank in range(2, number_of + 1)]
    spare, holding = total - reach - (number_of - 1), [1] * (number_of - 1)
    while spare > 0:
        movable = [i for i in range(number_of - 1) if holding[i] < reach]
        mass, left = sum([portions[i] for i in movable]), spare
        for i in movable:
            more = min(reach - holding[i], max(1, left * portions[i] // mass), spare)
            holding[i] = holding[i] + more
            spare = spare - more
    return np.array([reach] + holding)


def uneven_parts(own_key, amount, total, reach, slope):
    if amount == 2:
        one = jax.random.randint(own_key, (), max(1, total - reach), min(reach, total - 1) + 1)
        return jnp.stack([one, total - one])
    tallies = jnp.asarray(length_profile(amount, total, reach, slope), jnp.int32)
    couples = (amount - 1) // 2
    donor, taker = tallies[1:1 + 2 * couples:2], tallies[2:2 + 2 * couples:2]
    margin = jnp.minimum(donor - 1, reach - taker)
    passed = jax.random.randint(jax.random.fold_in(own_key, 1), (couples,), 0, 1 << 20) % (margin + 1)
    tallies = tallies.at[1:1 + 2 * couples:2].set(donor - passed).at[2:2 + 2 * couples:2].set(taker + passed)
    return tallies[jax.random.permutation(jax.random.fold_in(own_key, 2), amount)]


def normal_values(rng, extent, width, reach, cuts=(), kind=jnp.bfloat16):
    gain = block_levels(rng, extent, cuts, -0.22, 0.18) if cuts else 1.0
    values = jax.random.normal(rng, extent, jnp.float32) * width * gain
    return jnp.minimum(jnp.maximum(values, -reach), reach).astype(kind)


def setup_inputs(seed: int = 0) -> dict:
    streams_of = jax.random.split(jax.random.key(seed), 6)
    tokens = draw_tokens(jax.random.fold_in(streams_of[5], 71), 0)
    lengths = jax.vmap(lambda own: uneven_parts(own, SEQS, S_GRP, MOST, 2))(jax.random.split(streams_of[1], N_DP)).reshape((N_DP, SEQS)).astype(jnp.int32)
    in_weight = normal_values(streams_of[2], (D, 4 * D), D ** -0.5, 0.1875, ((0, 256),))
    out_weight = normal_values(streams_of[3], (D, D), D ** -0.5, 0.1875, ((0, 256),))
    cotangent = normal_values(streams_of[4], (TOKENS, D), 1.0, 6.0, ((0, 256),))
    return {"tokens": tokens, "lengths": lengths, "in_weight": in_weight, "out_weight": out_weight, "cotangent": cotangent}


epsilon = 1e-05

def normalize(values):
    centre = values - lax.optimization_barrier(jnp.mean(values, axis=-1, keepdims=True))
    inverse = lax.rsqrt(lax.optimization_barrier(jnp.mean(centre * centre, axis=-1, keepdims=True)) + epsilon)
    return (centre * inverse, inverse)

def norm_back(upstream, normed, inverse):
    first = lax.optimization_barrier(jnp.mean(upstream, axis=-1, keepdims=True))
    second = lax.optimization_barrier(jnp.mean(upstream * normed, axis=-1, keepdims=True))
    return inverse * (upstream - first - normed * second)

def head_masks(segments):
    position = jnp.arange(segments.shape[0], dtype=jnp.int32)
    same_seg = segments[:, None] == segments[None, :]
    causal = position[None, :] <= position[:, None]
    return same_seg & causal

def head_forward(queries, keys, values, segments):
    factor = HD ** (-0.5)
    scores = jnp.dot(queries.astype(jnp.float32), keys.astype(jnp.float32).T) * factor
    allowed = head_masks(segments)
    weights = jnp.where(allowed, jax.nn.silu(scores), 0.0).astype(jnp.bfloat16)
    return jnp.dot(weights.astype(jnp.float32), values.astype(jnp.float32)).astype(jnp.bfloat16)

def head_backward(queries, keys, values, d_attn, segments):
    factor = HD ** (-0.5)
    scores = jnp.dot(queries.astype(jnp.float32), keys.astype(jnp.float32).T) * factor
    allowed = head_masks(segments)
    sigma = jax.nn.sigmoid(scores)
    weights = jnp.where(allowed, jax.nn.silu(scores), 0.0).astype(jnp.bfloat16)
    d_upper = d_attn.astype(jnp.float32)
    d_weights = jnp.dot(d_upper, values.astype(jnp.float32).T)
    d_scores = (jnp.where(allowed, d_weights * sigma * (1.0 + scores * (1.0 - sigma)), 0.0) * factor).astype(jnp.bfloat16)
    d_scores32 = d_scores.astype(jnp.float32)
    grad_values = jnp.dot(weights.astype(jnp.float32).T, d_upper).astype(jnp.bfloat16)
    grad_queries = jnp.dot(d_scores32, keys.astype(jnp.float32)).astype(jnp.bfloat16)
    grad_keys = jnp.dot(d_scores32.T, queries.astype(jnp.float32)).astype(jnp.bfloat16)
    return (grad_values, grad_queries, grad_keys)

def split_heads(block):
    return block.reshape(S_GRP, H, HD).transpose(1, 0, 2)

def join_heads(stacked):
    return stacked.transpose(1, 0, 2).reshape(S_GRP, D)

def group_forward(packed):
    gated_group, segments = packed
    values = split_heads(gated_group[:, D:2 * D])
    queries = split_heads(gated_group[:, 2 * D:3 * D])
    keys = split_heads(gated_group[:, 3 * D:])

    def one_head(trio):
        return head_forward(trio[1], trio[2], trio[0], segments)
    return join_heads(lax.map(one_head, (values, queries, keys)))

def group_backward(packed):
    gated_group, d_group, segments = packed
    values = split_heads(gated_group[:, D:2 * D])
    queries = split_heads(gated_group[:, 2 * D:3 * D])
    keys = split_heads(gated_group[:, 3 * D:])
    d_heads = split_heads(d_group)

    def one_head(quad):
        return head_backward(quad[1], quad[2], quad[0], quad[3], segments)
    grad_values, grad_queries, grad_keys = lax.map(one_head, (values, queries, keys, d_heads))
    return jnp.concatenate([join_heads(grad_values), join_heads(grad_queries), join_heads(grad_keys)], axis=1)

def block_partials(left, right):
    left_blocks = left.reshape(N_DP, N_SEQ, TOK_DEV, left.shape[1])
    right_blocks = right.reshape(N_DP, N_SEQ, TOK_DEV, right.shape[1])
    zeros = jnp.zeros((left.shape[1], right.shape[1]), jnp.float32)

    def member_add(outer, member):

        def group_add(summed, group):
            part = jnp.dot(left_blocks[group, member].astype(jnp.float32).T, right_blocks[group, member].astype(jnp.float32))
            rounded = lax.optimization_barrier(part.astype(jnp.bfloat16)).astype(jnp.float32)
            return (summed + rounded, None)
        summed, unused = lax.scan(group_add, zeros, jnp.arange(N_DP, dtype=jnp.int32))
        return (outer + summed, None)
    result, unused = lax.scan(member_add, zeros, jnp.arange(N_SEQ, dtype=jnp.int32))
    return result

def reference(tokens, lengths, in_weight, out_weight, cotangent):
    token_f = tokens.astype(jnp.float32)
    normed_in, rstd_in = normalize(token_f)
    normed_bf = normed_in.astype(jnp.bfloat16)
    hidden = jnp.dot(normed_bf.astype(jnp.float32), in_weight.astype(jnp.float32))
    gated = jax.nn.silu(hidden).astype(jnp.bfloat16)
    position = jnp.arange(S_GRP, dtype=jnp.int32)
    ends = jnp.cumsum(lengths, axis=1).astype(jnp.int32)
    segments = lax.optimization_barrier(jnp.sum((position[None, :, None] >= ends[:, None, :-1]).astype(jnp.int32), axis=2)).astype(jnp.int32)
    gated_groups = gated.reshape(N_DP, S_GRP, 4 * D)
    attn = lax.map(group_forward, (gated_groups, segments)).reshape(TOKENS, D)
    normed_out, rstd_out = normalize(attn.astype(jnp.float32))
    upper = gated[:, :D].astype(jnp.float32)
    mixed = (normed_out * upper).astype(jnp.bfloat16)
    layer_out = (jnp.dot(mixed.astype(jnp.float32), out_weight.astype(jnp.float32)) + token_f).astype(jnp.bfloat16)
    cot_f = cotangent.astype(jnp.float32)
    d_mixed = jnp.dot(cot_f, out_weight.astype(jnp.float32).T)
    d_attn = norm_back(d_mixed * upper, normed_out, rstd_out).astype(jnp.bfloat16)
    d_trio = lax.map(group_backward, (gated_groups, d_attn.reshape(N_DP, S_GRP, D), segments)).reshape(TOKENS, 3 * D)
    d_gated = jnp.concatenate([d_mixed * normed_out, d_trio.astype(jnp.float32)], axis=1)
    sigma = jax.nn.sigmoid(hidden)
    d_hidden = (d_gated * sigma * (1.0 + hidden * (1.0 - sigma))).astype(jnp.bfloat16)
    d_normed = jnp.dot(d_hidden.astype(jnp.float32), in_weight.astype(jnp.float32).T)
    tokens_grad = (norm_back(d_normed, normed_in, rstd_in) + cot_f).astype(jnp.bfloat16)
    in_weight_grad = block_partials(normed_bf, d_hidden)
    out_weight_grad = block_partials(mixed, cotangent)
    return (layer_out, tokens_grad, in_weight_grad, out_weight_grad)
```

```python
import functools

import jax
import jax.numpy as jnp
from jax import lax
from jax.experimental import pallas as pl
from jax.experimental.pallas import tpu as pltpu
from jax.sharding import PartitionSpec as P

F32 = jnp.float32
BF16 = jnp.bfloat16
MESH = pl.DeviceIdType.MESH
DMA = pltpu.SemaphoreType.DMA

D = 1024
HEADS = 8
HD = 128
ROWS = 256
NZ = 8
epsilon = 1e-05
HALF_FACTOR = 0.5 * HD ** (-0.5)
VMEM = pl.BlockSpec(memory_space=pltpu.VMEM)
ABT = (((1,), (1,)), ((), ()))
ATB = (((0,), (0,)), ((), ()))


def dot(a, b, dims=(((1,), (0,)), ((), ()))):
    return lax.dot_general(a, b, dims, preferred_element_type=F32)


class Place:
    def __init__(self):
        g = lax.axis_index("dp")
        s = lax.axis_index("seq")
        self.z, self.ylo, self.k = g // 4, (g // 2) % 2, g % 2
        self.yhi, self.x = s // 4, s % 4
        self.w = self.k * 4 + self.x
        self.head = 2 * self.x + self.k
        self.moved = self.k != self.yhi

    def device(self, z=None, ylo=None, k=None, yhi=None, x=None):
        z = self.z if z is None else z
        ylo = self.ylo if ylo is None else ylo
        k = self.k if k is None else k
        yhi = self.yhi if yhi is None else yhi
        x = self.x if x is None else x
        return (z * 4 + ylo * 2 + k, yhi * 4 + x)

    def row(self, dk, dx):
        return (self.k + dk) % 2, (self.x + dx) % 4

    def along_z(self, d):
        return (self.z + d) % NZ

    def along_y(self, d):
        y = (self.yhi * 2 + self.ylo + d) % 4
        return y // 2, y % 2

    def partner(self):
        return self.device(k=self.yhi, yhi=self.k)

    def sibling(self):
        return self.device(k=1 - self.k)

    def row_peers(self):
        peers = []
        for d in range(1, 8):
            k, x = self.row(d // 4, d % 4)
            peers.append(self.device(k=k, x=x))
        return peers

    def zy_peers(self):
        peers = [self.device(z=self.along_z(d)) for d in range(1, NZ)]
        for d in range(1, 4):
            yhi, ylo = self.along_y(d)
            peers.append(self.device(ylo=ylo, yhi=yhi))
        return peers


def greet(me, peers, with_partner):
    barrier = pltpu.get_barrier_semaphore()
    for peer in peers:
        pl.semaphore_signal(barrier, inc=1, device_id=peer, device_id_type=MESH)
    if with_partner:

        @pl.when(me.moved)
        def _():
            pl.semaphore_signal(barrier, inc=1, device_id=me.partner(), device_id_type=MESH)

    if with_partner:
        pl.semaphore_wait(barrier, len(peers) + me.moved.astype(jnp.int32))
    else:
        pl.semaphore_wait(barrier, len(peers))


def copy(src, dst, send, recv, to):
    return pltpu.make_async_remote_copy(
        src_ref=src, dst_ref=dst, send_sem=send, recv_sem=recv, device_id=to, device_id_type=MESH
    )


class Sends:
    def __init__(self):
        self.started = []

    def push(self, src, dst, send, recv, to):
        one = copy(src, dst, send, recv, to)
        one.start()
        self.started.append(one)

    def drain(self):
        for one in self.started:
            one.wait_send()


def arrived(ref, send, recv, me):
    copy(ref, ref, send, recv, me.sibling()).wait_recv()


def normalize(values):
    centre = values - jnp.mean(values, axis=-1, keepdims=True)
    inverse = lax.rsqrt(jnp.mean(centre * centre, axis=-1, keepdims=True) + epsilon)
    return centre * inverse, inverse


def gather_kernel(
    tok, cot, wi, wo, lens,
    normed, gated, slope, win, wout, dmix, tokr, cotr, lens_out,
    wi_f, wi_send, wi_recv, wi_asm, wo_f, wo_send, wo_recv, wo_asm, dsend, len_send, len_recv,
    swap_s, swap_r, xi_s, xi_r, xo_s, xo_r, zi_s, zi_r, zo_s, zo_r, yi_s, yi_r, yo_s, yo_r, core_s, core_r,
    ag_s, ag_r, fw_s, dm_s, dm_r,
):
    me = Place()
    z, ylo, k, yhi, x, w = me.z, me.ylo, me.k, me.yhi, me.x, me.w
    sends = Sends()
    greet(me, me.row_peers() + me.zy_peers(), True)

    swap_tok = copy(tok, tokr, swap_s.at[0], swap_r.at[0], me.partner())
    swap_cot = copy(cot, cotr, swap_s.at[1], swap_r.at[1], me.partner())

    @pl.when(me.moved)
    def _():
        swap_tok.start()

    @pl.when(jnp.logical_not(me.moved))
    def _():
        tokr[...] = tok[...]
        cotr[...] = cot[...]

    len_send[...] = jnp.zeros_like(len_send)
    len_send[0:1, 0:4] = lens[...]
    sends.push(len_send, len_recv, swap_s.at[2], swap_r.at[2], me.sibling())

    wide = wi[...].astype(F32)
    for h in range(HEADS):
        for b in range(4):
            wi_f[h, b * 4 : b * 4 + 4, :] = wide[:, b * D + h * HD : b * D + (h + 1) * HD]
    wi_send[...] = wi_f[...].astype(BF16)
    for d in range(1, 8):
        pk, px = me.row(d // 4, d % 4)
        sends.push(
            wi_send.at[2 * px + pk], wi_recv.at[w], xi_s.at[d - 1], xi_r.at[d - 1], me.device(k=pk, x=px)
        )
    wi_recv[w] = wi_send[me.head]
    wide_o = wo[...].astype(F32)
    for b in range(8):
        wo_f[b * 4 : b * 4 + 4, :] = wide_o[:, b * HD : (b + 1) * HD]
    wo_send[...] = wo_f[...].astype(BF16)
    for d in range(1, 4):
        pk, px = me.row(0, d)
        sends.push(wo_send, wo_recv.at[x], xo_s.at[d - 1], xo_r.at[d - 1], me.device(x=px))
    wo_recv[x] = wo_send[...]

    def norm_own():
        normed[w] = normalize(tokr[...].astype(F32))[0].astype(BF16)

    def send_own():
        right, left = me.device(x=(x + 1) % 4), me.device(x=(x + 3) % 4)
        for step in range(2):
            for to, half, slot in ((right, step, 3), (left, 1 - step, 1)):
                part = normed.at[w, pl.ds(half * 128, 128)]
                sends.push(part, part, ag_s.at[slot, half], ag_r.at[slot, half], to)
        for half in range(2):
            part = normed.at[w, pl.ds(half * 128, 128)]
            sends.push(part, part, fw_s.at[0, half], ag_r.at[4, half], me.sibling())

    @pl.when(jnp.logical_not(me.moved))
    def _():
        norm_own()

    for d in range(1, 8):
        pk, px = me.row(d // 4, d % 4)
        sk, sx = (k + 2 - d // 4) % 2, (x + 4 - d % 4) % 4
        arrived(wi_recv.at[sk * 4 + sx], xi_s.at[d - 1], xi_r.at[d - 1], me)
    for src in range(8):
        piece = wi_recv[src].astype(F32)
        for b in range(4):
            wi_asm[src // 4, (src % 4) * 4 : (src % 4) * 4 + 4, b * HD : (b + 1) * HD] = piece[b * 4 : b * 4 + 4]
    for c in range(2):
        win[z, ylo, c, yhi] = wi_asm[c].astype(BF16)
    for d in range(1, NZ):
        part = win.at[z, ylo, :, yhi]
        sends.push(part, part, zi_s.at[d - 1], zi_r.at[d - 1], me.device(z=me.along_z(d)))

    @pl.when(me.moved)
    def _():
        swap_tok.wait_recv()
        norm_own()

    send_own()

    @pl.when(me.moved)
    def _():
        swap_cot.start()

    for d in range(1, 4):
        arrived(wo_recv.at[(x + 4 - d) % 4], xo_s.at[d - 1], xo_r.at[d - 1], me)
    for src in range(4):
        piece = wo_recv[src].astype(F32)
        for b in range(8):
            wo_asm[src * 4 : src * 4 + 4, b * HD : (b + 1) * HD] = piece[b * 4 : b * 4 + 4]
    wout[z, ylo, k, yhi] = wo_asm[...].astype(BF16)
    for d in range(1, NZ):
        part = wout.at[z, ylo, k, yhi]
        sends.push(part, part, zo_s.at[d - 1], zo_r.at[d - 1], me.device(z=me.along_z(d)))

    def rows_of(dx, half):
        return normed.at[k * 4 + (x + dx) % 4, pl.ds(half * 128, 128)]

    def take(dx, half):
        part = rows_of(dx, half)
        arrived(part, ag_s.at[dx, half], ag_r.at[dx, half], me)
        sends.push(part, part, fw_s.at[dx, half], ag_r.at[4 + dx, half], me.sibling())

    take(3, 0)
    part = rows_of(3, 0)
    sends.push(part, part, ag_s.at[2, 0], ag_r.at[2, 0], me.device(x=(x + 1) % 4))
    take(1, 1)
    part = rows_of(1, 1)
    sends.push(part, part, ag_s.at[2, 1], ag_r.at[2, 1], me.device(x=(x + 3) % 4))

    for d in range(1, NZ):
        arrived(win.at[(z + NZ - d) % NZ, ylo, :, yhi], zi_s.at[d - 1], zi_r.at[d - 1], me)
    for d in range(1, 4):
        phi, plo = me.along_y(d)
        part = win.at[:, ylo, :, yhi]
        sends.push(part, part, yi_s.at[d - 1], yi_r.at[d - 1], me.device(ylo=plo, yhi=phi))
    take(3, 1)
    take(1, 0)
    for d in range(1, NZ):
        arrived(wout.at[(z + NZ - d) % NZ, ylo, k, yhi], zo_s.at[d - 1], zo_r.at[d - 1], me)
    for d in range(1, 4):
        phi, plo = me.along_y(d)
        part = wout.at[:, ylo, k, yhi]
        sends.push(part, part, yo_s.at[d - 1], yo_r.at[d - 1], me.device(ylo=plo, yhi=phi))
    take(2, 0)
    take(2, 1)
    for d in range(1, 4):
        shi, slo = me.along_y(4 - d)
        arrived(win.at[:, slo, :, shi], yi_s.at[d - 1], yi_r.at[d - 1], me)

    def project(block):
        left = normed[block]
        for n in range(2):
            cols = pl.ds(n * 256, 256)
            hidden = dot(left, win[:, :, :, :, :, cols].reshape(D, 256))
            sigma = 0.5 + 0.5 * jnp.tanh(0.5 * hidden)
            value = hidden * sigma
            gated[block, :, cols] = value.astype(BF16)
            slope[block, :, cols] = (sigma + value * (1.0 - sigma)).astype(BF16)

    @pl.loop(0, 4)
    def _(i):
        project(k * 4 + i)

    for dx in range(4):
        for half in range(2):
            arrived(
                normed.at[(1 - k) * 4 + (x + dx) % 4, pl.ds(half * 128, 128)],
                fw_s.at[dx, half], ag_r.at[4 + dx, half], me,
            )

    @pl.loop(0, 4)
    def _(i):
        project((1 - k) * 4 + i)

    for d in range(1, 4):
        shi, slo = me.along_y(4 - d)
        arrived(wout.at[:, slo, k, shi], yo_s.at[d - 1], yo_r.at[d - 1], me)
    sends.push(wout.at[:, :, k], wout.at[:, :, k], core_s, core_r, me.sibling())

    @pl.when(me.moved)
    def _():
        swap_cot.wait_recv()

    arrived(wout.at[:, :, 1 - k], core_s, core_r, me)

    @pl.loop(0, 4)
    def _(i):
        pair = dot(cotr[...], wout[pl.ds(2 * i, 2)].reshape(256, D), ABT)
        dsend[2 * i] = pair[:, :HD].astype(BF16)
        dsend[2 * i + 1] = pair[:, HD:].astype(BF16)

    dmix[w] = dsend[me.head]
    for d in range(1, 8):
        pk, px = me.row(d // 4, d % 4)
        sends.push(dsend.at[2 * px + pk], dmix.at[w], dm_s.at[d - 1], dm_r.at[d - 1], me.device(k=pk, x=px))
    for d in range(1, 8):
        sk, sx = (k + 2 - d // 4) % 2, (x + 4 - d % 4) % 4
        arrived(dmix.at[sk * 4 + sx], dm_s.at[d - 1], dm_r.at[d - 1], me)
    arrived(len_recv, swap_s.at[2], swap_r.at[2], me)
    lens_out[...] = jnp.where(me.moved, len_recv[...], len_send[...])
    sends.drain()

    @pl.when(me.moved)
    def _():
        swap_tok.wait_send()
        swap_cot.wait_send()


def run_gather(tok, cot, wi, wo, lens):
    shapes = [
        ((8, ROWS, D), BF16), ((8, ROWS, 512), BF16), ((8, ROWS, 512), BF16),
        ((NZ, 2, 2, 2, 16, 512), BF16), ((NZ, 2, 2, 2, 16, D), BF16), ((8, ROWS, HD), BF16),
        ((ROWS, D), BF16), ((ROWS, D), BF16), ((8, 128), jnp.int32),
    ]
    scratch = [
        pltpu.VMEM((8, 16, 128), F32), pltpu.VMEM((8, 16, 128), BF16), pltpu.VMEM((8, 16, 128), BF16),
        pltpu.VMEM((2, 16, 512), F32),
        pltpu.VMEM((32, 128), F32), pltpu.VMEM((32, 128), BF16), pltpu.VMEM((4, 32, 128), BF16),
        pltpu.VMEM((16, D), F32), pltpu.VMEM((8, ROWS, HD), BF16),
        pltpu.VMEM((8, 128), jnp.int32), pltpu.VMEM((8, 128), jnp.int32),
        DMA((3,)), DMA((3,)), DMA((7,)), DMA((7,)), DMA((3,)), DMA((3,)),
        DMA((7,)), DMA((7,)), DMA((7,)), DMA((7,)), DMA((3,)), DMA((3,)), DMA((3,)), DMA((3,)), DMA, DMA,
        DMA((4, 2)), DMA((8, 2)), DMA((4, 2)), DMA((7,)), DMA((7,)),
    ]
    return pl.pallas_call(
        gather_kernel,
        out_shape=[jax.ShapeDtypeStruct(s, t) for s, t in shapes],
        in_specs=[VMEM] * 5,
        out_specs=[VMEM] * len(shapes),
        scratch_shapes=scratch,
        compiler_params=pltpu.CompilerParams(
            collective_id=0, has_side_effects=True, vmem_limit_bytes=48 << 20
        ),
        name="gather",
    )(tok, cot, wi, wo, lens)


def first_of(position, lens):
    e0 = lens[0:1, 0:1]
    e1 = e0 + lens[0:1, 1:2]
    e2 = e1 + lens[0:1, 2:3]
    zero = jnp.zeros_like(position)
    start = jnp.where(position >= e0, e0, zero)
    start = jnp.where(position >= e1, e1, start)
    return jnp.where(position >= e2, e2, start)


def attend_kernel(gated, dmix, lens, attn, stats):
    def block(i, reach):
        query = gated[i, :, 256:384]
        pos = i * ROWS + lax.broadcasted_iota(jnp.int32, (ROWS, 1), 0)
        start = first_of(pos, lens)
        total = jnp.zeros((ROWS, HD), F32)
        for off in range(reach + 1):
            j = i - off
            half = dot(query, gated[j, :, 384:512], ABT) * HALF_FACTOR
            weights = half + half * jnp.tanh(half)
            other = j * ROWS + lax.broadcasted_iota(jnp.int32, (ROWS, ROWS), 1)
            allowed = other >= start
            if off == 0:
                allowed = allowed & (other <= pos)
            weights = jnp.where(allowed, weights, 0.0).astype(BF16)
            total = total + dot(weights, gated[j, :, 128:256])
        rounded = total.astype(BF16)
        attn[i] = rounded
        value = rounded.astype(F32)
        upstream = dmix[i].astype(F32) * gated[i, :, 0:128].astype(F32)
        mean = jnp.mean(value, axis=-1, keepdims=True)
        centre = value - mean
        parts = (
            mean,
            jnp.sum(centre * centre, axis=-1, keepdims=True),
            jnp.sum(upstream, axis=-1, keepdims=True),
            jnp.sum(upstream * centre, axis=-1, keepdims=True),
        )
        lane = lax.broadcasted_iota(jnp.int32, (ROWS, HD), 1)
        packed = jnp.zeros((ROWS, HD), F32)
        for n, part in enumerate(parts):
            packed = jnp.where(lane == n, part, packed)
        stats[i] = packed.T[0:8]

    for i in range(4):
        block(i, i)

    @pl.loop(4, 8)
    def _(i):
        block(i, 4)


def run_attend(gated, dmix, lens):
    return pl.pallas_call(
        attend_kernel,
        out_shape=[jax.ShapeDtypeStruct((8, ROWS, HD), BF16), jax.ShapeDtypeStruct((8, 8, ROWS), F32)],
        in_specs=[VMEM] * 3,
        out_specs=[VMEM] * 2,
        compiler_params=pltpu.CompilerParams(vmem_limit_bytes=32 << 20),
        name="attend",
    )(gated, dmix, lens)


def middle_kernel(
    attn, stats, gated, slope, dmix, dattn, dupper, mixed, every, comb, msend, st_s, st_r, mx_s, mx_r
):
    me = Place()
    k, x, w = me.k, me.x, me.w
    sends = Sends()
    greet(me, me.row_peers(), False)
    for d in range(1, 8):
        pk, px = me.row(d // 4, d % 4)
        sends.push(stats, every.at[w], st_s.at[d - 1], st_r.at[d - 1], me.device(k=pk, x=px))
    every[w] = stats[...]
    for d in range(1, 8):
        sk, sx = (k + 2 - d // 4) % 2, (x + 4 - d % 4) % 4
        arrived(every.at[sk * 4 + sx], st_s.at[d - 1], st_r.at[d - 1], me)

    def block(i):
        mean, second, total, cross = (every[:, i, n, :] for n in range(4))
        middle = jnp.mean(mean, axis=0, keepdims=True)
        apart = mean - middle
        variance = jnp.sum(second + HD * apart * apart, axis=0, keepdims=True) / D
        inverse = lax.rsqrt(variance + epsilon)
        first = jnp.sum(total, axis=0, keepdims=True) / D
        other = inverse * jnp.sum(cross + apart * total, axis=0, keepdims=True) / D
        comb[0:1, :] = middle
        comb[1:2, :] = inverse
        comb[2:3, :] = first
        comb[3:4, :] = other
        turned = comb[...].T
        middle, inverse, first, other = (turned[:, n : n + 1] for n in range(4))
        upper = gated[i, :, 0:128].astype(F32)
        through = dmix[i].astype(F32)
        normal = (attn[i].astype(F32) - middle) * inverse
        msend[i] = (normal * upper).astype(BF16)
        upstream = through * upper
        dattn[i] = (inverse * (upstream - first - normal * other)).astype(BF16)
        dupper[i] = (through * normal * slope[i, :, 0:128].astype(F32)).astype(BF16)

    comb[...] = jnp.zeros_like(comb)

    @pl.loop(0, 8)
    def _(i):
        block(i)

    mixed[me.head] = msend[w]
    for d in range(1, 8):
        pk, px = me.row(d // 4, d % 4)
        sends.push(msend.at[pk * 4 + px], mixed.at[me.head], mx_s.at[d - 1], mx_r.at[d - 1], me.device(k=pk, x=px))
    for d in range(1, 8):
        sk, sx = (k + 2 - d // 4) % 2, (x + 4 - d % 4) % 4
        arrived(mixed.at[2 * sx + sk], mx_s.at[d - 1], mx_r.at[d - 1], me)
    sends.drain()


def run_middle(attn, stats, gated, slope, dmix):
    shape = jax.ShapeDtypeStruct((8, ROWS, HD), BF16)
    return pl.pallas_call(
        middle_kernel,
        out_shape=[shape] * 3,
        in_specs=[VMEM] * 5,
        out_specs=[VMEM] * 3,
        scratch_shapes=[
            pltpu.VMEM((8, 8, 8, ROWS), F32), pltpu.VMEM((128, ROWS), F32), pltpu.VMEM((8, ROWS, HD), BF16),
            DMA((7,)), DMA((7,)), DMA((7,)), DMA((7,)),
        ],
        compiler_params=pltpu.CompilerParams(
            collective_id=1, has_side_effects=True, vmem_limit_bytes=32 << 20
        ),
        name="middle",
    )(attn, stats, gated, slope, dmix)


def back_kernel(gated, slope, dattn, dupper, lens, dhidden, dquery):
    dquery[...] = jnp.zeros_like(dquery)
    dhidden[:, :, 0:128] = dupper[...]

    def block(j, reach):
        key = gated[j, :, 384:512]
        value = gated[j, :, 128:256]
        other = j * ROWS + lax.broadcasted_iota(jnp.int32, (ROWS, ROWS), 0)
        dkey = jnp.zeros((ROWS, HD), F32)
        dvalue = jnp.zeros((ROWS, HD), F32)
        for off in range(reach + 1):
            i = j + off
            query = gated[i, :, 256:384]
            grad = dattn[i]
            half = dot(key, query, ABT) * HALF_FACTOR
            pos = i * ROWS + lax.broadcasted_iota(jnp.int32, (1, ROWS), 1)
            allowed = other >= first_of(pos, lens)
            if off == 0:
                allowed = allowed & (other <= pos)
            double = jnp.where(allowed, 1.0 + jnp.tanh(half), 0.0)
            weights = half * double
            bend = double + weights * (2.0 - double)
            dscores = (dot(value, grad, ABT) * bend).astype(BF16)
            dvalue = dvalue + dot(weights.astype(BF16), grad)
            dkey = dkey + dot(dscores, query)
            dquery[i] += dot(dscores, key, ATB)
        dhidden[j, :, 128:256] = (dvalue * slope[j, :, 128:256].astype(F32)).astype(BF16)
        dhidden[j, :, 384:512] = (dkey * HALF_FACTOR * slope[j, :, 384:512].astype(F32)).astype(BF16)

    @pl.loop(0, 4)
    def _(j):
        block(j, 4)

    for j in range(4, 8):
        block(j, 7 - j)

    @pl.loop(0, 8)
    def _(i):
        dhidden[i, :, 256:384] = (dquery[i] * HALF_FACTOR * slope[i, :, 256:384].astype(F32)).astype(BF16)


def run_back(gated, slope, dattn, dupper, lens):
    return pl.pallas_call(
        back_kernel,
        out_shape=jax.ShapeDtypeStruct((8, ROWS, 512), BF16),
        in_specs=[VMEM] * 5,
        out_specs=VMEM,
        scratch_shapes=[pltpu.VMEM((8, ROWS, HD), F32)],
        compiler_params=pltpu.CompilerParams(vmem_limit_bytes=32 << 20),
        name="back",
    )(gated, slope, dattn, dupper, lens)


def reduce_kernel(
    normed, dhidden, win, wout, mixed, tokr, cotr,
    layer_out, tok_grad, wi_grad, wo_grad,
    lay, grad, esum, es_send, es_recv, x2_send, rl_recv, nb_send, nb_recv,
    gs, gy, gz_send, gz, gx_f, gx_recv, ps, pc, pk_sum, py, pz_send, pz, px_f, px_recv,
    sib_s, sib_r, rl_s, rl_r, nb_s, nb_r, gy_s, gy_r, gz_s, gz_r, gx_s, gx_r,
    pc_s, pc_r, py_s, py_r, pz_s, pz_r, px_s, px_r, sw_s, sw_r,
):
    me = Place()
    z, ylo, k, yhi, x, w = me.z, me.ylo, me.k, me.yhi, me.x, me.w
    sends = Sends()
    greet(me, me.row_peers() + me.zy_peers(), True)
    right, left = me.device(x=(x + 1) % 4), me.device(x=(x + 3) % 4)

    def back_product(block, n):
        return dot(dhidden[block], win[pl.ds(2 * n, 2)].reshape(256, 512), ABT)

    def partial(dx):
        there = (1 - k) * 4 + (x + dx) % 4
        here = k * 4 + (x + dx) % 4

        @pl.loop(0, 4)
        def _(n):
            cols = pl.ds(pl.multiple_of(n * 256, 256), 256)
            es_send[dx, :, cols] = back_product(there, n).astype(BF16)

        sends.push(es_send.at[dx], es_recv.at[dx], sib_s.at[dx], sib_r.at[dx], me.sibling())

        @pl.loop(0, 4)
        def _(n):
            cols = pl.ds(pl.multiple_of(n * 256, 256), 256)
            esum[dx, :, cols] = back_product(here, n)

    def from_sibling(dx):
        arrived(es_recv.at[dx], sib_s.at[dx], sib_r.at[dx], me)

    partial(2)
    partial(1)
    from_sibling(2)
    x2_send[...] = (esum[2] + es_recv[2].astype(F32)).astype(BF16)
    sends.push(x2_send.at[pl.ds(0, 128)], rl_recv.at[0], rl_s.at[0], rl_r.at[0], right)
    sends.push(x2_send.at[pl.ds(128, 128)], rl_recv.at[1], rl_s.at[1], rl_r.at[1], left)
    partial(3)

    from_sibling(1)
    nb_send[0, 128:256] = (esum[1, 128:256] + es_recv[1, 128:256].astype(F32)).astype(BF16)
    sends.push(nb_send.at[0, pl.ds(128, 128)], nb_recv.at[0, pl.ds(128, 128)], nb_s.at[0, 1], nb_r.at[0, 1], right)
    from_sibling(3)
    nb_send[1, 0:128] = (esum[3, 0:128] + es_recv[3, 0:128].astype(F32)).astype(BF16)
    sends.push(nb_send.at[1, pl.ds(0, 128)], nb_recv.at[1, pl.ds(0, 128)], nb_s.at[1, 0], nb_r.at[1, 0], left)

    @pl.loop(0, 4)
    def _(n):
        cols = pl.ds(pl.multiple_of(n * 256, 256), 256)
        product = dot(normed[:, :, cols].reshape(8 * ROWS, 256), dhidden[...].reshape(8 * ROWS, 512), ATB)
        gs[pl.ds(2 * n, 2)] = product.astype(BF16).reshape(2, 2, 2, 2, 16, 512)

    for d in range(1, 4):
        phi, plo = me.along_y(d)
        sends.push(gs.at[:, plo, :, phi], gy.at[d - 1], gy_s.at[d - 1], gy_r.at[d - 1], me.device(ylo=plo, yhi=phi))

    arrived(rl_recv.at[0], rl_s.at[0], rl_r.at[0], me)
    nb_send[0, 0:128] = (
        esum[1, 0:128] + es_recv[1, 0:128].astype(F32) + rl_recv[0].astype(F32)
    ).astype(BF16)
    sends.push(nb_send.at[0, pl.ds(0, 128)], nb_recv.at[0, pl.ds(0, 128)], nb_s.at[0, 0], nb_r.at[0, 0], right)
    arrived(rl_recv.at[1], rl_s.at[1], rl_r.at[1], me)
    nb_send[1, 128:256] = (
        esum[3, 128:256] + es_recv[3, 128:256].astype(F32) + rl_recv[1].astype(F32)
    ).astype(BF16)
    sends.push(nb_send.at[1, pl.ds(128, 128)], nb_recv.at[1, pl.ds(128, 128)], nb_s.at[1, 1], nb_r.at[1, 1], left)
    partial(0)

    @pl.loop(0, 4)
    def _(n):
        pair = jnp.concatenate([mixed[2 * n], mixed[2 * n + 1]], axis=1)
        product = dot(pair, cotr[...], ATB)
        ps[pl.ds(2 * n, 2)] = product.astype(BF16).reshape(2, 2, 2, 2, 16, D)

    sends.push(ps.at[:, :, 1 - k], pc, pc_s, pc_r, me.sibling())

    joined = jnp.concatenate([mixed[h] for h in range(HEADS)], axis=1)
    for n in range(4):
        cols = pl.ds(n * 256, 256)
        product = dot(joined, wout[:, :, :, :, :, cols].reshape(D, 256))
        lay[:, cols] = (product + tokr[:, cols].astype(F32)).astype(BF16)
    swap_lay = copy(lay, layer_out, sw_s.at[0], sw_r.at[0], me.partner())
    swap_grad = copy(grad, tok_grad, sw_s.at[1], sw_r.at[1], me.partner())

    @pl.when(me.moved)
    def _():
        swap_lay.start()

    @pl.when(jnp.logical_not(me.moved))
    def _():
        layer_out[...] = lay[...]

    arrived(pc, pc_s, pc_r, me)

    @pl.loop(0, NZ)
    def _(n):
        pk_sum[n] = (ps[n, :, k].astype(F32) + pc[n].astype(F32)).astype(BF16)

    for d in range(1, 4):
        phi, plo = me.along_y(d)
        sends.push(pk_sum.at[:, plo, phi], py.at[d - 1], py_s.at[d - 1], py_r.at[d - 1], me.device(ylo=plo, yhi=phi))

    for d in range(1, 4):
        arrived(gy.at[d - 1], gy_s.at[d - 1], gy_r.at[d - 1], me)

    @pl.loop(0, NZ)
    def _(n):
        total = gs[n, ylo, :, yhi].astype(F32)
        for d in range(3):
            total = total + gy[d, n].astype(F32)
        gz_send[n] = total.astype(BF16)

    for d in range(1, NZ):
        to = me.along_z(d)
        sends.push(gz_send.at[to], gz.at[d - 1], gz_s.at[d - 1], gz_r.at[d - 1], me.device(z=to))

    from_sibling(0)
    for side, half in ((0, 1), (1, 0), (0, 0), (1, 1)):
        arrived(nb_recv.at[side, pl.ds(half * 128, 128)], nb_s.at[side, half], nb_r.at[side, half], me)

    @pl.loop(0, 4)
    def _(n):
        part = pl.ds(pl.multiple_of(n * 64, 64), 64)
        upstream = (
            esum[0, part]
            + es_recv[0, part].astype(F32)
            + nb_recv[0, part].astype(F32)
            + nb_recv[1, part].astype(F32)
        )
        normal, inverse = normalize(tokr[part].astype(F32))
        first = jnp.mean(upstream, axis=-1, keepdims=True)
        second = jnp.mean(upstream * normal, axis=-1, keepdims=True)
        grad[part] = (inverse * (upstream - first - normal * second) + cotr[part].astype(F32)).astype(BF16)

    @pl.when(me.moved)
    def _():
        swap_grad.start()

    @pl.when(jnp.logical_not(me.moved))
    def _():
        tok_grad[...] = grad[...]

    for d in range(1, 4):
        arrived(py.at[d - 1], py_s.at[d - 1], py_r.at[d - 1], me)

    @pl.loop(0, NZ)
    def _(n):
        total = pk_sum[n, ylo, yhi].astype(F32)
        for d in range(3):
            total = total + py[d, n].astype(F32)
        pz_send[n] = total.astype(BF16)

    for d in range(1, NZ):
        to = me.along_z(d)
        sends.push(pz_send.at[to], pz.at[d - 1], pz_s.at[d - 1], pz_r.at[d - 1], me.device(z=to))

    for d in range(1, NZ):
        arrived(gz.at[d - 1], gz_s.at[d - 1], gz_r.at[d - 1], me)
    total = gz_send[z].astype(F32)
    for d in range(1, NZ):
        total = total + gz[d - 1].astype(F32)
    for c in range(2):
        for px in range(4):
            for b in range(4):
                gx_f[c * 4 + px, b * 4 : b * 4 + 4, :] = total[c, px * 4 : px * 4 + 4, b * HD : (b + 1) * HD]
    gx_recv[w] = gx_f[w]
    for d in range(1, 8):
        pk, px = me.row(d // 4, d % 4)
        sends.push(gx_f.at[pk * 4 + px], gx_recv.at[w], gx_s.at[d - 1], gx_r.at[d - 1], me.device(k=pk, x=px))

    for d in range(1, NZ):
        arrived(pz.at[d - 1], pz_s.at[d - 1], pz_r.at[d - 1], me)
    total = pz_send[z].astype(F32)
    for d in range(1, NZ):
        total = total + pz[d - 1].astype(F32)
    for px in range(4):
        for b in range(8):
            px_f[px, b * 4 : b * 4 + 4, :] = total[px * 4 : px * 4 + 4, b * HD : (b + 1) * HD]
    px_recv[x] = px_f[x]
    for d in range(1, 4):
        pk, px = me.row(0, d)
        sends.push(px_f.at[px], px_recv.at[x], px_s.at[d - 1], px_r.at[d - 1], me.device(x=px))

    for d in range(1, 8):
        sk, sx = (k + 2 - d // 4) % 2, (x + 4 - d % 4) % 4
        arrived(gx_recv.at[sk * 4 + sx], gx_s.at[d - 1], gx_r.at[d - 1], me)
    for src in range(8):
        h = 2 * (src % 4) + src // 4
        for b in range(4):
            wi_grad[:, b * D + h * HD : b * D + (h + 1) * HD] = gx_recv[src, b * 4 : b * 4 + 4, :]
    for d in range(1, 4):
        arrived(px_recv.at[(x + 4 - d) % 4], px_s.at[d - 1], px_r.at[d - 1], me)
    total = px_recv[0] + px_recv[1] + px_recv[2] + px_recv[3]
    for b in range(8):
        wo_grad[:, b * HD : (b + 1) * HD] = total[b * 4 : b * 4 + 4]
    sends.drain()

    @pl.when(me.moved)
    def _():
        swap_lay.wait()
        swap_grad.wait()


def run_reduce(normed, dhidden, win, wout, mixed, tokr, cotr):
    shapes = [((ROWS, D), BF16), ((ROWS, D), BF16), ((4, 4 * D), F32), ((4, D), F32)]
    scratch = [
        pltpu.VMEM((ROWS, D), BF16), pltpu.VMEM((ROWS, D), BF16),
        pltpu.VMEM((4, ROWS, D), F32), pltpu.VMEM((4, ROWS, D), BF16), pltpu.VMEM((4, ROWS, D), BF16),
        pltpu.VMEM((ROWS, D), BF16), pltpu.VMEM((2, 128, D), BF16),
        pltpu.VMEM((2, ROWS, D), BF16), pltpu.VMEM((2, ROWS, D), BF16),
        pltpu.VMEM((NZ, 2, 2, 2, 16, 512), BF16), pltpu.VMEM((3, NZ, 2, 16, 512), BF16),
        pltpu.VMEM((NZ, 2, 16, 512), BF16), pltpu.VMEM((7, 2, 16, 512), BF16),
        pltpu.VMEM((8, 16, 128), F32), pltpu.VMEM((8, 16, 128), F32),
        pltpu.VMEM((NZ, 2, 2, 2, 16, D), BF16), pltpu.VMEM((NZ, 2, 2, 16, D), BF16),
        pltpu.VMEM((NZ, 2, 2, 16, D), BF16), pltpu.VMEM((3, NZ, 16, D), BF16),
        pltpu.VMEM((NZ, 16, D), BF16), pltpu.VMEM((7, 16, D), BF16),
        pltpu.VMEM((4, 32, 128), F32), pltpu.VMEM((4, 32, 128), F32),
        DMA((4,)), DMA((4,)), DMA((2,)), DMA((2,)), DMA((2, 2)), DMA((2, 2)),
        DMA((3,)), DMA((3,)), DMA((7,)), DMA((7,)), DMA((7,)), DMA((7,)),
        DMA, DMA, DMA((3,)), DMA((3,)), DMA((7,)), DMA((7,)), DMA((3,)), DMA((3,)), DMA((2,)), DMA((2,)),
    ]
    return pl.pallas_call(
        reduce_kernel,
        out_shape=[jax.ShapeDtypeStruct(s, t) for s, t in shapes],
        in_specs=[VMEM] * 7,
        out_specs=[VMEM] * 4,
        scratch_shapes=scratch,
        compiler_params=pltpu.CompilerParams(
            collective_id=2, has_side_effects=True, vmem_limit_bytes=56 << 20
        ),
        name="reduce",
    )(normed, dhidden, win, wout, mixed, tokr, cotr)


def local(tokens, lengths, in_weight, out_weight, cotangent):
    normed, gated, slope, win, wout, dmix, tokr, cotr, lens = run_gather(
        tokens, cotangent, in_weight, out_weight, lengths
    )
    attn, stats = run_attend(gated, dmix, lens)
    dattn, dupper, mixed = run_middle(attn, stats, gated, slope, dmix)
    dhidden = run_back(gated, slope, dattn, dupper, lens)
    return tuple(run_reduce(normed, dhidden, win, wout, mixed, tokr, cotr))


def solution(mesh):
    both = P(("dp", "seq"), None)
    return jax.shard_map(
        local,
        mesh=mesh,
        in_specs=(both, P("dp", None), both, both, both),
        out_specs=(both, both, both, both),
        check_vma=False,
    )
```

```python
import functools

import jax
import jax.numpy as jnp
from jax import lax
from jax.experimental import pallas as pl
from jax.experimental.pallas import tpu as pltpu
from jax.sharding import PartitionSpec as P

F32 = jnp.float32
BF16 = jnp.bfloat16
MESH = pl.DeviceIdType.MESH
DMA = pltpu.SemaphoreType.DMA

D = 1024
HEADS = 8
HD = 128
ROWS = 256
NZ = 8
epsilon = 1e-05
HALF_FACTOR = 0.5 * HD ** (-0.5)
VMEM = pl.BlockSpec(memory_space=pltpu.VMEM)
ABT = (((1,), (1,)), ((), ()))
ATB = (((0,), (0,)), ((), ()))


def dot(a, b, dims=(((1,), (0,)), ((), ()))):
    return lax.dot_general(a, b, dims, preferred_element_type=F32)


class Place:
    def __init__(self):
        g = lax.axis_index("dp")
        s = lax.axis_index("seq")
        self.z, self.ylo, self.k = g // 4, (g // 2) % 2, g % 2
        self.yhi, self.x = s // 4, s % 4
        self.w = self.k * 4 + self.x
        self.head = 2 * self.x + self.k
        self.moved = self.k != self.yhi

    def device(self, z=None, ylo=None, k=None, yhi=None, x=None):
        z = self.z if z is None else z
        ylo = self.ylo if ylo is None else ylo
        k = self.k if k is None else k
        yhi = self.yhi if yhi is None else yhi
        x = self.x if x is None else x
        return (z * 4 + ylo * 2 + k, yhi * 4 + x)

    def row(self, dk, dx):
        return (self.k + dk) % 2, (self.x + dx) % 4

    def along_z(self, d):
        return (self.z + d) % NZ

    def along_y(self, d):
        y = (self.yhi * 2 + self.ylo + d) % 4
        return y // 2, y % 2

    def partner(self):
        return self.device(k=self.yhi, yhi=self.k)

    def sibling(self):
        return self.device(k=1 - self.k)

    def row_peers(self):
        peers = []
        for d in range(1, 8):
            k, x = self.row(d // 4, d % 4)
            peers.append(self.device(k=k, x=x))
        return peers

    def zy_peers(self):
        peers = [self.device(z=self.along_z(d)) for d in range(1, NZ)]
        for d in range(1, 4):
            yhi, ylo = self.along_y(d)
            peers.append(self.device(ylo=ylo, yhi=yhi))
        return peers


def greet(me, peers, with_partner):
    barrier = pltpu.get_barrier_semaphore()
    for peer in peers:
        pl.semaphore_signal(barrier, inc=1, device_id=peer, device_id_type=MESH)
    if with_partner:

        @pl.when(me.moved)
        def _():
            pl.semaphore_signal(barrier, inc=1, device_id=me.partner(), device_id_type=MESH)

    if with_partner:
        pl.semaphore_wait(barrier, len(peers) + me.moved.astype(jnp.int32))
    else:
        pl.semaphore_wait(barrier, len(peers))


def copy(src, dst, send, recv, to):
    return pltpu.make_async_remote_copy(
        src_ref=src, dst_ref=dst, send_sem=send, recv_sem=recv, device_id=to, device_id_type=MESH
    )


class Sends:
    def __init__(self):
        self.started = []

    def push(self, src, dst, send, recv, to):
        one = copy(src, dst, send, recv, to)
        one.start()
        self.started.append(one)

    def drain(self):
        for one in self.started:
            one.wait_send()


def arrived(ref, send, recv, me):
    copy(ref, ref, send, recv, me.sibling()).wait_recv()


def normalize(values):
    centre = values - jnp.mean(values, axis=-1, keepdims=True)
    inverse = lax.rsqrt(jnp.mean(centre * centre, axis=-1, keepdims=True) + epsilon)
    return centre * inverse, inverse


def first_of(position, lens):
    e0 = lens[0:1, 0:1]
    e1 = e0 + lens[0:1, 1:2]
    e2 = e1 + lens[0:1, 2:3]
    zero = jnp.zeros_like(position)
    start = jnp.where(position >= e0, e0, zero)
    start = jnp.where(position >= e1, e1, start)
    return jnp.where(position >= e2, e2, start)


BUFFERS = {
    "tokr": ((ROWS, D), BF16), "cotr": ((ROWS, D), BF16),
    "len_send": ((8, 128), jnp.int32), "len_recv": ((8, 128), jnp.int32), "lens": ((8, 128), jnp.int32),
    "wi_f": ((8, 16, 128), F32), "wi_send": ((8, 16, 128), BF16), "wi_recv": ((8, 16, 128), BF16),
    "wi_asm": ((2, 16, 512), F32),
    "wo_f": ((32, 128), F32), "wo_send": ((32, 128), BF16), "wo_recv": ((4, 32, 128), BF16), "wo_asm": ((16, D), F32),
    "win": ((NZ, 2, 2, 2, 16, 512), BF16), "wout": ((NZ, 2, 2, 2, 16, D), BF16),
    "normed": ((8, ROWS, D), BF16), "gated": ((8, ROWS, 512), BF16), "slope": ((8, ROWS, 512), BF16),
    "dsend": ((8, ROWS, HD), BF16), "dmix": ((8, ROWS, HD), BF16),
    "attn": ((8, ROWS, HD), BF16), "stats": ((8, 8, ROWS), F32), "every": ((8, 8, 8, ROWS), F32),
    "comb": ((128, ROWS), F32), "msend": ((8, ROWS, HD), BF16), "mixed": ((8, ROWS, HD), BF16),
    "dattn": ((8, ROWS, HD), BF16), "dhidden": ((8, ROWS, 512), BF16), "dquery": ((8, ROWS, HD), F32),
    "lay": ((ROWS, D), BF16), "grad": ((ROWS, D), BF16),
    "esum": ((4, ROWS, D), F32), "es_send": ((4, ROWS, D), BF16), "es_recv": ((4, ROWS, D), BF16),
    "x2_send": ((ROWS, D), BF16), "rl_recv": ((2, 128, D), BF16),
    "nb_send": ((2, ROWS, D), BF16), "nb_recv": ((2, ROWS, D), BF16),
    "gs": ((NZ, 2, 2, 2, 16, 512), BF16), "gy": ((3, NZ, 2, 16, 512), BF16),
    "gz_send": ((NZ, 2, 16, 512), BF16), "gz": ((7, 2, 16, 512), BF16),
    "gx_f": ((8, 16, 128), F32), "gx_recv": ((8, 16, 128), F32),
    "ps": ((NZ, 2, 2, 2, 16, D), BF16), "pc": ((NZ, 2, 2, 16, D), BF16), "pk_sum": ((NZ, 2, 2, 16, D), BF16),
    "py": ((3, NZ, 16, D), BF16), "pz_send": ((NZ, 16, D), BF16), "pz": ((7, 16, D), BF16),
    "px_f": ((4, 32, 128), F32), "px_recv": ((4, 32, 128), F32),
}
SEMAPHORES = {
    "load": (2,), "swap": (4,), "xi": (7,), "xo": (3,), "zi": (7,), "zo": (7,), "yi": (3,), "yo": (3,), "core": (1,),
    "ag": (8, 2), "fw": (4, 2), "dm": (7,), "st": (7,), "mx": (7,), "sib": (4,), "rl": (2,), "nb": (2, 2),
    "gy": (3,), "gz": (7,), "gx": (7,), "pc": (1,), "py": (3,), "pz": (7,), "px": (3,), "sw": (2,),
}


class Refs:
    def __init__(self, buffers, semaphores):
        for name, ref in zip(BUFFERS, buffers):
            setattr(self, name, ref)
        for n, name in enumerate(SEMAPHORES):
            setattr(self, name + "_s", semaphores[2 * n])
            setattr(self, name + "_r", semaphores[2 * n + 1])


def project(r, block):
    left = r.normed[block]
    for n in range(2):
        cols = pl.ds(n * 256, 256)
        hidden = dot(left, r.win[:, :, :, :, :, cols].reshape(D, 256))
        sigma = 0.5 + 0.5 * jnp.tanh(0.5 * hidden)
        value = hidden * sigma
        r.gated[block, :, cols] = value.astype(BF16)
        r.slope[block, :, cols] = (sigma + value * (1.0 - sigma)).astype(BF16)


def attend(r, i, reach):
    query = r.gated[i, :, 256:384]
    pos = i * ROWS + lax.broadcasted_iota(jnp.int32, (ROWS, 1), 0)
    start = first_of(pos, r.lens)
    total = jnp.zeros((ROWS, HD), F32)
    for off in range(reach + 1):
        j = i - off
        half = dot(query, r.gated[j, :, 384:512], ABT) * HALF_FACTOR
        weights = half + half * jnp.tanh(half)
        other = j * ROWS + lax.broadcasted_iota(jnp.int32, (ROWS, ROWS), 1)
        allowed = other >= start
        if off == 0:
            allowed = allowed & (other <= pos)
        weights = jnp.where(allowed, weights, 0.0).astype(BF16)
        total = total + dot(weights, r.gated[j, :, 128:256])
    r.attn[i] = total.astype(BF16)


def row_stats(r, i):
    value = r.attn[i].astype(F32)
    upstream = r.dmix[i].astype(F32) * r.gated[i, :, 0:128].astype(F32)
    mean = jnp.mean(value, axis=-1, keepdims=True)
    centre = value - mean
    parts = (
        mean,
        jnp.sum(centre * centre, axis=-1, keepdims=True),
        jnp.sum(upstream, axis=-1, keepdims=True),
        jnp.sum(upstream * centre, axis=-1, keepdims=True),
    )
    lane = lax.broadcasted_iota(jnp.int32, (ROWS, HD), 1)
    packed = jnp.zeros((ROWS, HD), F32)
    for n, part in enumerate(parts):
        packed = jnp.where(lane == n, part, packed)
    r.stats[i] = packed.T[0:8]


def gate_rows(r, i):
    mean, second, total, cross = (r.every[:, i, n, :] for n in range(4))
    middle = jnp.mean(mean, axis=0, keepdims=True)
    apart = mean - middle
    variance = jnp.sum(second + HD * apart * apart, axis=0, keepdims=True) / D
    inverse = lax.rsqrt(variance + epsilon)
    first = jnp.sum(total, axis=0, keepdims=True) / D
    other = inverse * jnp.sum(cross + apart * total, axis=0, keepdims=True) / D
    r.comb[0:1, :] = middle
    r.comb[1:2, :] = inverse
    r.comb[2:3, :] = first
    r.comb[3:4, :] = other
    turned = r.comb[...].T
    middle, inverse, first, other = (turned[:, n : n + 1] for n in range(4))
    upper = r.gated[i, :, 0:128].astype(F32)
    through = r.dmix[i].astype(F32)
    normal = (r.attn[i].astype(F32) - middle) * inverse
    r.msend[i] = (normal * upper).astype(BF16)
    upstream = through * upper
    r.dattn[i] = (inverse * (upstream - first - normal * other)).astype(BF16)
    r.dhidden[i, :, 0:128] = (through * normal * r.slope[i, :, 0:128].astype(F32)).astype(BF16)


def attend_back(r, j, reach):
    key = r.gated[j, :, 384:512]
    value = r.gated[j, :, 128:256]
    other = j * ROWS + lax.broadcasted_iota(jnp.int32, (ROWS, ROWS), 0)
    dkey = jnp.zeros((ROWS, HD), F32)
    dvalue = jnp.zeros((ROWS, HD), F32)
    for off in range(reach + 1):
        i = j + off
        query = r.gated[i, :, 256:384]
        grad = r.dattn[i]
        half = dot(key, query, ABT) * HALF_FACTOR
        pos = i * ROWS + lax.broadcasted_iota(jnp.int32, (1, ROWS), 1)
        allowed = other >= first_of(pos, r.lens)
        if off == 0:
            allowed = allowed & (other <= pos)
        double = jnp.where(allowed, 1.0 + jnp.tanh(half), 0.0)
        weights = half * double
        bend = double + weights * (2.0 - double)
        dscores = (dot(value, grad, ABT) * bend).astype(BF16)
        dvalue = dvalue + dot(weights.astype(BF16), grad)
        dkey = dkey + dot(dscores, query)
        r.dquery[i] += dot(dscores, key, ATB)
    r.dhidden[j, :, 128:256] = (dvalue * r.slope[j, :, 128:256].astype(F32)).astype(BF16)
    r.dhidden[j, :, 384:512] = (dkey * HALF_FACTOR * r.slope[j, :, 384:512].astype(F32)).astype(BF16)


def kernel(tok, cot, wi, wo, lengths, layer_out, tok_grad, wi_grad, wo_grad, *scratch):
    me = Place()
    z, ylo, k, yhi, x, w = me.z, me.ylo, me.k, me.yhi, me.x, me.w
    r = Refs(scratch[: len(BUFFERS)], scratch[len(BUFFERS) :])
    sends = Sends()
    right, left = me.device(x=(x + 1) % 4), me.device(x=(x + 3) % 4)
    stays = jnp.logical_not(me.moved)

    def row_source(d):
        return (k + 2 - d // 4) % 2, (x + 4 - d % 4) % 4

    load_tok = pltpu.make_async_copy(tok, r.tokr, r.load_r.at[0])
    load_cot = pltpu.make_async_copy(cot, r.cotr, r.load_r.at[1])

    @pl.when(stays)
    def _():
        load_tok.start()
        load_cot.start()

    greet(me, me.row_peers() + me.zy_peers(), True)

    swap_tok = [
        copy(tok.at[part], r.tokr.at[part], r.swap_s.at[n], r.swap_r.at[n], me.partner())
        for n, part in ((0, pl.ds(0, 128)), (1, pl.ds(128, 128)))
    ]
    swap_cot = copy(cot, r.cotr, r.swap_s.at[2], r.swap_r.at[2], me.partner())

    @pl.when(me.moved)
    def _():
        swap_tok[0].start()
        swap_tok[1].start()

    wide = wi[...].astype(F32)
    for h in range(HEADS):
        for b in range(4):
            r.wi_f[h, b * 4 : b * 4 + 4, :] = wide[:, b * D + h * HD : b * D + (h + 1) * HD]
    r.wi_send[...] = r.wi_f[...].astype(BF16)
    for d in range(1, 8):
        pk, px = me.row(d // 4, d % 4)
        sends.push(
            r.wi_send.at[2 * px + pk], r.wi_recv.at[w], r.xi_s.at[d - 1], r.xi_r.at[d - 1], me.device(k=pk, x=px)
        )
    r.wi_recv[w] = r.wi_send[me.head]
    wide_o = wo[...].astype(F32)
    for b in range(8):
        r.wo_f[b * 4 : b * 4 + 4, :] = wide_o[:, b * HD : (b + 1) * HD]
    r.wo_send[...] = r.wo_f[...].astype(BF16)
    for d in range(1, 4):
        pk, px = me.row(0, d)
        sends.push(r.wo_send, r.wo_recv.at[x], r.xo_s.at[d - 1], r.xo_r.at[d - 1], me.device(x=px))
    r.wo_recv[x] = r.wo_send[...]
    r.len_send[...] = jnp.zeros_like(r.len_send)
    r.len_send[0:1, 0:4] = lengths[...]
    sends.push(r.len_send, r.len_recv, r.swap_s.at[3], r.swap_r.at[3], me.sibling())

    def norm_half(half):
        part = pl.ds(half * 128, 128)
        r.normed[w, part] = normalize(r.tokr[part].astype(F32))[0].astype(BF16)

    def own(half):
        return r.normed.at[w, pl.ds(half * 128, 128)]

    own_sends = []
    for half in range(2):
        own_sends.append(copy(own(half), own(half), r.ag_s.at[3, half], r.ag_r.at[3, half], right))
        own_sends.append(copy(own(half), own(half), r.ag_s.at[1, half], r.ag_r.at[1, half], left))
        own_sends.append(copy(own(half), own(half), r.fw_s.at[0, half], r.ag_r.at[4, half], me.sibling()))

    @pl.when(stays)
    def _():
        load_tok.wait()
        norm_half(0)
        norm_half(1)
        for n in (0, 4, 3, 1, 2, 5):
            own_sends[n].start()

    for d in range(1, 8):
        sk, sx = row_source(d)
        arrived(r.wi_recv.at[sk * 4 + sx], r.xi_s.at[d - 1], r.xi_r.at[d - 1], me)
    for src in range(8):
        piece = r.wi_recv[src].astype(F32)
        for b in range(4):
            r.wi_asm[src // 4, (src % 4) * 4 : (src % 4) * 4 + 4, b * HD : (b + 1) * HD] = piece[b * 4 : b * 4 + 4]
    for c in range(2):
        r.win[z, ylo, c, yhi] = r.wi_asm[c].astype(BF16)
    for d in range(1, NZ):
        part = r.win.at[z, ylo, :, yhi]
        sends.push(part, part, r.zi_s.at[d - 1], r.zi_r.at[d - 1], me.device(z=me.along_z(d)))

    for d in range(1, 4):
        arrived(r.wo_recv.at[(x + 4 - d) % 4], r.xo_s.at[d - 1], r.xo_r.at[d - 1], me)
    for src in range(4):
        piece = r.wo_recv[src].astype(F32)
        for b in range(8):
            r.wo_asm[src * 4 : src * 4 + 4, b * HD : (b + 1) * HD] = piece[b * 4 : b * 4 + 4]
    r.wout[z, ylo, k, yhi] = r.wo_asm[...].astype(BF16)
    for d in range(1, NZ):
        part = r.wout.at[z, ylo, k, yhi]
        sends.push(part, part, r.zo_s.at[d - 1], r.zo_r.at[d - 1], me.device(z=me.along_z(d)))

    @pl.when(me.moved)
    def _():
        swap_tok[0].wait_recv()
        norm_half(0)
        for n in (0, 1, 2):
            own_sends[n].start()
        swap_tok[1].wait_recv()
        norm_half(1)
        for n in (4, 3, 5):
            own_sends[n].start()

    def rows_of(dx, half):
        return r.normed.at[k * 4 + (x + dx) % 4, pl.ds(half * 128, 128)]

    def take(dx, half):
        part = rows_of(dx, half)
        arrived(part, r.ag_s.at[dx, half], r.ag_r.at[dx, half], me)
        sends.push(part, part, r.fw_s.at[dx, half], r.ag_r.at[4 + dx, half], me.sibling())

    take(3, 0)
    part = rows_of(3, 0)
    sends.push(part, part, r.ag_s.at[2, 0], r.ag_r.at[2, 0], right)
    take(1, 1)
    part = rows_of(1, 1)
    sends.push(part, part, r.ag_s.at[2, 1], r.ag_r.at[2, 1], left)

    for d in range(1, NZ):
        arrived(r.win.at[(z + NZ - d) % NZ, ylo, :, yhi], r.zi_s.at[d - 1], r.zi_r.at[d - 1], me)
    for d in range(1, 4):
        phi, plo = me.along_y(d)
        part = r.win.at[:, ylo, :, yhi]
        sends.push(part, part, r.yi_s.at[d - 1], r.yi_r.at[d - 1], me.device(ylo=plo, yhi=phi))

    @pl.when(me.moved)
    def _():
        swap_cot.start()

    take(3, 1)
    take(1, 0)
    for d in range(1, NZ):
        arrived(r.wout.at[(z + NZ - d) % NZ, ylo, k, yhi], r.zo_s.at[d - 1], r.zo_r.at[d - 1], me)
    for d in range(1, 4):
        phi, plo = me.along_y(d)
        part = r.wout.at[:, ylo, k, yhi]
        sends.push(part, part, r.yo_s.at[d - 1], r.yo_r.at[d - 1], me.device(ylo=plo, yhi=phi))
    arrived(r.len_recv, r.swap_s.at[3], r.swap_r.at[3], me)
    r.lens[...] = jnp.where(me.moved, r.len_recv[...], r.len_send[...])
    take(2, 0)
    take(2, 1)
    for d in range(1, 4):
        shi, slo = me.along_y(4 - d)
        arrived(r.win.at[:, slo, :, shi], r.yi_s.at[d - 1], r.yi_r.at[d - 1], me)

    @pl.loop(0, 4)
    def _(i):
        project(r, k * 4 + i)

    for dx in range(4):
        for half in range(2):
            arrived(
                r.normed.at[(1 - k) * 4 + (x + dx) % 4, pl.ds(half * 128, 128)],
                r.fw_s.at[dx, half], r.ag_r.at[4 + dx, half], me,
            )

    @pl.loop(0, 4)
    def _(i):
        project(r, (1 - k) * 4 + i)

    for i in range(4):
        attend(r, i, i)

    for d in range(1, 4):
        shi, slo = me.along_y(4 - d)
        arrived(r.wout.at[:, slo, k, shi], r.yo_s.at[d - 1], r.yo_r.at[d - 1], me)
    sends.push(r.wout.at[:, :, k], r.wout.at[:, :, k], r.core_s.at[0], r.core_r.at[0], me.sibling())

    @pl.loop(4, 8)
    def _(i):
        attend(r, i, 4)

    @pl.when(me.moved)
    def _():
        swap_cot.wait_recv()

    @pl.when(stays)
    def _():
        load_cot.wait()

    arrived(r.wout.at[:, :, 1 - k], r.core_s.at[0], r.core_r.at[0], me)

    @pl.loop(0, 4)
    def _(i):
        pair = dot(r.cotr[...], r.wout[pl.ds(2 * i, 2)].reshape(256, D), ABT)
        r.dsend[2 * i] = pair[:, :HD].astype(BF16)
        r.dsend[2 * i + 1] = pair[:, HD:].astype(BF16)

    r.dmix[w] = r.dsend[me.head]
    for d in range(1, 8):
        pk, px = me.row(d // 4, d % 4)
        sends.push(
            r.dsend.at[2 * px + pk], r.dmix.at[w], r.dm_s.at[d - 1], r.dm_r.at[d - 1], me.device(k=pk, x=px)
        )
    for d in range(1, 8):
        sk, sx = row_source(d)
        arrived(r.dmix.at[sk * 4 + sx], r.dm_s.at[d - 1], r.dm_r.at[d - 1], me)

    @pl.loop(0, 8)
    def _(i):
        row_stats(r, i)

    for d in range(1, 8):
        pk, px = me.row(d // 4, d % 4)
        sends.push(r.stats, r.every.at[w], r.st_s.at[d - 1], r.st_r.at[d - 1], me.device(k=pk, x=px))
    r.every[w] = r.stats[...]
    r.comb[...] = jnp.zeros_like(r.comb)
    r.dquery[...] = jnp.zeros_like(r.dquery)
    for d in range(1, 8):
        sk, sx = row_source(d)
        arrived(r.every.at[sk * 4 + sx], r.st_s.at[d - 1], r.st_r.at[d - 1], me)

    @pl.loop(0, 8)
    def _(i):
        gate_rows(r, i)

    r.mixed[me.head] = r.msend[w]
    for d in range(1, 8):
        pk, px = me.row(d // 4, d % 4)
        sends.push(
            r.msend.at[pk * 4 + px], r.mixed.at[me.head], r.mx_s.at[d - 1], r.mx_r.at[d - 1], me.device(k=pk, x=px)
        )

    @pl.loop(0, 3)
    def _(j):
        attend_back(r, j, 4)

    for d in range(1, 8):
        sk, sx = row_source(d)
        arrived(r.mixed.at[2 * sx + sk], r.mx_s.at[d - 1], r.mx_r.at[d - 1], me)

    @pl.loop(0, 4)
    def _(n):
        pair = jnp.concatenate([r.mixed[2 * n], r.mixed[2 * n + 1]], axis=1)
        product = dot(pair, r.cotr[...], ATB)
        r.ps[pl.ds(2 * n, 2)] = product.astype(BF16).reshape(2, 2, 2, 2, 16, D)

    sends.push(r.ps.at[:, :, 1 - k], r.pc, r.pc_s.at[0], r.pc_r.at[0], me.sibling())

    joined = jnp.concatenate([r.mixed[h] for h in range(HEADS)], axis=1)
    for n in range(4):
        cols = pl.ds(n * 256, 256)
        product = dot(joined, r.wout[:, :, :, :, :, cols].reshape(D, 256))
        r.lay[:, cols] = (product + r.tokr[:, cols].astype(F32)).astype(BF16)
    swap_lay = copy(r.lay, layer_out, r.sw_s.at[0], r.sw_r.at[0], me.partner())
    swap_grad = copy(r.grad, tok_grad, r.sw_s.at[1], r.sw_r.at[1], me.partner())

    @pl.when(stays)
    def _():
        layer_out[...] = r.lay[...]

    arrived(r.pc, r.pc_s.at[0], r.pc_r.at[0], me)

    @pl.loop(0, NZ)
    def _(n):
        r.pk_sum[n] = (r.ps[n, :, k].astype(F32) + r.pc[n].astype(F32)).astype(BF16)

    for d in range(1, 4):
        phi, plo = me.along_y(d)
        sends.push(
            r.pk_sum.at[:, plo, phi], r.py.at[d - 1], r.py_s.at[d - 1], r.py_r.at[d - 1], me.device(ylo=plo, yhi=phi)
        )

    @pl.when(me.moved)
    def _():
        swap_lay.start()

    @pl.loop(3, 4)
    def _(j):
        attend_back(r, j, 4)

    for j in range(4, 8):
        attend_back(r, j, 7 - j)

    @pl.loop(0, 8)
    def _(i):
        r.dhidden[i, :, 256:384] = (r.dquery[i] * HALF_FACTOR * r.slope[i, :, 256:384].astype(F32)).astype(BF16)

    def back_product(block, n):
        return dot(r.dhidden[block], r.win[pl.ds(2 * n, 2)].reshape(256, 512), ABT)

    def partial(dx):
        there = (1 - k) * 4 + (x + dx) % 4
        here = k * 4 + (x + dx) % 4

        @pl.loop(0, 4)
        def _(n):
            cols = pl.ds(pl.multiple_of(n * 256, 256), 256)
            r.es_send[dx, :, cols] = back_product(there, n).astype(BF16)

        sends.push(r.es_send.at[dx], r.es_recv.at[dx], r.sib_s.at[dx], r.sib_r.at[dx], me.sibling())

        @pl.loop(0, 4)
        def _(n):
            cols = pl.ds(pl.multiple_of(n * 256, 256), 256)
            r.esum[dx, :, cols] = back_product(here, n)

    def from_sibling(dx):
        arrived(r.es_recv.at[dx], r.sib_s.at[dx], r.sib_r.at[dx], me)

    def to_neighbour(side, half, extra):
        part = pl.ds(half * 128, 128)
        dx = 1 + 2 * side
        total = r.esum[dx, part] + r.es_recv[dx, part].astype(F32)
        if extra is not None:
            total = total + extra.astype(F32)
        r.nb_send[side, part] = total.astype(BF16)
        sends.push(
            r.nb_send.at[side, part], r.nb_recv.at[side, part],
            r.nb_s.at[side, half], r.nb_r.at[side, half], (right, left)[side],
        )

    partial(2)
    partial(1)
    from_sibling(2)
    r.x2_send[...] = (r.esum[2] + r.es_recv[2].astype(F32)).astype(BF16)
    sends.push(r.x2_send.at[pl.ds(0, 128)], r.rl_recv.at[0], r.rl_s.at[0], r.rl_r.at[0], right)
    sends.push(r.x2_send.at[pl.ds(128, 128)], r.rl_recv.at[1], r.rl_s.at[1], r.rl_r.at[1], left)
    partial(3)
    from_sibling(1)
    to_neighbour(0, 1, None)
    from_sibling(3)
    to_neighbour(1, 0, None)

    @pl.loop(0, 4)
    def _(n):
        cols = pl.ds(pl.multiple_of(n * 256, 256), 256)
        product = dot(r.normed[:, :, cols].reshape(8 * ROWS, 256), r.dhidden[...].reshape(8 * ROWS, 512), ATB)
        r.gs[pl.ds(2 * n, 2)] = product.astype(BF16).reshape(2, 2, 2, 2, 16, 512)

    for d in range(1, 4):
        phi, plo = me.along_y(d)
        sends.push(
            r.gs.at[:, plo, :, phi], r.gy.at[d - 1], r.gy_s.at[d - 1], r.gy_r.at[d - 1], me.device(ylo=plo, yhi=phi)
        )

    for side in range(2):
        arrived(r.rl_recv.at[side], r.rl_s.at[side], r.rl_r.at[side], me)
        to_neighbour(side, side, r.rl_recv[side])
    partial(0)

    for d in range(1, 4):
        arrived(r.py.at[d - 1], r.py_s.at[d - 1], r.py_r.at[d - 1], me)

    @pl.loop(0, NZ)
    def _(n):
        total = r.pk_sum[n, ylo, yhi].astype(F32)
        for d in range(3):
            total = total + r.py[d, n].astype(F32)
        r.pz_send[n] = total.astype(BF16)

    for d in range(1, NZ):
        to = me.along_z(d)
        sends.push(r.pz_send.at[to], r.pz.at[d - 1], r.pz_s.at[d - 1], r.pz_r.at[d - 1], me.device(z=to))

    for d in range(1, 4):
        arrived(r.gy.at[d - 1], r.gy_s.at[d - 1], r.gy_r.at[d - 1], me)

    @pl.loop(0, NZ)
    def _(n):
        total = r.gs[n, ylo, :, yhi].astype(F32)
        for d in range(3):
            total = total + r.gy[d, n].astype(F32)
        r.gz_send[n] = total.astype(BF16)

    for d in range(1, NZ):
        to = me.along_z(d)
        sends.push(r.gz_send.at[to], r.gz.at[d - 1], r.gz_s.at[d - 1], r.gz_r.at[d - 1], me.device(z=to))

    from_sibling(0)
    for side, half in ((0, 1), (1, 0), (0, 0), (1, 1)):
        arrived(r.nb_recv.at[side, pl.ds(half * 128, 128)], r.nb_s.at[side, half], r.nb_r.at[side, half], me)

    @pl.loop(0, 4)
    def _(n):
        part = pl.ds(pl.multiple_of(n * 64, 64), 64)
        upstream = (
            r.esum[0, part]
            + r.es_recv[0, part].astype(F32)
            + r.nb_recv[0, part].astype(F32)
            + r.nb_recv[1, part].astype(F32)
        )
        normal, inverse = normalize(r.tokr[part].astype(F32))
        first = jnp.mean(upstream, axis=-1, keepdims=True)
        second = jnp.mean(upstream * normal, axis=-1, keepdims=True)
        r.grad[part] = (inverse * (upstream - first - normal * second) + r.cotr[part].astype(F32)).astype(BF16)

    @pl.when(me.moved)
    def _():
        swap_grad.start()

    @pl.when(stays)
    def _():
        tok_grad[...] = r.grad[...]

    for d in range(1, NZ):
        arrived(r.pz.at[d - 1], r.pz_s.at[d - 1], r.pz_r.at[d - 1], me)
    total = r.pz_send[z].astype(F32)
    for d in range(1, NZ):
        total = total + r.pz[d - 1].astype(F32)
    for px in range(4):
        for b in range(8):
            r.px_f[px, b * 4 : b * 4 + 4, :] = total[px * 4 : px * 4 + 4, b * HD : (b + 1) * HD]
    r.px_recv[x] = r.px_f[x]
    for d in range(1, 4):
        pk, px = me.row(0, d)
        sends.push(r.px_f.at[px], r.px_recv.at[x], r.px_s.at[d - 1], r.px_r.at[d - 1], me.device(x=px))

    for d in range(1, NZ):
        arrived(r.gz.at[d - 1], r.gz_s.at[d - 1], r.gz_r.at[d - 1], me)
    total = r.gz_send[z].astype(F32)
    for d in range(1, NZ):
        total = total + r.gz[d - 1].astype(F32)
    for c in range(2):
        for px in range(4):
            for b in range(4):
                r.gx_f[c * 4 + px, b * 4 : b * 4 + 4, :] = total[c, px * 4 : px * 4 + 4, b * HD : (b + 1) * HD]
    r.gx_recv[w] = r.gx_f[w]
    for d in range(1, 8):
        pk, px = me.row(d // 4, d % 4)
        sends.push(
            r.gx_f.at[pk * 4 + px], r.gx_recv.at[w], r.gx_s.at[d - 1], r.gx_r.at[d - 1], me.device(k=pk, x=px)
        )

    for d in range(1, 4):
        arrived(r.px_recv.at[(x + 4 - d) % 4], r.px_s.at[d - 1], r.px_r.at[d - 1], me)
    total = r.px_recv[0] + r.px_recv[1] + r.px_recv[2] + r.px_recv[3]
    for b in range(8):
        wo_grad[:, b * HD : (b + 1) * HD] = total[b * 4 : b * 4 + 4]
    for d in range(1, 8):
        sk, sx = row_source(d)
        arrived(r.gx_recv.at[sk * 4 + sx], r.gx_s.at[d - 1], r.gx_r.at[d - 1], me)
    for src in range(8):
        h = 2 * (src % 4) + src // 4
        for b in range(4):
            wi_grad[:, b * D + h * HD : b * D + (h + 1) * HD] = r.gx_recv[src, b * 4 : b * 4 + 4, :]
    sends.drain()
    for one in own_sends:
        one.wait_send()

    @pl.when(me.moved)
    def _():
        for one in swap_tok:
            one.wait_send()
        swap_cot.wait_send()
        swap_lay.wait()
        swap_grad.wait()


def local(tokens, lengths, in_weight, out_weight, cotangent):
    anywhere = pl.BlockSpec(memory_space=pl.ANY)
    shapes = [((ROWS, D), BF16), ((ROWS, D), BF16), ((4, 4 * D), F32), ((4, D), F32)]
    scratch = [pltpu.VMEM(shape, kind) for shape, kind in BUFFERS.values()]
    for shape in SEMAPHORES.values():
        scratch += [DMA(shape), DMA(shape)]
    return tuple(
        pl.pallas_call(
            kernel,
            out_shape=[jax.ShapeDtypeStruct(s, t) for s, t in shapes],
            in_specs=[anywhere, anywhere, VMEM, VMEM, VMEM],
            out_specs=[VMEM] * 4,
            scratch_shapes=scratch,
            compiler_params=pltpu.CompilerParams(
                collective_id=0, has_side_effects=True, vmem_limit_bytes=60 << 20
            ),
            name="layer",
        )(tokens, cotangent, in_weight, out_weight, lengths)
    )


def solution(mesh):
    both = P(("dp", "seq"), None)
    return jax.shard_map(
        local,
        mesh=mesh,
        in_specs=(both, P("dp", None), both, both, both),
        out_specs=(both, both, both, both),
        check_vma=False,
    )
```

```python
import functools

import jax
import jax.numpy as jnp
from jax import lax
from jax.experimental import pallas as pl
from jax.experimental.pallas import tpu as pltpu
from jax.sharding import PartitionSpec as P

F32 = jnp.float32
BF16 = jnp.bfloat16
MESH = pl.DeviceIdType.MESH
DMA = pltpu.SemaphoreType.DMA

D = 1024
HEADS = 8
HD = 128
ROWS = 256
NZ = 8
epsilon = 1e-05
HALF_FACTOR = 0.5 * HD ** (-0.5)
VMEM = pl.BlockSpec(memory_space=pltpu.VMEM)
ABT = (((1,), (1,)), ((), ()))
ATB = (((0,), (0,)), ((), ()))


def dot(a, b, dims=(((1,), (0,)), ((), ()))):
    return lax.dot_general(a, b, dims, preferred_element_type=F32)


class Place:
    def __init__(self):
        g = lax.axis_index("dp")
        s = lax.axis_index("seq")
        self.z, self.ylo, self.k = g // 4, (g // 2) % 2, g % 2
        self.yhi, self.x = s // 4, s % 4
        self.w = self.k * 4 + self.x
        self.head = 2 * self.x + self.k
        self.moved = self.k != self.yhi

    def device(self, z=None, ylo=None, k=None, yhi=None, x=None):
        z = self.z if z is None else z
        ylo = self.ylo if ylo is None else ylo
        k = self.k if k is None else k
        yhi = self.yhi if yhi is None else yhi
        x = self.x if x is None else x
        return (z * 4 + ylo * 2 + k, yhi * 4 + x)

    def row(self, dk, dx):
        return (self.k + dk) % 2, (self.x + dx) % 4

    def along_z(self, d):
        return (self.z + d) % NZ

    def along_y(self, d):
        y = (self.yhi * 2 + self.ylo + d) % 4
        return y // 2, y % 2

    def partner(self):
        return self.device(k=self.yhi, yhi=self.k)

    def sibling(self):
        return self.device(k=1 - self.k)

    def row_peers(self):
        peers = []
        for d in range(1, 8):
            k, x = self.row(d // 4, d % 4)
            peers.append(self.device(k=k, x=x))
        return peers

    def zy_peers(self):
        peers = [self.device(z=self.along_z(d)) for d in range(1, NZ)]
        for d in range(1, 4):
            yhi, ylo = self.along_y(d)
            peers.append(self.device(ylo=ylo, yhi=yhi))
        return peers


def greet(me, peers, meanwhile):
    barrier = pltpu.get_barrier_semaphore()
    for peer in peers:
        pl.semaphore_signal(barrier, inc=1, device_id=peer, device_id_type=MESH)

    @pl.when(me.moved)
    def _():
        pl.semaphore_signal(barrier, inc=1, device_id=me.partner(), device_id_type=MESH)

    meanwhile()
    pl.semaphore_wait(barrier, len(peers) + me.moved.astype(jnp.int32))


def copy(src, dst, send, recv, to):
    return pltpu.make_async_remote_copy(
        src_ref=src, dst_ref=dst, send_sem=send, recv_sem=recv, device_id=to, device_id_type=MESH
    )


class Sends:
    def __init__(self):
        self.started = []

    def push(self, src, dst, send, recv, to):
        one = copy(src, dst, send, recv, to)
        one.start()
        self.started.append(one)

    def drain(self):
        for one in self.started:
            one.wait_send()


def arrived(ref, send, recv, me):
    copy(ref, ref, send, recv, me.sibling()).wait_recv()


def normalize(values):
    centre = values - jnp.mean(values, axis=-1, keepdims=True)
    inverse = lax.rsqrt(jnp.mean(centre * centre, axis=-1, keepdims=True) + epsilon)
    return centre * inverse, inverse


def first_of(position, lens):
    e0 = lens[0:1, 0:1]
    e1 = e0 + lens[0:1, 1:2]
    e2 = e1 + lens[0:1, 2:3]
    zero = jnp.zeros_like(position)
    start = jnp.where(position >= e0, e0, zero)
    start = jnp.where(position >= e1, e1, start)
    return jnp.where(position >= e2, e2, start)


BUFFERS = {
    "tokr": ((ROWS, D), BF16), "cotr": ((ROWS, D), BF16),
    "len_send": ((8, 128), jnp.int32), "len_recv": ((8, 128), jnp.int32), "lens": ((8, 128), jnp.int32),
    "wi_f": ((8, 16, 128), F32), "wi_send": ((8, 16, 128), BF16), "wi_recv": ((8, 16, 128), BF16),
    "wi_asm": ((2, 16, 512), F32),
    "wo_f": ((4, 16, 128), F32), "wo_send": ((4, 16, 128), BF16), "wo_recv": ((4, 16, 128), BF16),
    "wo_asm": ((16, 256), F32),
    "win": ((NZ, 2, 2, 2, 16, 512), BF16), "wout": ((4, NZ, 2, 2, 2, 16, 256), BF16),
    "normed": ((8, ROWS, D), BF16), "gated": ((8, ROWS, 512), BF16), "slope": ((8, ROWS, 512), BF16),
    "dsend": ((8, ROWS, HD), BF16), "dmix": ((8, ROWS, HD), BF16),
    "attn": ((8, ROWS, HD), BF16), "stats": ((4, 8, ROWS), F32), "every": ((8, 4, 8, ROWS), F32),
    "comb": ((128, ROWS), F32), "msend": ((8, ROWS, HD), BF16), "mixed": ((8, ROWS, HD), BF16),
    "dattn": ((8, ROWS, HD), BF16), "dhidden": ((8, ROWS, 512), BF16), "dquery": ((8, ROWS, HD), F32),
    "lay": ((ROWS, D), BF16), "grad": ((ROWS, D), BF16),
    "esum": ((4, ROWS, D), F32), "es_send": ((4, ROWS, D), BF16), "es_recv": ((4, ROWS, D), BF16),
    "x2_send": ((ROWS, D), BF16), "rl_recv": ((2, 128, D), BF16),
    "nb_send": ((2, ROWS, D), BF16), "nb_recv": ((2, ROWS, D), BF16),
    "gs": ((NZ, 2, 2, 2, 16, 512), BF16),
    "gy": ((3, NZ, 16, 512), BF16), "gz_send": ((NZ, 16, 512), BF16), "gz": ((7, 16, 512), BF16),
    "hz": ((7, 2, 2, 16, 512), BF16), "hy_send": ((2, 2, 16, 512), BF16), "hy": ((3, 16, 512), BF16),
    "gx_f": ((8, 16, 128), F32), "gx_recv": ((8, 16, 128), F32),
    "ps": ((4, NZ, 2, 2, 2, 16, 256), BF16), "pc": ((4, NZ, 2, 2, 16, 256), BF16),
    "pk_sum": ((4, NZ, 2, 2, 16, 256), BF16), "pq": ((3, NZ, 2, 2, 16, 256), BF16), "pq_sum": ((NZ, 2, 2, 16, 256), BF16),
    "py": ((3, NZ, 16, 256), BF16), "pz_send": ((NZ, 16, 256), BF16), "pz": ((7, 16, 256), BF16),
    "px_f": ((4, 8, 128), F32), "px_recv": ((4, 8, 128), F32),
}
SEMAPHORES = {
    "load": (2,), "swap": (4,), "xi": (7,), "xo": (3,), "zi": (7,), "zo": (7,), "yi": (3,), "yo": (3,), "xq": (3,), "core": (4,),
    "zj": (7,), "yj": (3,),
    "ag": (8, 2), "fw": (4, 2), "dm": (7,), "st": (7,), "mx": (7,), "sib": (4,), "rl": (2,), "nb": (2, 2),
    "gy": (3,), "gz": (7,), "hy": (3,), "hz": (7,), "gx": (7,),
    "pc": (1,), "pq": (3,), "py": (3,), "pz": (7,), "px": (3,), "sw": (3,),
}


class Refs:
    def __init__(self, buffers, semaphores):
        for name, ref in zip(BUFFERS, buffers):
            setattr(self, name, ref)
        for n, name in enumerate(SEMAPHORES):
            setattr(self, name + "_s", semaphores[2 * n])
            setattr(self, name + "_r", semaphores[2 * n + 1])


def project(r, block):
    left = r.normed[block]
    for n in range(2):
        cols = pl.ds(n * 256, 256)
        hidden = dot(left, r.win[:, :, :, :, :, cols].reshape(D, 256))
        sigma = 0.5 + 0.5 * jnp.tanh(0.5 * hidden)
        value = hidden * sigma
        r.gated[block, :, cols] = value.astype(BF16)
        r.slope[block, :, cols] = (sigma + value * (1.0 - sigma)).astype(BF16)


def attend(r, i, reach):
    query = r.gated[i, :, 256:384]
    pos = i * ROWS + lax.broadcasted_iota(jnp.int32, (ROWS, 1), 0)
    start = first_of(pos, r.lens)
    total = jnp.zeros((ROWS, HD), F32)
    for off in range(reach + 1):
        j = i - off
        half = dot(query, r.gated[j, :, 384:512], ABT) * HALF_FACTOR
        weights = half + half * jnp.tanh(half)
        other = j * ROWS + lax.broadcasted_iota(jnp.int32, (ROWS, ROWS), 1)
        allowed = other >= start
        if off == 0:
            allowed = allowed & (other <= pos)
        weights = jnp.where(allowed, weights, 0.0).astype(BF16)
        total = total + dot(weights, r.gated[j, :, 128:256])
    r.attn[i] = total.astype(BF16)


def row_stats(r, pair, side):
    i = 2 * pair + side
    value = r.attn[i].astype(F32)
    upstream = r.dmix[i].astype(F32) * r.gated[i, :, 0:128].astype(F32)
    mean = jnp.mean(value, axis=-1, keepdims=True)
    centre = value - mean
    parts = (
        mean,
        jnp.sum(centre * centre, axis=-1, keepdims=True),
        jnp.sum(upstream, axis=-1, keepdims=True),
        jnp.sum(upstream * centre, axis=-1, keepdims=True),
    )
    lane = lax.broadcasted_iota(jnp.int32, (ROWS, HD), 1)
    packed = jnp.zeros((ROWS, HD), F32)
    for n, part in enumerate(parts):
        packed = jnp.where(lane == n, part, packed)
    r.stats[pair, 4 * side : 4 * side + 4] = packed.T[0:4]


def gate_rows(r, pair, side):
    i = 2 * pair + side
    mean, second, total, cross = (r.every[:, pair, 4 * side + n, :] for n in range(4))
    middle = jnp.mean(mean, axis=0, keepdims=True)
    apart = mean - middle
    variance = jnp.sum(second + HD * apart * apart, axis=0, keepdims=True) / D
    inverse = lax.rsqrt(variance + epsilon)
    first = jnp.sum(total, axis=0, keepdims=True) / D
    other = inverse * jnp.sum(cross + apart * total, axis=0, keepdims=True) / D
    r.comb[0:1, :] = middle
    r.comb[1:2, :] = inverse
    r.comb[2:3, :] = first
    r.comb[3:4, :] = other
    turned = r.comb[...].T
    middle, inverse, first, other = (turned[:, n : n + 1] for n in range(4))
    upper = r.gated[i, :, 0:128].astype(F32)
    through = r.dmix[i].astype(F32)
    normal = (r.attn[i].astype(F32) - middle) * inverse
    r.msend[i] = (normal * upper).astype(BF16)
    upstream = through * upper
    r.dattn[i] = (inverse * (upstream - first - normal * other)).astype(BF16)
    r.dhidden[i, :, 0:128] = (through * normal * r.slope[i, :, 0:128].astype(F32)).astype(BF16)


def attend_back(r, j, reach):
    key = r.gated[j, :, 384:512]
    value = r.gated[j, :, 128:256]
    other = j * ROWS + lax.broadcasted_iota(jnp.int32, (ROWS, ROWS), 0)
    dkey = jnp.zeros((ROWS, HD), F32)
    dvalue = jnp.zeros((ROWS, HD), F32)
    for off in range(reach + 1):
        i = j + off
        query = r.gated[i, :, 256:384]
        grad = r.dattn[i]
        half = dot(key, query, ABT) * HALF_FACTOR
        pos = i * ROWS + lax.broadcasted_iota(jnp.int32, (1, ROWS), 1)
        allowed = other >= first_of(pos, r.lens)
        if off == 0:
            allowed = allowed & (other <= pos)
        double = jnp.where(allowed, 1.0 + jnp.tanh(half), 0.0)
        weights = half * double
        bend = double + weights * (2.0 - double)
        dscores = (dot(value, grad, ABT) * bend).astype(BF16)
        dvalue = dvalue + dot(weights.astype(BF16), grad)
        dkey = dkey + dot(dscores, query)
        r.dquery[i] += dot(dscores, key, ATB)
    r.dhidden[j, :, 128:256] = (dvalue * r.slope[j, :, 128:256].astype(F32)).astype(BF16)
    r.dhidden[j, :, 384:512] = (dkey * HALF_FACTOR * r.slope[j, :, 384:512].astype(F32)).astype(BF16)


def kernel(tok, cot, wi, wo, lengths, layer_out, tok_grad, wi_grad, wo_grad, *scratch):
    me = Place()
    z, ylo, k, yhi, x, w = me.z, me.ylo, me.k, me.yhi, me.x, me.w
    r = Refs(scratch[: len(BUFFERS)], scratch[len(BUFFERS) :])
    sends = Sends()
    right, left = me.device(x=(x + 1) % 4), me.device(x=(x + 3) % 4)
    stays = jnp.logical_not(me.moved)

    def row_source(d):
        return (k + 2 - d // 4) % 2, (x + 4 - d % 4) % 4

    load_tok = pltpu.make_async_copy(tok, r.tokr, r.load_r.at[0])
    load_cot = pltpu.make_async_copy(cot, r.cotr, r.load_r.at[1])

    @pl.when(stays)
    def _():
        load_tok.start()
        load_cot.start()

    def prepare():
        wide = wi[...].astype(F32)
        for h in range(HEADS):
            for b in range(4):
                r.wi_f[h, b * 4 : b * 4 + 4, :] = wide[:, b * D + h * HD : b * D + (h + 1) * HD]
        r.wi_send[...] = r.wi_f[...].astype(BF16)
        wide_o = wo[...].astype(F32)
        r.wo_f[...] = jnp.zeros_like(r.wo_f)
        for b in range(8):
            r.wo_f[b // 2, (b % 2) * 4 : (b % 2) * 4 + 4, :] = wide_o[:, b * HD : (b + 1) * HD]
        r.wo_send[...] = r.wo_f[...].astype(BF16)
        r.len_send[...] = jnp.zeros_like(r.len_send)
        r.len_send[0:1, 0:4] = lengths[...]

    greet(me, me.row_peers() + me.zy_peers(), prepare)

    swap_tok = [
        copy(tok.at[part], r.tokr.at[part], r.swap_s.at[n], r.swap_r.at[n], me.partner())
        for n, part in ((0, pl.ds(0, 128)), (1, pl.ds(128, 128)))
    ]
    swap_cot = copy(cot, r.cotr, r.swap_s.at[2], r.swap_r.at[2], me.partner())

    for d in range(1, 8):
        pk, px = me.row(d // 4, d % 4)
        sends.push(
            r.wi_send.at[2 * px + pk], r.wi_recv.at[w], r.xi_s.at[d - 1], r.xi_r.at[d - 1], me.device(k=pk, x=px)
        )
    r.wi_recv[w] = r.wi_send[me.head]
    for d in range(1, 4):
        pk, px = me.row(0, d)
        sends.push(r.wo_send.at[px], r.wo_recv.at[x], r.xo_s.at[d - 1], r.xo_r.at[d - 1], me.device(x=px))
    r.wo_recv[x] = r.wo_send[x]

    @pl.when(me.moved)
    def _():
        swap_tok[0].start()
        swap_tok[1].start()

    sends.push(r.len_send, r.len_recv, r.swap_s.at[3], r.swap_r.at[3], me.sibling())

    def norm_half(half):
        part = pl.ds(half * 128, 128)
        r.normed[w, part] = normalize(r.tokr[part].astype(F32))[0].astype(BF16)

    def own(half):
        return r.normed.at[w, pl.ds(half * 128, 128)]

    own_sends = []
    for half in range(2):
        own_sends.append(copy(own(half), own(half), r.ag_s.at[3, half], r.ag_r.at[3, half], right))
        own_sends.append(copy(own(half), own(half), r.ag_s.at[1, half], r.ag_r.at[1, half], left))
        own_sends.append(copy(own(half), own(half), r.fw_s.at[0, half], r.ag_r.at[4, half], me.sibling()))

    def rows_of(dx, half):
        return r.normed.at[k * 4 + (x + dx) % 4, pl.ds(half * 128, 128)]

    def onward(dx, half, sem, recv, to):
        return copy(rows_of(dx, half), rows_of(dx, half), sem, recv, to)

    first_sends = [
        onward(3, 0, r.ag_s.at[2, 0], r.ag_r.at[2, 0], right),
        onward(3, 0, r.fw_s.at[3, 0], r.ag_r.at[7, 0], me.sibling()),
        onward(1, 1, r.ag_s.at[2, 1], r.ag_r.at[2, 1], left),
        onward(1, 1, r.fw_s.at[1, 1], r.ag_r.at[5, 1], me.sibling()),
    ]

    def take_first():
        arrived(rows_of(3, 0), r.ag_s.at[3, 0], r.ag_r.at[3, 0], me)
        first_sends[0].start()
        first_sends[1].start()
        arrived(rows_of(1, 1), r.ag_s.at[1, 1], r.ag_r.at[1, 1], me)
        first_sends[2].start()
        first_sends[3].start()

    def take(dx, half):
        part = rows_of(dx, half)
        arrived(part, r.ag_s.at[dx, half], r.ag_r.at[dx, half], me)
        sends.push(part, part, r.fw_s.at[dx, half], r.ag_r.at[4 + dx, half], me.sibling())

    @pl.when(stays)
    def _():
        load_tok.wait()
        norm_half(0)
        norm_half(1)
        for n in (0, 4, 3, 1, 2, 5):
            own_sends[n].start()

    for d in range(1, 8):
        sk, sx = row_source(d)
        arrived(r.wi_recv.at[sk * 4 + sx], r.xi_s.at[d - 1], r.xi_r.at[d - 1], me)
    for src in range(8):
        piece = r.wi_recv[src].astype(F32)
        for b in range(4):
            r.wi_asm[src // 4, (src % 4) * 4 : (src % 4) * 4 + 4, b * HD : (b + 1) * HD] = piece[b * 4 : b * 4 + 4]
    for c in range(2):
        r.win[z, ylo, c, yhi] = r.wi_asm[c].astype(BF16)
    for d in range(1, 4):
        phi, plo = me.along_y(d)
        part = r.win.at[z, ylo, 1, yhi]
        sends.push(part, part, r.yj_s.at[d - 1], r.yj_r.at[d - 1], me.device(ylo=plo, yhi=phi))
    for d in range(1, NZ):
        part = r.win.at[z, ylo, 0, yhi]
        sends.push(part, part, r.zi_s.at[d - 1], r.zi_r.at[d - 1], me.device(z=me.along_z(d)))

    for d in range(1, 4):
        arrived(r.wo_recv.at[(x + 4 - d) % 4], r.xo_s.at[d - 1], r.xo_r.at[d - 1], me)
    for src in range(4):
        piece = r.wo_recv[src].astype(F32)
        for b in range(2):
            r.wo_asm[src * 4 : src * 4 + 4, b * HD : (b + 1) * HD] = piece[b * 4 : b * 4 + 4]
    r.wout[x, z, ylo, k, yhi] = r.wo_asm[...].astype(BF16)
    for d in range(1, NZ):
        part = r.wout.at[x, z, ylo, k, yhi]
        sends.push(part, part, r.zo_s.at[d - 1], r.zo_r.at[d - 1], me.device(z=me.along_z(d)))

    @pl.when(stays)
    def _():
        take_first()

    @pl.when(me.moved)
    def _():
        swap_tok[0].wait_recv()
        norm_half(0)
        for n in (0, 1, 2):
            own_sends[n].start()
        swap_tok[1].wait_recv()
        norm_half(1)
        for n in (4, 3, 5):
            own_sends[n].start()

    for d in range(1, 4):
        shi, slo = me.along_y(4 - d)
        arrived(r.win.at[z, slo, 1, shi], r.yj_s.at[d - 1], r.yj_r.at[d - 1], me)
    for d in range(1, NZ):
        part = r.win.at[z, :, 1, :]
        sends.push(part, part, r.zj_s.at[d - 1], r.zj_r.at[d - 1], me.device(z=me.along_z(d)))

    for d in range(1, NZ):
        arrived(r.win.at[(z + NZ - d) % NZ, ylo, 0, yhi], r.zi_s.at[d - 1], r.zi_r.at[d - 1], me)
    for d in range(1, 4):
        phi, plo = me.along_y(d)
        part = r.win.at[:, ylo, 0, yhi]
        sends.push(part, part, r.yi_s.at[d - 1], r.yi_r.at[d - 1], me.device(ylo=plo, yhi=phi))

    for d in range(1, NZ):
        arrived(r.wout.at[x, (z + NZ - d) % NZ, ylo, k, yhi], r.zo_s.at[d - 1], r.zo_r.at[d - 1], me)
    for d in range(1, 4):
        phi, plo = me.along_y(d)
        part = r.wout.at[x, :, ylo, k, yhi]
        sends.push(part, part, r.yo_s.at[d - 1], r.yo_r.at[d - 1], me.device(ylo=plo, yhi=phi))

    @pl.when(me.moved)
    def _():
        swap_cot.start()
        take_first()

    take(3, 1)
    take(1, 0)
    take(2, 0)
    take(2, 1)
    for d in range(1, 4):
        shi, slo = me.along_y(4 - d)
        arrived(r.wout.at[x, :, slo, k, shi], r.yo_s.at[d - 1], r.yo_r.at[d - 1], me)
    part = r.wout.at[x, :, :, k]
    for d in range(1, 4):
        pk, px = me.row(0, d)
        sends.push(part, part, r.xq_s.at[d - 1], r.xq_r.at[d - 1], me.device(x=px))
    sends.push(part, part, r.core_s.at[0], r.core_r.at[0], me.sibling())
    arrived(r.len_recv, r.swap_s.at[3], r.swap_r.at[3], me)
    r.lens[...] = jnp.where(me.moved, r.len_recv[...], r.len_send[...])
    for d in range(1, 4):
        shi, slo = me.along_y(4 - d)
        arrived(r.win.at[:, slo, 0, shi], r.yi_s.at[d - 1], r.yi_r.at[d - 1], me)
    for d in range(1, NZ):
        arrived(r.win.at[(z + NZ - d) % NZ, :, 1, :], r.zj_s.at[d - 1], r.zj_r.at[d - 1], me)

    @pl.loop(0, 4)
    def _(i):
        project(r, k * 4 + i)

    for dx in range(4):
        for half in range(2):
            arrived(
                r.normed.at[(1 - k) * 4 + (x + dx) % 4, pl.ds(half * 128, 128)],
                r.fw_s.at[dx, half], r.ag_r.at[4 + dx, half], me,
            )

    @pl.loop(0, 4)
    def _(i):
        project(r, (1 - k) * 4 + i)

    for i in range(4):
        attend(r, i, i)

    for d in range(1, 4):
        part = r.wout.at[(x + 4 - d) % 4, :, :, k]
        arrived(part, r.xq_s.at[d - 1], r.xq_r.at[d - 1], me)
        sends.push(part, part, r.core_s.at[d], r.core_r.at[d], me.sibling())

    @pl.loop(4, 8)
    def _(i):
        attend(r, i, 4)

    @pl.when(me.moved)
    def _():
        swap_cot.wait_recv()

    @pl.when(stays)
    def _():
        load_cot.wait()

    for d in range(4):
        arrived(r.wout.at[(x + 4 - d) % 4, :, :, 1 - k], r.core_s.at[d], r.core_r.at[d], me)

    @pl.loop(0, 4)
    def _(i):
        pair = jnp.zeros((ROWS, 256), F32)
        for q in range(4):
            pair = pair + dot(r.cotr[:, q * 256 : (q + 1) * 256], r.wout[q, pl.ds(2 * i, 2)].reshape(256, 256), ABT)
        r.dsend[2 * i] = pair[:, :HD].astype(BF16)
        r.dsend[2 * i + 1] = pair[:, HD:].astype(BF16)

    r.dmix[w] = r.dsend[me.head]
    for d in range(1, 8):
        pk, px = me.row(d // 4, d % 4)
        sends.push(
            r.dsend.at[2 * px + pk], r.dmix.at[w], r.dm_s.at[d - 1], r.dm_r.at[d - 1], me.device(k=pk, x=px)
        )
    for d in range(1, 8):
        sk, sx = row_source(d)
        arrived(r.dmix.at[sk * 4 + sx], r.dm_s.at[d - 1], r.dm_r.at[d - 1], me)

    @pl.loop(0, 4)
    def _(pair):
        row_stats(r, pair, 0)
        row_stats(r, pair, 1)

    for d in range(1, 8):
        pk, px = me.row(d // 4, d % 4)
        sends.push(r.stats, r.every.at[w], r.st_s.at[d - 1], r.st_r.at[d - 1], me.device(k=pk, x=px))
    r.every[w] = r.stats[...]
    r.comb[...] = jnp.zeros_like(r.comb)
    r.dquery[...] = jnp.zeros_like(r.dquery)
    for d in range(1, 8):
        sk, sx = row_source(d)
        arrived(r.every.at[sk * 4 + sx], r.st_s.at[d - 1], r.st_r.at[d - 1], me)

    @pl.loop(0, 4)
    def _(pair):
        gate_rows(r, pair, 0)
        gate_rows(r, pair, 1)

    r.mixed[me.head] = r.msend[w]
    for d in range(1, 8):
        pk, px = me.row(d // 4, d % 4)
        sends.push(
            r.msend.at[pk * 4 + px], r.mixed.at[me.head], r.mx_s.at[d - 1], r.mx_r.at[d - 1], me.device(k=pk, x=px)
        )

    @pl.loop(0, 3)
    def _(j):
        attend_back(r, j, 4)

    for d in range(1, 8):
        sk, sx = row_source(d)
        arrived(r.mixed.at[2 * sx + sk], r.mx_s.at[d - 1], r.mx_r.at[d - 1], me)

    @pl.loop(0, 4)
    def _(n):
        pair = jnp.concatenate([r.mixed[2 * n], r.mixed[2 * n + 1]], axis=1)
        product = dot(pair, r.cotr[...], ATB).astype(BF16)
        for q in range(4):
            r.ps[q, pl.ds(2 * n, 2)] = product[:, q * 256 : (q + 1) * 256].reshape(2, 2, 2, 2, 16, 256)

    sends.push(r.ps.at[:, :, :, 1 - k], r.pc, r.pc_s.at[0], r.pc_r.at[0], me.sibling())

    joined = jnp.concatenate([r.mixed[h] for h in range(HEADS)], axis=1)
    for n in range(4):
        cols = pl.ds(n * 256, 256)
        product = dot(joined, r.wout[n].reshape(D, 256))
        r.lay[:, cols] = (product + r.tokr[:, cols].astype(F32)).astype(BF16)
    swap_lay = copy(r.lay, layer_out, r.sw_s.at[0], r.sw_r.at[0], me.partner())
    swap_grad = [
        copy(r.grad.at[part], tok_grad.at[part], r.sw_s.at[n], r.sw_r.at[n], me.partner())
        for n, part in ((1, pl.ds(0, 128)), (2, pl.ds(128, 128)))
    ]

    @pl.when(stays)
    def _():
        layer_out[...] = r.lay[...]

    arrived(r.pc, r.pc_s.at[0], r.pc_r.at[0], me)

    @pl.loop(0, NZ)
    def _(n):
        for q in range(4):
            r.pk_sum[q, n] = (r.ps[q, n, :, k].astype(F32) + r.pc[q, n].astype(F32)).astype(BF16)

    for d in range(1, 4):
        pk, px = me.row(0, d)
        sends.push(r.pk_sum.at[px], r.pq.at[d - 1], r.pq_s.at[d - 1], r.pq_r.at[d - 1], me.device(x=px))

    @pl.when(me.moved)
    def _():
        swap_lay.start()

    @pl.loop(3, 4)
    def _(j):
        attend_back(r, j, 4)

    for j in range(4, 8):
        attend_back(r, j, 7 - j)

    @pl.loop(0, 8)
    def _(i):
        r.dhidden[i, :, 256:384] = (r.dquery[i] * HALF_FACTOR * r.slope[i, :, 256:384].astype(F32)).astype(BF16)

    def back_product(block, n):
        return dot(r.dhidden[block], r.win[pl.ds(2 * n, 2)].reshape(256, 512), ABT)

    def partial(dx):
        there = (1 - k) * 4 + (x + dx) % 4
        here = k * 4 + (x + dx) % 4

        @pl.loop(0, 4)
        def _(n):
            cols = pl.ds(pl.multiple_of(n * 256, 256), 256)
            r.es_send[dx, :, cols] = back_product(there, n).astype(BF16)

        sends.push(r.es_send.at[dx], r.es_recv.at[dx], r.sib_s.at[dx], r.sib_r.at[dx], me.sibling())

        @pl.loop(0, 4)
        def _(n):
            cols = pl.ds(pl.multiple_of(n * 256, 256), 256)
            r.esum[dx, :, cols] = back_product(here, n)

    def from_sibling(dx):
        arrived(r.es_recv.at[dx], r.sib_s.at[dx], r.sib_r.at[dx], me)

    def to_neighbour(side, half, extra):
        part = pl.ds(half * 128, 128)
        dx = 1 + 2 * side
        total = r.esum[dx, part] + r.es_recv[dx, part].astype(F32)
        if extra is not None:
            total = total + extra.astype(F32)
        r.nb_send[side, part] = total.astype(BF16)
        sends.push(
            r.nb_send.at[side, part], r.nb_recv.at[side, part],
            r.nb_s.at[side, half], r.nb_r.at[side, half], (right, left)[side],
        )

    partial(2)
    partial(1)
    from_sibling(2)
    r.x2_send[...] = (r.esum[2] + r.es_recv[2].astype(F32)).astype(BF16)
    sends.push(r.x2_send.at[pl.ds(0, 128)], r.rl_recv.at[0], r.rl_s.at[0], r.rl_r.at[0], right)
    sends.push(r.x2_send.at[pl.ds(128, 128)], r.rl_recv.at[1], r.rl_s.at[1], r.rl_r.at[1], left)
    partial(3)
    from_sibling(1)
    to_neighbour(0, 1, None)
    from_sibling(3)
    to_neighbour(1, 0, None)

    @pl.loop(0, 4)
    def _(n):
        cols = pl.ds(pl.multiple_of(n * 256, 256), 256)
        product = dot(r.normed[:, :, cols].reshape(8 * ROWS, 256), r.dhidden[...].reshape(8 * ROWS, 512), ATB)
        r.gs[pl.ds(2 * n, 2)] = product.astype(BF16).reshape(2, 2, 2, 2, 16, 512)

    for d in range(1, NZ):
        to = me.along_z(d)
        sends.push(r.gs.at[to, :, 1, :], r.hz.at[d - 1], r.hz_s.at[d - 1], r.hz_r.at[d - 1], me.device(z=to))
    for d in range(1, 4):
        phi, plo = me.along_y(d)
        sends.push(
            r.gs.at[:, plo, 0, phi], r.gy.at[d - 1], r.gy_s.at[d - 1], r.gy_r.at[d - 1], me.device(ylo=plo, yhi=phi)
        )

    for d in range(1, 4):
        arrived(r.pq.at[d - 1], r.pq_s.at[d - 1], r.pq_r.at[d - 1], me)

    @pl.loop(0, NZ)
    def _(n):
        total = r.pk_sum[x, n].astype(F32)
        for d in range(3):
            total = total + r.pq[d, n].astype(F32)
        r.pq_sum[n] = total.astype(BF16)

    for d in range(1, 4):
        phi, plo = me.along_y(d)
        sends.push(
            r.pq_sum.at[:, plo, phi], r.py.at[d - 1], r.py_s.at[d - 1], r.py_r.at[d - 1], me.device(ylo=plo, yhi=phi)
        )

    for side in range(2):
        arrived(r.rl_recv.at[side], r.rl_s.at[side], r.rl_r.at[side], me)
        to_neighbour(side, side, r.rl_recv[side])
    partial(0)

    for d in range(1, 4):
        arrived(r.gy.at[d - 1], r.gy_s.at[d - 1], r.gy_r.at[d - 1], me)

    @pl.loop(0, NZ)
    def _(n):
        total = r.gs[n, ylo, 0, yhi].astype(F32)
        for d in range(3):
            total = total + r.gy[d, n].astype(F32)
        r.gz_send[n] = total.astype(BF16)

    for d in range(1, NZ):
        to = me.along_z(d)
        sends.push(r.gz_send.at[to], r.gz.at[d - 1], r.gz_s.at[d - 1], r.gz_r.at[d - 1], me.device(z=to))
    for d in range(1, NZ):
        arrived(r.hz.at[d - 1], r.hz_s.at[d - 1], r.hz_r.at[d - 1], me)
    for n in range(2):
        total = r.gs[z, n, 1].astype(F32)
        for d in range(7):
            total = total + r.hz[d, n].astype(F32)
        r.hy_send[n] = total.astype(BF16)
    for d in range(1, 4):
        phi, plo = me.along_y(d)
        sends.push(
            r.hy_send.at[plo, phi], r.hy.at[d - 1], r.hy_s.at[d - 1], r.hy_r.at[d - 1], me.device(ylo=plo, yhi=phi)
        )

    for d in range(1, 4):
        arrived(r.py.at[d - 1], r.py_s.at[d - 1], r.py_r.at[d - 1], me)

    @pl.loop(0, NZ)
    def _(n):
        total = r.pq_sum[n, ylo, yhi].astype(F32)
        for d in range(3):
            total = total + r.py[d, n].astype(F32)
        r.pz_send[n] = total.astype(BF16)

    for d in range(1, NZ):
        to = me.along_z(d)
        sends.push(r.pz_send.at[to], r.pz.at[d - 1], r.pz_s.at[d - 1], r.pz_r.at[d - 1], me.device(z=to))

    from_sibling(0)

    def finish(half):
        for side in range(2):
            arrived(r.nb_recv.at[side, pl.ds(half * 128, 128)], r.nb_s.at[side, half], r.nb_r.at[side, half], me)
        for n in range(2):
            part = pl.ds(half * 128 + n * 64, 64)
            upstream = (
                r.esum[0, part]
                + r.es_recv[0, part].astype(F32)
                + r.nb_recv[0, part].astype(F32)
                + r.nb_recv[1, part].astype(F32)
            )
            normal, inverse = normalize(r.tokr[part].astype(F32))
            first = jnp.mean(upstream, axis=-1, keepdims=True)
            second = jnp.mean(upstream * normal, axis=-1, keepdims=True)
            r.grad[part] = (inverse * (upstream - first - normal * second) + r.cotr[part].astype(F32)).astype(BF16)

        @pl.when(me.moved)
        def _():
            swap_grad[half].start()

        @pl.when(stays)
        def _():
            part = pl.ds(half * 128, 128)
            tok_grad[part] = r.grad[part]

    finish(0)
    finish(1)

    for d in range(1, NZ):
        arrived(r.pz.at[d - 1], r.pz_s.at[d - 1], r.pz_r.at[d - 1], me)
    total = r.pz_send[z].astype(F32)
    for d in range(1, NZ):
        total = total + r.pz[d - 1].astype(F32)
    for px in range(4):
        for b in range(2):
            r.px_f[px, b * 4 : b * 4 + 4, :] = total[px * 4 : px * 4 + 4, b * HD : (b + 1) * HD]
    r.px_recv[x] = r.px_f[x]
    for d in range(1, 4):
        pk, px = me.row(0, d)
        sends.push(r.px_f.at[px], r.px_recv.at[x], r.px_s.at[d - 1], r.px_r.at[d - 1], me.device(x=px))

    for d in range(1, NZ):
        arrived(r.gz.at[d - 1], r.gz_s.at[d - 1], r.gz_r.at[d - 1], me)
    for d in range(1, 4):
        arrived(r.hy.at[d - 1], r.hy_s.at[d - 1], r.hy_r.at[d - 1], me)
    total = r.gz_send[z].astype(F32)
    for d in range(7):
        total = total + r.gz[d].astype(F32)
    other = r.hy_send[ylo, yhi].astype(F32)
    for d in range(3):
        other = other + r.hy[d].astype(F32)
    for c in range(2):
        for px in range(4):
            for b in range(4):
                r.gx_f[c * 4 + px, b * 4 : b * 4 + 4, :] = (total, other)[c][
                    px * 4 : px * 4 + 4, b * HD : (b + 1) * HD
                ]
    r.gx_recv[w] = r.gx_f[w]
    for d in range(1, 8):
        pk, px = me.row(d // 4, d % 4)
        sends.push(
            r.gx_f.at[pk * 4 + px], r.gx_recv.at[w], r.gx_s.at[d - 1], r.gx_r.at[d - 1], me.device(k=pk, x=px)
        )

    for d in range(1, 4):
        arrived(r.px_recv.at[(x + 4 - d) % 4], r.px_s.at[d - 1], r.px_r.at[d - 1], me)
    for b in range(8):
        wo_grad[:, b * HD : (b + 1) * HD] = r.px_recv[b // 2, (b % 2) * 4 : (b % 2) * 4 + 4]
    for d in range(1, 8):
        sk, sx = row_source(d)
        arrived(r.gx_recv.at[sk * 4 + sx], r.gx_s.at[d - 1], r.gx_r.at[d - 1], me)
    for src in range(8):
        h = 2 * (src % 4) + src // 4
        for b in range(4):
            wi_grad[:, b * D + h * HD : b * D + (h + 1) * HD] = r.gx_recv[src, b * 4 : b * 4 + 4, :]
    sends.drain()
    for one in own_sends + first_sends:
        one.wait_send()

    @pl.when(me.moved)
    def _():
        for one in swap_tok:
            one.wait_send()
        swap_cot.wait_send()
        swap_lay.wait()
        for one in swap_grad:
            one.wait()


def local(tokens, lengths, in_weight, out_weight, cotangent):
    anywhere = pl.BlockSpec(memory_space=pl.ANY)
    shapes = [((ROWS, D), BF16), ((ROWS, D), BF16), ((4, 4 * D), F32), ((4, D), F32)]
    scratch = [pltpu.VMEM(shape, kind) for shape, kind in BUFFERS.values()]
    for shape in SEMAPHORES.values():
        scratch += [DMA(shape), DMA(shape)]
    return tuple(
        pl.pallas_call(
            kernel,
            out_shape=[jax.ShapeDtypeStruct(s, t) for s, t in shapes],
            in_specs=[anywhere, anywhere, VMEM, VMEM, VMEM],
            out_specs=[VMEM] * 4,
            scratch_shapes=scratch,
            compiler_params=pltpu.CompilerParams(
                collective_id=0, has_side_effects=True, vmem_limit_bytes=60 << 20
            ),
            name="layer",
        )(tokens, cotangent, in_weight, out_weight, lengths)
    )


def solution(mesh):
    both = P(("dp", "seq"), None)
    return jax.shard_map(
        local,
        mesh=mesh,
        in_specs=(both, P("dp", None), both, both, both),
        out_specs=(both, both, both, both),
        check_vma=False,
    )
```

```python
import functools

import jax
import jax.numpy as jnp
from jax import lax
from jax.experimental import pallas as pl
from jax.experimental.pallas import tpu as pltpu
from jax.sharding import PartitionSpec as P

F32 = jnp.float32
BF16 = jnp.bfloat16
MESH = pl.DeviceIdType.MESH
DMA = pltpu.SemaphoreType.DMA

D = 1024
HEADS = 8
HD = 128
ROWS = 256
NZ = 8
epsilon = 1e-05
HALF_FACTOR = 0.5 * HD ** (-0.5)
VMEM = pl.BlockSpec(memory_space=pltpu.VMEM)
ABT = (((1,), (1,)), ((), ()))
ATB = (((0,), (0,)), ((), ()))


def dot(a, b, dims=(((1,), (0,)), ((), ()))):
    return lax.dot_general(a, b, dims, preferred_element_type=F32)


class Place:
    def __init__(self):
        g = lax.axis_index("dp")
        s = lax.axis_index("seq")
        self.z, self.ylo, self.k = g // 4, (g // 2) % 2, g % 2
        self.yhi, self.x = s // 4, s % 4
        self.w = self.k * 4 + self.x
        self.head = 2 * self.x + self.k
        self.moved = self.k != self.yhi

    def device(self, z=None, ylo=None, k=None, yhi=None, x=None):
        z = self.z if z is None else z
        ylo = self.ylo if ylo is None else ylo
        k = self.k if k is None else k
        yhi = self.yhi if yhi is None else yhi
        x = self.x if x is None else x
        return (z * 4 + ylo * 2 + k, yhi * 4 + x)

    def row(self, dk, dx):
        return (self.k + dk) % 2, (self.x + dx) % 4

    def along_z(self, d):
        return (self.z + d) % NZ

    def along_y(self, d):
        y = (self.yhi * 2 + self.ylo + d) % 4
        return y // 2, y % 2

    def partner(self):
        return self.device(k=self.yhi, yhi=self.k)

    def sibling(self):
        return self.device(k=1 - self.k)

    def row_peers(self):
        peers = []
        for d in range(1, 8):
            k, x = self.row(d // 4, d % 4)
            peers.append(self.device(k=k, x=x))
        return peers

    def zy_peers(self):
        peers = [self.device(z=self.along_z(d)) for d in range(1, NZ)]
        for d in range(1, 4):
            yhi, ylo = self.along_y(d)
            peers.append(self.device(ylo=ylo, yhi=yhi))
        return peers


def greet(me, peers, meanwhile):
    barrier = pltpu.get_barrier_semaphore()
    for peer in peers:
        pl.semaphore_signal(barrier, inc=1, device_id=peer, device_id_type=MESH)

    @pl.when(me.moved)
    def _():
        pl.semaphore_signal(barrier, inc=1, device_id=me.partner(), device_id_type=MESH)

    meanwhile()
    pl.semaphore_wait(barrier, len(peers) + me.moved.astype(jnp.int32))


def copy(src, dst, send, recv, to):
    return pltpu.make_async_remote_copy(
        src_ref=src, dst_ref=dst, send_sem=send, recv_sem=recv, device_id=to, device_id_type=MESH
    )


class Sends:
    def __init__(self):
        self.started = []

    def push(self, src, dst, send, recv, to):
        one = copy(src, dst, send, recv, to)
        one.start()
        self.started.append(one)

    def drain(self):
        for one in self.started:
            one.wait_send()


def arrived(ref, send, recv, me):
    copy(ref, ref, send, recv, me.sibling()).wait_recv()


def normalize(values):
    centre = values - jnp.mean(values, axis=-1, keepdims=True)
    inverse = lax.rsqrt(jnp.mean(centre * centre, axis=-1, keepdims=True) + epsilon)
    return centre * inverse, inverse


def first_of(position, lens):
    e0 = lens[0:1, 0:1]
    e1 = e0 + lens[0:1, 1:2]
    e2 = e1 + lens[0:1, 2:3]
    zero = jnp.zeros_like(position)
    start = jnp.where(position >= e0, e0, zero)
    start = jnp.where(position >= e1, e1, start)
    return jnp.where(position >= e2, e2, start)


BUFFERS = {
    "tokr": ((ROWS, D), BF16), "cotr": ((ROWS, D), BF16),
    "len_send": ((8, 128), jnp.int32), "len_recv": ((8, 128), jnp.int32), "lens": ((8, 128), jnp.int32),
    "wi_f": ((8, 16, 128), F32), "wi_send": ((8, 16, 128), BF16), "wi_recv": ((8, 16, 128), BF16),
    "wi_asm": ((2, 16, 512), F32),
    "wo_f": ((2, 16, 128), F32), "wo_send": ((2, 16, 128), BF16), "wo_recv": ((4, 16, 128), BF16),
    "wo_asm": ((2, 16, 256), F32),
    "win": ((NZ, 2, 2, 2, 16, 512), BF16), "wout": ((2, 2, NZ, 2, 2, 2, 16, 256), BF16),
    "normed": ((8, ROWS, D), BF16), "gated": ((8, ROWS, 512), BF16), "slope": ((8, ROWS, 512), BF16),
    "dsend": ((8, ROWS, HD), BF16), "dmix": ((8, ROWS, HD), BF16),
    "attn": ((8, ROWS, HD), BF16), "stats": ((4, 8, ROWS), F32), "every": ((8, 4, 8, ROWS), F32),
    "comb": ((128, ROWS), F32), "msend": ((8, ROWS, HD), BF16), "mixed": ((8, ROWS, HD), BF16),
    "dattn": ((8, ROWS, HD), BF16), "dhidden": ((8, ROWS, 512), BF16), "dquery": ((8, ROWS, HD), F32),
    "lay": ((ROWS, D), BF16), "grad": ((ROWS, D), BF16),
    "esum": ((4, ROWS, D), F32), "es_send": ((4, ROWS, D), BF16), "es_recv": ((4, ROWS, D), BF16),
    "x2_send": ((ROWS, D), BF16), "rl_recv": ((2, 128, D), BF16),
    "nb_send": ((2, ROWS, D), BF16), "nb_recv": ((2, ROWS, D), BF16),
    "gs": ((NZ, 2, 2, 2, 16, 512), BF16),
    "gy": ((3, NZ, 16, 512), BF16), "gz_send": ((NZ, 16, 512), BF16), "gz": ((7, 16, 512), BF16),
    "hz": ((7, 2, 2, 16, 512), BF16), "hy_send": ((2, 2, 16, 512), BF16), "hy": ((3, 16, 512), BF16),
    "gx_f": ((8, 16, 128), F32), "gx_recv": ((8, 16, 128), F32),
    "ps": ((2, 2, NZ, 2, 2, 2, 16, 256), BF16), "pc": ((2, 2, NZ, 2, 2, 16, 256), BF16),
    "pk_sum": ((2, 2, NZ, 2, 2, 16, 256), BF16), "pq": ((2, NZ, 2, 2, 16, 256), BF16),
    "pq_sum": ((2, NZ, 2, 2, 16, 256), BF16),
    "py": ((3, 2, NZ, 16, 256), BF16), "pz_send": ((NZ, 2, 16, 256), BF16), "pz": ((7, 2, 16, 256), BF16),
    "px_f": ((4, 16, 128), F32), "px_recv": ((4, 16, 128), F32),
}
SEMAPHORES = {
    "load": (2,), "swap": (6,), "xi": (7,), "xo": (3,), "zi": (7,), "zo": (7,), "yi": (3,), "yo": (3,), "xq": (2,), "core": (3,),
    "zj": (7,), "yj": (3,),
    "ag": (8, 4), "fw": (4, 4), "dm": (7,), "st": (7,), "mx": (7,), "sib": (4,), "rl": (2,), "nb": (2, 2),
    "gy": (3,), "gz": (7,), "hy": (3,), "hz": (7,), "gx": (7,),
    "pc": (1,), "pq": (2,), "py": (3,), "pz": (7,), "px": (3,), "sw": (3,),
}


class Refs:
    def __init__(self, buffers, semaphores):
        for name, ref in zip(BUFFERS, buffers):
            setattr(self, name, ref)
        for n, name in enumerate(SEMAPHORES):
            setattr(self, name + "_s", semaphores[2 * n])
            setattr(self, name + "_r", semaphores[2 * n + 1])


def project(r, block):
    left = r.normed[block]
    for n in range(2):
        cols = pl.ds(n * 256, 256)
        hidden = dot(left, r.win[:, :, :, :, :, cols].reshape(D, 256))
        sigma = 0.5 + 0.5 * jnp.tanh(0.5 * hidden)
        value = hidden * sigma
        r.gated[block, :, cols] = value.astype(BF16)
        r.slope[block, :, cols] = (sigma + value * (1.0 - sigma)).astype(BF16)


def attend(r, i, reach):
    query = r.gated[i, :, 256:384]
    pos = i * ROWS + lax.broadcasted_iota(jnp.int32, (ROWS, 1), 0)
    start = first_of(pos, r.lens)
    total = jnp.zeros((ROWS, HD), F32)
    for off in range(reach + 1):
        j = i - off
        half = dot(query, r.gated[j, :, 384:512], ABT) * HALF_FACTOR
        weights = half + half * jnp.tanh(half)
        other = j * ROWS + lax.broadcasted_iota(jnp.int32, (ROWS, ROWS), 1)
        allowed = other >= start
        if off == 0:
            allowed = allowed & (other <= pos)
        weights = jnp.where(allowed, weights, 0.0).astype(BF16)
        total = total + dot(weights, r.gated[j, :, 128:256])
    r.attn[i] = total.astype(BF16)


def row_stats(r, pair, side):
    i = 2 * pair + side
    value = r.attn[i].astype(F32)
    upstream = r.dmix[i].astype(F32) * r.gated[i, :, 0:128].astype(F32)
    mean = jnp.mean(value, axis=-1, keepdims=True)
    centre = value - mean
    parts = (
        mean,
        jnp.sum(centre * centre, axis=-1, keepdims=True),
        jnp.sum(upstream, axis=-1, keepdims=True),
        jnp.sum(upstream * centre, axis=-1, keepdims=True),
    )
    lane = lax.broadcasted_iota(jnp.int32, (ROWS, HD), 1)
    packed = jnp.zeros((ROWS, HD), F32)
    for n, part in enumerate(parts):
        packed = jnp.where(lane == n, part, packed)
    r.stats[pair, 4 * side : 4 * side + 4] = packed.T[0:4]


def gate_rows(r, pair, side):
    i = 2 * pair + side
    mean, second, total, cross = (r.every[:, pair, 4 * side + n, :] for n in range(4))
    middle = jnp.mean(mean, axis=0, keepdims=True)
    apart = mean - middle
    variance = jnp.sum(second + HD * apart * apart, axis=0, keepdims=True) / D
    inverse = lax.rsqrt(variance + epsilon)
    first = jnp.sum(total, axis=0, keepdims=True) / D
    other = inverse * jnp.sum(cross + apart * total, axis=0, keepdims=True) / D
    r.comb[0:1, :] = middle
    r.comb[1:2, :] = inverse
    r.comb[2:3, :] = first
    r.comb[3:4, :] = other
    turned = r.comb[...].T
    middle, inverse, first, other = (turned[:, n : n + 1] for n in range(4))
    upper = r.gated[i, :, 0:128].astype(F32)
    through = r.dmix[i].astype(F32)
    normal = (r.attn[i].astype(F32) - middle) * inverse
    r.msend[i] = (normal * upper).astype(BF16)
    upstream = through * upper
    r.dattn[i] = (inverse * (upstream - first - normal * other)).astype(BF16)
    r.dhidden[i, :, 0:128] = (through * normal * r.slope[i, :, 0:128].astype(F32)).astype(BF16)


def attend_back(r, j, reach):
    key = r.gated[j, :, 384:512]
    value = r.gated[j, :, 128:256]
    other = j * ROWS + lax.broadcasted_iota(jnp.int32, (ROWS, ROWS), 0)
    dkey = jnp.zeros((ROWS, HD), F32)
    dvalue = jnp.zeros((ROWS, HD), F32)
    for off in range(reach + 1):
        i = j + off
        query = r.gated[i, :, 256:384]
        grad = r.dattn[i]
        half = dot(key, query, ABT) * HALF_FACTOR
        pos = i * ROWS + lax.broadcasted_iota(jnp.int32, (1, ROWS), 1)
        allowed = other >= first_of(pos, r.lens)
        if off == 0:
            allowed = allowed & (other <= pos)
        double = jnp.where(allowed, 1.0 + jnp.tanh(half), 0.0)
        weights = half * double
        bend = double + weights * (2.0 - double)
        dscores = (dot(value, grad, ABT) * bend).astype(BF16)
        dvalue = dvalue + dot(weights.astype(BF16), grad)
        dkey = dkey + dot(dscores, query)
        r.dquery[i] += dot(dscores, key, ATB)
    r.dhidden[j, :, 128:256] = (dvalue * r.slope[j, :, 128:256].astype(F32)).astype(BF16)
    r.dhidden[j, :, 384:512] = (dkey * HALF_FACTOR * r.slope[j, :, 384:512].astype(F32)).astype(BF16)


def kernel(tok, cot, wi, wo, lengths, layer_out, tok_grad, wi_grad, wo_grad, *scratch):
    me = Place()
    z, ylo, k, yhi, x, w = me.z, me.ylo, me.k, me.yhi, me.x, me.w
    r = Refs(scratch[: len(BUFFERS)], scratch[len(BUFFERS) :])
    sends = Sends()
    right, left = me.device(x=(x + 1) % 4), me.device(x=(x + 3) % 4)
    stays = jnp.logical_not(me.moved)

    def row_source(d):
        return (k + 2 - d // 4) % 2, (x + 4 - d % 4) % 4

    load_tok = pltpu.make_async_copy(tok, r.tokr, r.load_r.at[0])
    load_cot = pltpu.make_async_copy(cot, r.cotr, r.load_r.at[1])

    @pl.when(stays)
    def _():
        load_tok.start()
        load_cot.start()

    def prepare():
        wide = wi[...].astype(F32)
        for h in range(HEADS):
            for b in range(4):
                r.wi_f[h, b * 4 : b * 4 + 4, :] = wide[:, b * D + h * HD : b * D + (h + 1) * HD]
        r.wi_send[...] = r.wi_f[...].astype(BF16)
        wide_o = wo[...].astype(F32)
        r.wo_f[...] = jnp.zeros_like(r.wo_f)
        for b in range(8):
            r.wo_f[b // 2 % 2, (b // 4 * 2 + b % 2) * 4 : (b // 4 * 2 + b % 2) * 4 + 4, :] = wide_o[:, b * HD : (b + 1) * HD]
        r.wo_send[...] = r.wo_f[...].astype(BF16)
        r.len_send[...] = jnp.zeros_like(r.len_send)
        r.len_send[0:1, 0:4] = lengths[...]

    greet(me, me.row_peers() + me.zy_peers(), prepare)

    swap_tok = [
        copy(tok.at[part], r.tokr.at[part], r.swap_s.at[n], r.swap_r.at[n], me.partner())
        for n, part in ((n, pl.ds(n * 64, 64)) for n in range(4))
    ]
    swap_cot = copy(cot, r.cotr, r.swap_s.at[4], r.swap_r.at[4], me.partner())

    for d in range(1, 8):
        pk, px = me.row(d // 4, d % 4)
        sends.push(
            r.wi_send.at[2 * px + pk], r.wi_recv.at[w], r.xi_s.at[d - 1], r.xi_r.at[d - 1], me.device(k=pk, x=px)
        )
    r.wi_recv[w] = r.wi_send[me.head]
    for d in range(1, 4):
        pk, px = me.row(0, d)
        sends.push(r.wo_send.at[px % 2], r.wo_recv.at[x], r.xo_s.at[d - 1], r.xo_r.at[d - 1], me.device(x=px))
    r.wo_recv[x] = r.wo_send[x % 2]

    @pl.when(me.moved)
    def _():
        for n in (0, 2, 1, 3):
            swap_tok[n].start()

    sends.push(r.len_send, r.len_recv, r.swap_s.at[5], r.swap_r.at[5], me.sibling())

    def norm_chunk(n):
        part = pl.ds(n * 64, 64)
        r.normed[w, part] = normalize(r.tokr[part].astype(F32))[0].astype(BF16)

    def rows_of(dx, n):
        return r.normed.at[k * 4 + (x + dx) % 4, pl.ds(n * 64, 64)]

    def onward(dx, n, slot, to):
        return copy(rows_of(dx, n), rows_of(dx, n), r.ag_s.at[slot, n], r.ag_r.at[slot, n], to)

    def across(dx, n):
        return copy(rows_of(dx, n), rows_of(dx, n), r.fw_s.at[dx, n], r.ag_r.at[4 + dx, n], me.sibling())

    to_right = [onward(0, n, 3, right) for n in range(4)]
    to_left = [onward(0, n, 1, left) for n in range(4)]
    to_sibling = [across(0, n) for n in range(4)]
    relay = {n: onward(3, n, 2, right) if n < 2 else onward(1, n, 2, left) for n in range(4)}
    relay_sibling = {n: across(3 if n < 2 else 1, n) for n in range(4)}

    def send_chunk(n):
        (to_right if n < 2 else to_left)[n].start()
        to_sibling[n].start()

    def send_rest():
        for n in (2, 3):
            to_right[n].start()
            to_left[n - 2].start()

    def take_first():
        for n in (0, 2, 1, 3):
            slot = 3 if n < 2 else 1
            arrived(rows_of(slot, n), r.ag_s.at[slot, n], r.ag_r.at[slot, n], me)
            relay[n].start()
            relay_sibling[n].start()

    def take(dx, n):
        part = rows_of(dx, n)
        arrived(part, r.ag_s.at[dx, n], r.ag_r.at[dx, n], me)
        sends.push(part, part, r.fw_s.at[dx, n], r.ag_r.at[4 + dx, n], me.sibling())

    @pl.when(stays)
    def _():
        load_tok.wait()
        for n in (0, 2, 1, 3):
            norm_chunk(n)
            send_chunk(n)
        send_rest()

    for d in range(1, 8):
        sk, sx = row_source(d)
        arrived(r.wi_recv.at[sk * 4 + sx], r.xi_s.at[d - 1], r.xi_r.at[d - 1], me)
    for src in range(8):
        piece = r.wi_recv[src].astype(F32)
        for b in range(4):
            r.wi_asm[src // 4, (src % 4) * 4 : (src % 4) * 4 + 4, b * HD : (b + 1) * HD] = piece[b * 4 : b * 4 + 4]
    for c in range(2):
        r.win[z, ylo, c, yhi] = r.wi_asm[c].astype(BF16)
    for d in range(1, 4):
        phi, plo = me.along_y(d)
        part = r.win.at[z, ylo, 1, yhi]
        sends.push(part, part, r.yj_s.at[d - 1], r.yj_r.at[d - 1], me.device(ylo=plo, yhi=phi))
    for d in range(1, NZ):
        part = r.win.at[z, ylo, 0, yhi]
        sends.push(part, part, r.zi_s.at[d - 1], r.zi_r.at[d - 1], me.device(z=me.along_z(d)))

    for d in range(1, 4):
        arrived(r.wo_recv.at[(x + 4 - d) % 4], r.xo_s.at[d - 1], r.xo_r.at[d - 1], me)
    for src in range(4):
        piece = r.wo_recv[src].astype(F32)
        for b in range(4):
            r.wo_asm[b // 2, src * 4 : src * 4 + 4, b % 2 * HD : (b % 2 + 1) * HD] = piece[b * 4 : b * 4 + 4]
    for n in range(2):
        r.wout[x % 2, n, z, ylo, k, yhi] = r.wo_asm[n].astype(BF16)
    for d in range(1, NZ):
        part = r.wout.at[x % 2, :, z, ylo, k, yhi]
        sends.push(part, part, r.zo_s.at[d - 1], r.zo_r.at[d - 1], me.device(z=me.along_z(d)))

    @pl.when(stays)
    def _():
        take_first()

    @pl.when(me.moved)
    def _():
        for n in (0, 2, 1, 3):
            swap_tok[n].wait_recv()
            norm_chunk(n)
            send_chunk(n)
        send_rest()

    for d in range(1, 4):
        shi, slo = me.along_y(4 - d)
        arrived(r.win.at[z, slo, 1, shi], r.yj_s.at[d - 1], r.yj_r.at[d - 1], me)
    for d in range(1, NZ):
        part = r.win.at[z, :, 1, :]
        sends.push(part, part, r.zj_s.at[d - 1], r.zj_r.at[d - 1], me.device(z=me.along_z(d)))

    for d in range(1, NZ):
        arrived(r.win.at[(z + NZ - d) % NZ, ylo, 0, yhi], r.zi_s.at[d - 1], r.zi_r.at[d - 1], me)
    for d in range(1, 4):
        phi, plo = me.along_y(d)
        part = r.win.at[:, ylo, 0, yhi]
        sends.push(part, part, r.yi_s.at[d - 1], r.yi_r.at[d - 1], me.device(ylo=plo, yhi=phi))

    for d in range(1, NZ):
        arrived(r.wout.at[x % 2, :, (z + NZ - d) % NZ, ylo, k, yhi], r.zo_s.at[d - 1], r.zo_r.at[d - 1], me)
    for d in range(1, 4):
        phi, plo = me.along_y(d)
        part = r.wout.at[x % 2, :, :, ylo, k, yhi]
        sends.push(part, part, r.yo_s.at[d - 1], r.yo_r.at[d - 1], me.device(ylo=plo, yhi=phi))

    @pl.when(me.moved)
    def _():
        swap_cot.start()
        take_first()

    for dx, n in ((3, 2), (1, 0), (3, 3), (1, 1), (2, 0), (2, 2), (2, 1), (2, 3)):
        take(dx, n)
    arrived(r.len_recv, r.swap_s.at[5], r.swap_r.at[5], me)
    r.lens[...] = jnp.where(me.moved, r.len_recv[...], r.len_send[...])
    for d in range(1, 4):
        shi, slo = me.along_y(4 - d)
        arrived(r.win.at[:, slo, 0, shi], r.yi_s.at[d - 1], r.yi_r.at[d - 1], me)
    for d in range(1, NZ):
        arrived(r.win.at[(z + NZ - d) % NZ, :, 1, :], r.zj_s.at[d - 1], r.zj_r.at[d - 1], me)

    @pl.loop(0, 4)
    def _(i):
        project(r, k * 4 + i)

    for d in range(1, 4):
        shi, slo = me.along_y(4 - d)
        arrived(r.wout.at[x % 2, :, :, slo, k, shi], r.yo_s.at[d - 1], r.yo_r.at[d - 1], me)
    for n, to in ((0, right), (1, left)):
        part = r.wout.at[x % 2, n, :, :, k]
        sends.push(part, part, r.xq_s.at[n], r.xq_r.at[n], to)
    part = r.wout.at[x % 2, :, :, :, k]
    sends.push(part, part, r.core_s.at[2], r.core_r.at[2], me.sibling())
    for dx in range(4):
        for n in range(4):
            arrived(
                r.normed.at[(1 - k) * 4 + (x + dx) % 4, pl.ds(n * 64, 64)],
                r.fw_s.at[dx, n], r.ag_r.at[4 + dx, n], me,
            )

    @pl.loop(0, 4)
    def _(i):
        project(r, (1 - k) * 4 + i)

    for i in range(4):
        attend(r, i, i)

    for n in range(2):
        part = r.wout.at[(x + 1) % 2, n, :, :, k]
        arrived(part, r.xq_s.at[n], r.xq_r.at[n], me)
        sends.push(part, part, r.core_s.at[n], r.core_r.at[n], me.sibling())

    @pl.loop(4, 6)
    def _(i):
        attend(r, i, 4)

    @pl.when(me.moved)
    def _():
        swap_cot.wait_recv()

    @pl.when(stays)
    def _():
        load_cot.wait()

    arrived(r.wout.at[x % 2, :, :, :, 1 - k], r.core_s.at[2], r.core_r.at[2], me)
    for n in range(2):
        arrived(r.wout.at[(x + 1) % 2, n, :, :, 1 - k], r.core_s.at[n], r.core_r.at[n], me)
    for dx in (2, 1, 3, 0):
        px = (x + dx) % 4
        pair = jnp.zeros((ROWS, 256), F32)
        for q in range(4):
            columns = r.wout[q % 2, q // 2, pl.ds(2 * px, 2)].reshape(256, 256)
            pair = pair + dot(r.cotr[:, q * 256 : (q + 1) * 256], columns, ABT)
        r.dsend[2 * px] = pair[:, :HD].astype(BF16)
        r.dsend[2 * px + 1] = pair[:, HD:].astype(BF16)
        for dk in range(2):
            d = 4 * dk + dx
            if d:
                pk = (k + dk) % 2
                sends.push(
                    r.dsend.at[2 * px + pk], r.dmix.at[w], r.dm_s.at[d - 1], r.dm_r.at[d - 1], me.device(k=pk, x=px)
                )
    r.dmix[w] = r.dsend[me.head]

    @pl.loop(6, 8)
    def _(i):
        attend(r, i, 4)

    for d in range(1, 8):
        sk, sx = row_source(d)
        arrived(r.dmix.at[sk * 4 + sx], r.dm_s.at[d - 1], r.dm_r.at[d - 1], me)

    @pl.loop(0, 4)
    def _(pair):
        row_stats(r, pair, 0)
        row_stats(r, pair, 1)

    for d in range(1, 8):
        pk, px = me.row(d // 4, d % 4)
        sends.push(r.stats, r.every.at[w], r.st_s.at[d - 1], r.st_r.at[d - 1], me.device(k=pk, x=px))
    r.every[w] = r.stats[...]
    r.comb[...] = jnp.zeros_like(r.comb)
    r.dquery[...] = jnp.zeros_like(r.dquery)
    for d in range(1, 8):
        sk, sx = row_source(d)
        arrived(r.every.at[sk * 4 + sx], r.st_s.at[d - 1], r.st_r.at[d - 1], me)

    @pl.loop(0, 4)
    def _(pair):
        gate_rows(r, pair, 0)
        gate_rows(r, pair, 1)

    r.mixed[me.head] = r.msend[w]
    for d in range(1, 8):
        pk, px = me.row(d // 4, d % 4)
        sends.push(
            r.msend.at[pk * 4 + px], r.mixed.at[me.head], r.mx_s.at[d - 1], r.mx_r.at[d - 1], me.device(k=pk, x=px)
        )

    @pl.loop(0, 4)
    def _(j):
        attend_back(r, j, 4)

    for d in range(1, 8):
        sk, sx = row_source(d)
        arrived(r.mixed.at[2 * sx + sk], r.mx_s.at[d - 1], r.mx_r.at[d - 1], me)

    @pl.loop(0, 4)
    def _(n):
        pair = jnp.concatenate([r.mixed[2 * n], r.mixed[2 * n + 1]], axis=1)
        product = dot(pair, r.cotr[...], ATB).astype(BF16)
        for q in range(4):
            r.ps[q % 2, q // 2, pl.ds(2 * n, 2)] = product[:, q * 256 : (q + 1) * 256].reshape(2, 2, 2, 2, 16, 256)

    sends.push(r.ps.at[:, :, :, :, 1 - k], r.pc, r.pc_s.at[0], r.pc_r.at[0], me.sibling())

    joined = jnp.concatenate([r.mixed[h] for h in range(HEADS)], axis=1)
    for n in range(4):
        cols = pl.ds(n * 256, 256)
        product = dot(joined, r.wout[n % 2, n // 2].reshape(D, 256))
        r.lay[:, cols] = (product + r.tokr[:, cols].astype(F32)).astype(BF16)
    swap_lay = copy(r.lay, layer_out, r.sw_s.at[0], r.sw_r.at[0], me.partner())
    swap_grad = [
        copy(r.grad.at[part], tok_grad.at[part], r.sw_s.at[n], r.sw_r.at[n], me.partner())
        for n, part in ((1, pl.ds(0, 128)), (2, pl.ds(128, 128)))
    ]

    @pl.when(stays)
    def _():
        layer_out[...] = r.lay[...]

    @pl.when(me.moved)
    def _():
        swap_lay.start()

    attend_back(r, 4, 3)
    arrived(r.pc, r.pc_s.at[0], r.pc_r.at[0], me)

    @pl.loop(0, NZ)
    def _(n):
        for q in range(4):
            c, m = q % 2, q // 2
            r.pk_sum[c, m, n] = (r.ps[c, m, n, :, k].astype(F32) + r.pc[c, m, n].astype(F32)).astype(BF16)

    for n, to in ((0, right), (1, left)):
        sends.push(r.pk_sum.at[(x + 1) % 2, n], r.pq.at[n], r.pq_s.at[n], r.pq_r.at[n], to)

    for j in range(5, 8):
        attend_back(r, j, 7 - j)

    @pl.loop(0, 8)
    def _(i):
        r.dhidden[i, :, 256:384] = (r.dquery[i] * HALF_FACTOR * r.slope[i, :, 256:384].astype(F32)).astype(BF16)

    def back_product(block, n):
        return dot(r.dhidden[block], r.win[pl.ds(2 * n, 2)].reshape(256, 512), ABT)

    def partial(dx):
        there = (1 - k) * 4 + (x + dx) % 4
        here = k * 4 + (x + dx) % 4

        @pl.loop(0, 4)
        def _(n):
            cols = pl.ds(pl.multiple_of(n * 256, 256), 256)
            r.es_send[dx, :, cols] = back_product(there, n).astype(BF16)

        sends.push(r.es_send.at[dx], r.es_recv.at[dx], r.sib_s.at[dx], r.sib_r.at[dx], me.sibling())

        @pl.loop(0, 4)
        def _(n):
            cols = pl.ds(pl.multiple_of(n * 256, 256), 256)
            r.esum[dx, :, cols] = back_product(here, n)

    def from_sibling(dx):
        arrived(r.es_recv.at[dx], r.sib_s.at[dx], r.sib_r.at[dx], me)

    def to_neighbour(side, half, extra):
        part = pl.ds(half * 128, 128)
        dx = 1 + 2 * side
        total = r.esum[dx, part] + r.es_recv[dx, part].astype(F32)
        if extra is not None:
            total = total + extra.astype(F32)
        r.nb_send[side, part] = total.astype(BF16)
        sends.push(
            r.nb_send.at[side, part], r.nb_recv.at[side, part],
            r.nb_s.at[side, half], r.nb_r.at[side, half], (right, left)[side],
        )

    partial(2)
    partial(1)
    from_sibling(2)
    r.x2_send[...] = (r.esum[2] + r.es_recv[2].astype(F32)).astype(BF16)
    sends.push(r.x2_send.at[pl.ds(0, 128)], r.rl_recv.at[0], r.rl_s.at[0], r.rl_r.at[0], right)
    sends.push(r.x2_send.at[pl.ds(128, 128)], r.rl_recv.at[1], r.rl_s.at[1], r.rl_r.at[1], left)
    for m in range(2):
        arrived(r.pq.at[m], r.pq_s.at[m], r.pq_r.at[m], me)

    @pl.loop(0, NZ)
    def _(n):
        for m in range(2):
            r.pq_sum[m, n] = (r.pk_sum[x % 2, m, n].astype(F32) + r.pq[m, n].astype(F32)).astype(BF16)

    for d in range(1, 4):
        phi, plo = me.along_y(d)
        sends.push(
            r.pq_sum.at[:, :, plo, phi], r.py.at[d - 1], r.py_s.at[d - 1], r.py_r.at[d - 1], me.device(ylo=plo, yhi=phi)
        )

    partial(3)
    from_sibling(1)
    to_neighbour(0, 1, None)
    from_sibling(3)
    to_neighbour(1, 0, None)

    @pl.loop(0, 4)
    def _(n):
        cols = pl.ds(pl.multiple_of(n * 256, 256), 256)
        product = dot(r.normed[:, :, cols].reshape(8 * ROWS, 256), r.dhidden[...].reshape(8 * ROWS, 512), ATB)
        r.gs[pl.ds(2 * n, 2)] = product.astype(BF16).reshape(2, 2, 2, 2, 16, 512)

    for d in range(1, NZ):
        to = me.along_z(d)
        sends.push(r.gs.at[to, :, 1, :], r.hz.at[d - 1], r.hz_s.at[d - 1], r.hz_r.at[d - 1], me.device(z=to))
    for d in range(1, 4):
        phi, plo = me.along_y(d)
        sends.push(
            r.gs.at[:, plo, 0, phi], r.gy.at[d - 1], r.gy_s.at[d - 1], r.gy_r.at[d - 1], me.device(ylo=plo, yhi=phi)
        )

    for side in range(2):
        arrived(r.rl_recv.at[side], r.rl_s.at[side], r.rl_r.at[side], me)
        to_neighbour(side, side, r.rl_recv[side])
    for d in range(1, 4):
        arrived(r.py.at[d - 1], r.py_s.at[d - 1], r.py_r.at[d - 1], me)

    @pl.loop(0, NZ)
    def _(n):
        for m in range(2):
            total = r.pq_sum[m, n, ylo, yhi].astype(F32)
            for d in range(3):
                total = total + r.py[d, m, n].astype(F32)
            r.pz_send[n, m] = total.astype(BF16)

    for d in range(1, NZ):
        to = me.along_z(d)
        sends.push(r.pz_send.at[to], r.pz.at[d - 1], r.pz_s.at[d - 1], r.pz_r.at[d - 1], me.device(z=to))

    partial(0)

    for d in range(1, 4):
        arrived(r.gy.at[d - 1], r.gy_s.at[d - 1], r.gy_r.at[d - 1], me)

    @pl.loop(0, NZ)
    def _(n):
        total = r.gs[n, ylo, 0, yhi].astype(F32)
        for d in range(3):
            total = total + r.gy[d, n].astype(F32)
        r.gz_send[n] = total.astype(BF16)

    for d in range(1, NZ):
        to = me.along_z(d)
        sends.push(r.gz_send.at[to], r.gz.at[d - 1], r.gz_s.at[d - 1], r.gz_r.at[d - 1], me.device(z=to))
    from_sibling(0)

    def finish(half):
        for side in range(2):
            arrived(r.nb_recv.at[side, pl.ds(half * 128, 128)], r.nb_s.at[side, half], r.nb_r.at[side, half], me)
        for n in range(2):
            part = pl.ds(half * 128 + n * 64, 64)
            upstream = (
                r.esum[0, part]
                + r.es_recv[0, part].astype(F32)
                + r.nb_recv[0, part].astype(F32)
                + r.nb_recv[1, part].astype(F32)
            )
            normal, inverse = normalize(r.tokr[part].astype(F32))
            first = jnp.mean(upstream, axis=-1, keepdims=True)
            second = jnp.mean(upstream * normal, axis=-1, keepdims=True)
            r.grad[part] = (inverse * (upstream - first - normal * second) + r.cotr[part].astype(F32)).astype(BF16)

        @pl.when(me.moved)
        def _():
            swap_grad[half].start()

        @pl.when(stays)
        def _():
            part = pl.ds(half * 128, 128)
            tok_grad[part] = r.grad[part]

    finish(0)
    finish(1)

    for d in range(1, NZ):
        arrived(r.hz.at[d - 1], r.hz_s.at[d - 1], r.hz_r.at[d - 1], me)
    for n in range(2):
        total = r.gs[z, n, 1].astype(F32)
        for d in range(7):
            total = total + r.hz[d, n].astype(F32)
        r.hy_send[n] = total.astype(BF16)
    for d in range(1, 4):
        phi, plo = me.along_y(d)
        sends.push(
            r.hy_send.at[plo, phi], r.hy.at[d - 1], r.hy_s.at[d - 1], r.hy_r.at[d - 1], me.device(ylo=plo, yhi=phi)
        )

    for d in range(1, NZ):
        arrived(r.pz.at[d - 1], r.pz_s.at[d - 1], r.pz_r.at[d - 1], me)
    total = r.pz_send[z].astype(F32)
    for d in range(1, NZ):
        total = total + r.pz[d - 1].astype(F32)
    for px in range(4):
        for b in range(4):
            r.px_f[px, b * 4 : b * 4 + 4, :] = total[b // 2, px * 4 : px * 4 + 4, b % 2 * HD : (b % 2 + 1) * HD]
    r.px_recv[x] = r.px_f[x]
    for d in range(1, 4):
        pk, px = me.row(0, d)
        sends.push(r.px_f.at[px], r.px_recv.at[x], r.px_s.at[d - 1], r.px_r.at[d - 1], me.device(x=px))

    for d in range(1, NZ):
        arrived(r.gz.at[d - 1], r.gz_s.at[d - 1], r.gz_r.at[d - 1], me)
    for d in range(1, 4):
        arrived(r.hy.at[d - 1], r.hy_s.at[d - 1], r.hy_r.at[d - 1], me)
    total = r.gz_send[z].astype(F32)
    for d in range(7):
        total = total + r.gz[d].astype(F32)
    other = r.hy_send[ylo, yhi].astype(F32)
    for d in range(3):
        other = other + r.hy[d].astype(F32)
    for c in range(2):
        for px in range(4):
            for b in range(4):
                r.gx_f[c * 4 + px, b * 4 : b * 4 + 4, :] = (total, other)[c][
                    px * 4 : px * 4 + 4, b * HD : (b + 1) * HD
                ]
    r.gx_recv[w] = r.gx_f[w]
    for d in range(1, 8):
        pk, px = me.row(d // 4, d % 4)
        sends.push(
            r.gx_f.at[pk * 4 + px], r.gx_recv.at[w], r.gx_s.at[d - 1], r.gx_r.at[d - 1], me.device(k=pk, x=px)
        )

    for d in range(1, 4):
        arrived(r.px_recv.at[(x + 4 - d) % 4], r.px_s.at[d - 1], r.px_r.at[d - 1], me)
    for c in range(2):
        total = r.px_recv[c] + r.px_recv[c + 2]
        for n in range(4):
            b = n // 2 * 4 + c * 2 + n % 2
            wo_grad[:, b * HD : (b + 1) * HD] = total[n * 4 : n * 4 + 4]
    for d in range(1, 8):
        sk, sx = row_source(d)
        arrived(r.gx_recv.at[sk * 4 + sx], r.gx_s.at[d - 1], r.gx_r.at[d - 1], me)
    for src in range(8):
        h = 2 * (src % 4) + src // 4
        for b in range(4):
            wi_grad[:, b * D + h * HD : b * D + (h + 1) * HD] = r.gx_recv[src, b * 4 : b * 4 + 4, :]
    sends.drain()
    for one in to_right + to_left + to_sibling + list(relay.values()) + list(relay_sibling.values()):
        one.wait_send()

    @pl.when(me.moved)
    def _():
        for one in swap_tok:
            one.wait_send()
        swap_cot.wait_send()
        swap_lay.wait()
        for one in swap_grad:
            one.wait()


def local(tokens, lengths, in_weight, out_weight, cotangent):
    anywhere = pl.BlockSpec(memory_space=pl.ANY)
    shapes = [((ROWS, D), BF16), ((ROWS, D), BF16), ((4, 4 * D), F32), ((4, D), F32)]
    scratch = [pltpu.VMEM(shape, kind) for shape, kind in BUFFERS.values()]
    for shape in SEMAPHORES.values():
        scratch += [DMA(shape), DMA(shape)]
    return tuple(
        pl.pallas_call(
            kernel,
            out_shape=[jax.ShapeDtypeStruct(s, t) for s, t in shapes],
            in_specs=[anywhere, anywhere, VMEM, VMEM, VMEM],
            out_specs=[VMEM] * 4,
            scratch_shapes=scratch,
            compiler_params=pltpu.CompilerParams(
                collective_id=0, has_side_effects=True, vmem_limit_bytes=60 << 20
            ),
            name="layer",
        )(tokens, cotangent, in_weight, out_weight, lengths)
    )


def solution(mesh):
    both = P(("dp", "seq"), None)
    return jax.shard_map(
        local,
        mesh=mesh,
        in_specs=(both, P("dp", None), both, both, both),
        out_specs=(both, both, both, both),
        check_vma=False,
    )
```

```python
import functools

import jax
import jax.numpy as jnp
from jax import lax
from jax.experimental import pallas as pl
from jax.experimental.pallas import tpu as pltpu
from jax.sharding import PartitionSpec as P

F32 = jnp.float32
BF16 = jnp.bfloat16
MESH = pl.DeviceIdType.MESH
DMA = pltpu.SemaphoreType.DMA

D = 1024
HEADS = 8
HD = 128
ROWS = 256
NZ = 8
epsilon = 1e-05
HALF_FACTOR = 0.5 * HD ** (-0.5)
VMEM = pl.BlockSpec(memory_space=pltpu.VMEM)
ABT = (((1,), (1,)), ((), ()))
ATB = (((0,), (0,)), ((), ()))


def dot(a, b, dims=(((1,), (0,)), ((), ()))):
    return lax.dot_general(a, b, dims, preferred_element_type=F32)


class Place:
    def __init__(self):
        g = lax.axis_index("dp")
        s = lax.axis_index("seq")
        self.z, self.ylo, self.k = g // 4, (g // 2) % 2, g % 2
        self.yhi, self.x = s // 4, s % 4
        self.w = self.k * 4 + self.x
        self.head = 2 * self.x + self.k
        self.moved = self.k != self.yhi

    def device(self, z=None, ylo=None, k=None, yhi=None, x=None):
        z = self.z if z is None else z
        ylo = self.ylo if ylo is None else ylo
        k = self.k if k is None else k
        yhi = self.yhi if yhi is None else yhi
        x = self.x if x is None else x
        return (z * 4 + ylo * 2 + k, yhi * 4 + x)

    def row(self, dk, dx):
        return (self.k + dk) % 2, (self.x + dx) % 4

    def along_z(self, d):
        return (self.z + d) % NZ

    def along_y(self, d):
        y = (self.yhi * 2 + self.ylo + d) % 4
        return y // 2, y % 2

    def partner(self):
        return self.device(k=self.yhi, yhi=self.k)

    def sibling(self):
        return self.device(k=1 - self.k)

    def row_peers(self):
        peers = []
        for d in range(1, 8):
            k, x = self.row(d // 4, d % 4)
            peers.append(self.device(k=k, x=x))
        return peers

    def zy_peers(self):
        peers = [self.device(z=self.along_z(d)) for d in range(1, NZ)]
        for d in range(1, 4):
            yhi, ylo = self.along_y(d)
            peers.append(self.device(ylo=ylo, yhi=yhi))
        return peers


def greet(me, peers, meanwhile):
    barrier = pltpu.get_barrier_semaphore()
    for peer in peers:
        pl.semaphore_signal(barrier, inc=1, device_id=peer, device_id_type=MESH)

    @pl.when(me.moved)
    def _():
        pl.semaphore_signal(barrier, inc=1, device_id=me.partner(), device_id_type=MESH)

    meanwhile()
    pl.semaphore_wait(barrier, len(peers) + me.moved.astype(jnp.int32))


def copy(src, dst, send, recv, to):
    return pltpu.make_async_remote_copy(
        src_ref=src, dst_ref=dst, send_sem=send, recv_sem=recv, device_id=to, device_id_type=MESH
    )


class Sends:
    def __init__(self):
        self.started = []

    def push(self, src, dst, send, recv, to):
        one = copy(src, dst, send, recv, to)
        one.start()
        self.started.append(one)

    def drain(self):
        for one in self.started:
            one.wait_send()


def arrived(ref, send, recv, me):
    copy(ref, ref, send, recv, me.sibling()).wait_recv()


def normalize(values):
    centre = values - jnp.mean(values, axis=-1, keepdims=True)
    inverse = lax.rsqrt(jnp.mean(centre * centre, axis=-1, keepdims=True) + epsilon)
    return centre * inverse, inverse


def first_of(position, lens):
    e0 = lens[0:1, 0:1]
    e1 = e0 + lens[0:1, 1:2]
    e2 = e1 + lens[0:1, 2:3]
    zero = jnp.zeros_like(position)
    start = jnp.where(position >= e0, e0, zero)
    start = jnp.where(position >= e1, e1, start)
    return jnp.where(position >= e2, e2, start)


BUFFERS = {
    "tokr": ((ROWS, D), BF16), "cotr": ((ROWS, D), BF16),
    "len_send": ((8, 128), jnp.int32), "len_recv": ((8, 128), jnp.int32), "lens": ((8, 128), jnp.int32),
    "wi_f": ((8, 16, 128), F32), "wi_send": ((8, 16, 128), BF16), "wi_recv": ((8, 16, 128), BF16),
    "wi_asm": ((2, 16, 512), F32),
    "wo_f": ((2, 16, 128), F32), "wo_send": ((2, 16, 128), BF16), "wo_recv": ((4, 16, 128), BF16),
    "wo_asm": ((2, 16, 256), F32),
    "win": ((NZ, 2, 2, 2, 16, 512), BF16), "wout": ((2, 2, NZ, 2, 2, 2, 16, 256), BF16),
    "normed": ((8, ROWS, D), BF16), "gated": ((8, ROWS, 512), BF16), "slope": ((8, ROWS, 512), BF16),
    "dsend": ((8, ROWS, HD), BF16), "dmix": ((8, ROWS, HD), BF16),
    "attn": ((8, ROWS, HD), BF16), "centre": ((8, ROWS, HD), F32), "dpart": ((4, ROWS, 256), F32),
    "stats_a": ((2, 8, ROWS), F32), "every_a": ((8, 2, 8, ROWS), F32),
    "stats_b": ((2, 8, ROWS), F32), "every_b": ((8, 2, 8, ROWS), F32),
    "comb": ((128, ROWS), F32), "msend": ((8, ROWS, HD), BF16), "mixed": ((8, ROWS, HD), BF16),
    "dattn": ((8, ROWS, HD), BF16), "dhidden": ((8, ROWS, 512), BF16), "dquery": ((8, ROWS, HD), F32),
    "lay": ((ROWS, D), BF16), "grad": ((ROWS, D), BF16),
    "esum": ((4, ROWS, D), F32), "es_send": ((4, ROWS, D), BF16), "es_recv": ((4, ROWS, D), BF16),
    "x2_send": ((ROWS, D), BF16), "rl_recv": ((2, 128, D), BF16),
    "nb_send": ((2, ROWS, D), BF16), "nb_recv": ((2, ROWS, D), BF16),
    "gs": ((NZ, 2, 2, 2, 16, 512), BF16),
    "gy": ((3, NZ, 16, 512), BF16), "gz_send": ((NZ, 16, 512), BF16), "gz": ((7, 16, 512), BF16),
    "hz": ((7, 2, 2, 16, 512), BF16), "hy_send": ((2, 2, 16, 512), BF16), "hy": ((3, 16, 512), BF16),
    "gx_f": ((8, 16, 128), F32), "gx_recv": ((8, 16, 128), F32),
    "ps": ((2, 2, NZ, 2, 2, 2, 16, 256), BF16), "pc": ((2, 2, NZ, 2, 2, 16, 256), BF16),
    "pk_sum": ((2, 2, NZ, 2, 2, 16, 256), BF16), "pq": ((2, NZ, 2, 2, 16, 256), BF16),
    "pq_sum": ((2, NZ, 2, 2, 16, 256), BF16),
    "py": ((3, 2, NZ, 16, 256), BF16), "pz_send": ((NZ, 2, 16, 256), BF16), "pz": ((7, 2, 16, 256), BF16),
    "px_f": ((4, 16, 128), F32), "px_recv": ((4, 16, 128), F32),
}
SEMAPHORES = {
    "load": (2,), "swap": (6,), "xi": (7,), "xo": (3,), "zi": (7,), "zo": (7,), "yi": (3,), "yo": (3,), "xq": (2,), "core": (3,),
    "zj": (7,), "yj": (3,),
    "ag": (8, 4), "fw": (4, 4), "dm": (7,), "sa": (7,), "sb": (7,), "mx": (7,), "sib": (4,), "rl": (2,), "nb": (2, 2),
    "gy": (3,), "gz": (7,), "hy": (3,), "hz": (7,), "gx": (7,),
    "pc": (1,), "pq": (2,), "py": (3,), "pz": (7,), "px": (3,), "sw": (3,),
}


class Refs:
    def __init__(self, buffers, semaphores):
        for name, ref in zip(BUFFERS, buffers):
            setattr(self, name, ref)
        for n, name in enumerate(SEMAPHORES):
            setattr(self, name + "_s", semaphores[2 * n])
            setattr(self, name + "_r", semaphores[2 * n + 1])


def project(r, block):
    left = r.normed[block]
    for n in range(2):
        cols = pl.ds(n * 256, 256)
        hidden = dot(left, r.win[:, :, :, :, :, cols].reshape(D, 256))
        sigma = 0.5 + 0.5 * jnp.tanh(0.5 * hidden)
        value = hidden * sigma
        r.gated[block, :, cols] = value.astype(BF16)
        r.slope[block, :, cols] = (sigma + value * (1.0 - sigma)).astype(BF16)


def attend(r, i, reach):
    query = r.gated[i, :, 256:384]
    pos = i * ROWS + lax.broadcasted_iota(jnp.int32, (ROWS, 1), 0)
    start = first_of(pos, r.lens)
    total = jnp.zeros((ROWS, HD), F32)
    for off in range(reach + 1):
        j = i - off
        half = dot(query, r.gated[j, :, 384:512], ABT) * HALF_FACTOR
        weights = half + half * jnp.tanh(half)
        other = j * ROWS + lax.broadcasted_iota(jnp.int32, (ROWS, ROWS), 1)
        allowed = other >= start
        if off == 0:
            allowed = allowed & (other <= pos)
        weights = jnp.where(allowed, weights, 0.0).astype(BF16)
        total = total + dot(weights, r.gated[j, :, 128:256])
    r.attn[i] = total.astype(BF16)


def two_columns(first, second):
    lane = lax.broadcasted_iota(jnp.int32, (ROWS, HD), 1)
    return jnp.where(lane == 0, first, jnp.where(lane == 1, second, 0.0)).T[0:2]


def attn_stats(r, quad, n):
    i = 4 * quad + n
    value = r.attn[i].astype(F32)
    mean = jnp.mean(value, axis=-1, keepdims=True)
    centre = value - mean
    r.centre[i] = centre
    r.stats_a[quad, 2 * n : 2 * n + 2] = two_columns(mean, jnp.sum(centre * centre, axis=-1, keepdims=True))


def upstream_stats(r, quad, n):
    i = 4 * quad + n
    upstream = r.dmix[i].astype(F32) * r.gated[i, :, 0:128].astype(F32)
    r.stats_b[quad, 2 * n : 2 * n + 2] = two_columns(
        jnp.sum(upstream, axis=-1, keepdims=True), jnp.sum(upstream * r.centre[i], axis=-1, keepdims=True)
    )


def gate_rows(r, quad, n):
    i = 4 * quad + n
    mean, second = (r.every_a[:, quad, 2 * n + m, :] for m in range(2))
    total, cross = (r.every_b[:, quad, 2 * n + m, :] for m in range(2))
    middle = jnp.mean(mean, axis=0, keepdims=True)
    apart = mean - middle
    variance = jnp.sum(second + HD * apart * apart, axis=0, keepdims=True) / D
    inverse = lax.rsqrt(variance + epsilon)
    first = jnp.sum(total, axis=0, keepdims=True) / D
    other = inverse * jnp.sum(cross + apart * total, axis=0, keepdims=True) / D
    r.comb[0:1, :] = middle
    r.comb[1:2, :] = inverse
    r.comb[2:3, :] = first
    r.comb[3:4, :] = other
    turned = r.comb[...].T
    middle, inverse, first, other = (turned[:, n : n + 1] for n in range(4))
    upper = r.gated[i, :, 0:128].astype(F32)
    through = r.dmix[i].astype(F32)
    normal = (r.attn[i].astype(F32) - middle) * inverse
    r.msend[i] = (normal * upper).astype(BF16)
    upstream = through * upper
    r.dattn[i] = (inverse * (upstream - first - normal * other)).astype(BF16)
    r.dhidden[i, :, 0:128] = (through * normal * r.slope[i, :, 0:128].astype(F32)).astype(BF16)


def attend_back(r, j, reach):
    key = r.gated[j, :, 384:512]
    value = r.gated[j, :, 128:256]
    other = j * ROWS + lax.broadcasted_iota(jnp.int32, (ROWS, ROWS), 0)
    dkey = jnp.zeros((ROWS, HD), F32)
    dvalue = jnp.zeros((ROWS, HD), F32)
    for off in range(reach + 1):
        i = j + off
        query = r.gated[i, :, 256:384]
        grad = r.dattn[i]
        half = dot(key, query, ABT) * HALF_FACTOR
        pos = i * ROWS + lax.broadcasted_iota(jnp.int32, (1, ROWS), 1)
        allowed = other >= first_of(pos, r.lens)
        if off == 0:
            allowed = allowed & (other <= pos)
        double = jnp.where(allowed, 1.0 + jnp.tanh(half), 0.0)
        weights = half * double
        bend = double + weights * (2.0 - double)
        dscores = (dot(value, grad, ABT) * bend).astype(BF16)
        dvalue = dvalue + dot(weights.astype(BF16), grad)
        dkey = dkey + dot(dscores, query)
        r.dquery[i] += dot(dscores, key, ATB)
    r.dhidden[j, :, 128:256] = (dvalue * r.slope[j, :, 128:256].astype(F32)).astype(BF16)
    r.dhidden[j, :, 384:512] = (dkey * HALF_FACTOR * r.slope[j, :, 384:512].astype(F32)).astype(BF16)


def kernel(tok, cot, wi, wo, lengths, layer_out, tok_grad, wi_grad, wo_grad, *scratch):
    me = Place()
    z, ylo, k, yhi, x, w = me.z, me.ylo, me.k, me.yhi, me.x, me.w
    r = Refs(scratch[: len(BUFFERS)], scratch[len(BUFFERS) :])
    sends = Sends()
    right, left = me.device(x=(x + 1) % 4), me.device(x=(x + 3) % 4)
    stays = jnp.logical_not(me.moved)

    def row_source(d):
        return (k + 2 - d // 4) % 2, (x + 4 - d % 4) % 4

    load_tok = pltpu.make_async_copy(tok, r.tokr, r.load_r.at[0])
    load_cot = pltpu.make_async_copy(cot, r.cotr, r.load_r.at[1])

    @pl.when(stays)
    def _():
        load_tok.start()
        load_cot.start()

    def prepare():
        wide = wi[...].astype(F32)
        for h in range(HEADS):
            for b in range(4):
                r.wi_f[h, b * 4 : b * 4 + 4, :] = wide[:, b * D + h * HD : b * D + (h + 1) * HD]
        r.wi_send[...] = r.wi_f[...].astype(BF16)
        wide_o = wo[...].astype(F32)
        r.wo_f[...] = jnp.zeros_like(r.wo_f)
        for b in range(8):
            r.wo_f[b // 2 % 2, (b // 4 * 2 + b % 2) * 4 : (b // 4 * 2 + b % 2) * 4 + 4, :] = wide_o[:, b * HD : (b + 1) * HD]
        r.wo_send[...] = r.wo_f[...].astype(BF16)
        r.len_send[...] = jnp.zeros_like(r.len_send)
        r.len_send[0:1, 0:4] = lengths[...]

    greet(me, me.row_peers() + me.zy_peers(), prepare)

    swap_tok = [
        copy(tok.at[part], r.tokr.at[part], r.swap_s.at[n], r.swap_r.at[n], me.partner())
        for n, part in ((n, pl.ds(n * 64, 64)) for n in range(4))
    ]
    swap_cot = copy(cot, r.cotr, r.swap_s.at[4], r.swap_r.at[4], me.partner())

    for d in range(1, 8):
        pk, px = me.row(d // 4, d % 4)
        sends.push(
            r.wi_send.at[2 * px + pk], r.wi_recv.at[w], r.xi_s.at[d - 1], r.xi_r.at[d - 1], me.device(k=pk, x=px)
        )
    r.wi_recv[w] = r.wi_send[me.head]
    for d in range(1, 4):
        pk, px = me.row(0, d)
        sends.push(r.wo_send.at[px % 2], r.wo_recv.at[x], r.xo_s.at[d - 1], r.xo_r.at[d - 1], me.device(x=px))
    r.wo_recv[x] = r.wo_send[x % 2]

    @pl.when(me.moved)
    def _():
        for n in (0, 2, 1, 3):
            swap_tok[n].start()

    sends.push(r.len_send, r.len_recv, r.swap_s.at[5], r.swap_r.at[5], me.sibling())

    def norm_chunk(n):
        part = pl.ds(n * 64, 64)
        r.normed[w, part] = normalize(r.tokr[part].astype(F32))[0].astype(BF16)

    def rows_of(dx, n):
        return r.normed.at[k * 4 + (x + dx) % 4, pl.ds(n * 64, 64)]

    def onward(dx, n, slot, to):
        return copy(rows_of(dx, n), rows_of(dx, n), r.ag_s.at[slot, n], r.ag_r.at[slot, n], to)

    def across(dx, n):
        return copy(rows_of(dx, n), rows_of(dx, n), r.fw_s.at[dx, n], r.ag_r.at[4 + dx, n], me.sibling())

    to_right = [onward(0, n, 3, right) for n in range(4)]
    to_left = [onward(0, n, 1, left) for n in range(4)]
    to_sibling = [across(0, n) for n in range(4)]
    relay = {n: onward(3, n, 2, right) if n < 2 else onward(1, n, 2, left) for n in range(4)}
    relay_sibling = {n: across(3 if n < 2 else 1, n) for n in range(4)}

    def send_chunk(n):
        (to_right if n < 2 else to_left)[n].start()
        to_sibling[n].start()

    def send_rest():
        for n in (2, 3):
            to_right[n].start()
            to_left[n - 2].start()

    def take_first():
        for n in (0, 2, 1, 3):
            slot = 3 if n < 2 else 1
            arrived(rows_of(slot, n), r.ag_s.at[slot, n], r.ag_r.at[slot, n], me)
            relay[n].start()
            relay_sibling[n].start()

    def take(dx, n):
        part = rows_of(dx, n)
        arrived(part, r.ag_s.at[dx, n], r.ag_r.at[dx, n], me)
        sends.push(part, part, r.fw_s.at[dx, n], r.ag_r.at[4 + dx, n], me.sibling())

    @pl.when(stays)
    def _():
        load_tok.wait()
        for n in (0, 2, 1, 3):
            norm_chunk(n)
            send_chunk(n)
        send_rest()

    for d in range(1, 8):
        sk, sx = row_source(d)
        arrived(r.wi_recv.at[sk * 4 + sx], r.xi_s.at[d - 1], r.xi_r.at[d - 1], me)
    for src in range(8):
        piece = r.wi_recv[src].astype(F32)
        for b in range(4):
            r.wi_asm[src // 4, (src % 4) * 4 : (src % 4) * 4 + 4, b * HD : (b + 1) * HD] = piece[b * 4 : b * 4 + 4]
    for c in range(2):
        r.win[z, ylo, c, yhi] = r.wi_asm[c].astype(BF16)
    for d in range(1, 4):
        phi, plo = me.along_y(d)
        part = r.win.at[z, ylo, 1, yhi]
        sends.push(part, part, r.yj_s.at[d - 1], r.yj_r.at[d - 1], me.device(ylo=plo, yhi=phi))
    for d in range(1, NZ):
        part = r.win.at[z, ylo, 0, yhi]
        sends.push(part, part, r.zi_s.at[d - 1], r.zi_r.at[d - 1], me.device(z=me.along_z(d)))

    for d in range(1, 4):
        arrived(r.wo_recv.at[(x + 4 - d) % 4], r.xo_s.at[d - 1], r.xo_r.at[d - 1], me)
    for src in range(4):
        piece = r.wo_recv[src].astype(F32)
        for b in range(4):
            r.wo_asm[b // 2, src * 4 : src * 4 + 4, b % 2 * HD : (b % 2 + 1) * HD] = piece[b * 4 : b * 4 + 4]
    for n in range(2):
        r.wout[x % 2, n, z, ylo, k, yhi] = r.wo_asm[n].astype(BF16)
    for d in range(1, NZ):
        part = r.wout.at[x % 2, :, z, ylo, k, yhi]
        sends.push(part, part, r.zo_s.at[d - 1], r.zo_r.at[d - 1], me.device(z=me.along_z(d)))

    @pl.when(stays)
    def _():
        take_first()

    @pl.when(me.moved)
    def _():
        for n in (0, 2, 1, 3):
            swap_tok[n].wait_recv()
            norm_chunk(n)
            send_chunk(n)
        send_rest()

    for d in range(1, 4):
        shi, slo = me.along_y(4 - d)
        arrived(r.win.at[z, slo, 1, shi], r.yj_s.at[d - 1], r.yj_r.at[d - 1], me)
    for d in range(1, NZ):
        part = r.win.at[z, :, 1, :]
        sends.push(part, part, r.zj_s.at[d - 1], r.zj_r.at[d - 1], me.device(z=me.along_z(d)))

    for d in range(1, NZ):
        arrived(r.win.at[(z + NZ - d) % NZ, ylo, 0, yhi], r.zi_s.at[d - 1], r.zi_r.at[d - 1], me)
    for d in range(1, 4):
        phi, plo = me.along_y(d)
        part = r.win.at[:, ylo, 0, yhi]
        sends.push(part, part, r.yi_s.at[d - 1], r.yi_r.at[d - 1], me.device(ylo=plo, yhi=phi))

    for d in range(1, NZ):
        arrived(r.wout.at[x % 2, :, (z + NZ - d) % NZ, ylo, k, yhi], r.zo_s.at[d - 1], r.zo_r.at[d - 1], me)
    for d in range(1, 4):
        phi, plo = me.along_y(d)
        part = r.wout.at[x % 2, :, :, ylo, k, yhi]
        sends.push(part, part, r.yo_s.at[d - 1], r.yo_r.at[d - 1], me.device(ylo=plo, yhi=phi))

    @pl.when(me.moved)
    def _():
        swap_cot.start()
        take_first()

    for dx, n in ((3, 2), (1, 0), (3, 3), (1, 1), (2, 0), (2, 2), (2, 1), (2, 3)):
        take(dx, n)
    arrived(r.len_recv, r.swap_s.at[5], r.swap_r.at[5], me)
    r.lens[...] = jnp.where(me.moved, r.len_recv[...], r.len_send[...])
    for d in range(1, 4):
        shi, slo = me.along_y(4 - d)
        arrived(r.win.at[:, slo, 0, shi], r.yi_s.at[d - 1], r.yi_r.at[d - 1], me)
    for d in range(1, NZ):
        arrived(r.win.at[(z + NZ - d) % NZ, :, 1, :], r.zj_s.at[d - 1], r.zj_r.at[d - 1], me)

    @pl.loop(0, 4)
    def _(i):
        project(r, k * 4 + i)

    for d in range(1, 4):
        shi, slo = me.along_y(4 - d)
        arrived(r.wout.at[x % 2, :, :, slo, k, shi], r.yo_s.at[d - 1], r.yo_r.at[d - 1], me)
    for n, to in ((0, right), (1, left)):
        part = r.wout.at[x % 2, n, :, :, k]
        sends.push(part, part, r.xq_s.at[n], r.xq_r.at[n], to)
    part = r.wout.at[x % 2, :, :, :, k]
    sends.push(part, part, r.core_s.at[2], r.core_r.at[2], me.sibling())
    for dx in range(4):
        for n in range(4):
            arrived(
                r.normed.at[(1 - k) * 4 + (x + dx) % 4, pl.ds(n * 64, 64)],
                r.fw_s.at[dx, n], r.ag_r.at[4 + dx, n], me,
            )

    @pl.loop(0, 4)
    def _(i):
        project(r, (1 - k) * 4 + i)

    for i in range(4):
        attend(r, i, i)

    @pl.when(me.moved)
    def _():
        swap_cot.wait_recv()

    @pl.when(stays)
    def _():
        load_cot.wait()

    arrived(r.wout.at[x % 2, :, :, :, 1 - k], r.core_s.at[2], r.core_r.at[2], me)
    def through(px, side):
        pair = jnp.zeros((ROWS, 256), F32)
        for m in range(2):
            cols = pl.ds(pl.multiple_of((side + 2 * m) * 256, 256), 256)
            pair = pair + dot(r.cotr[:, cols], r.wout[side, m, pl.ds(2 * px, 2)].reshape(256, 256), ABT)
        return pair

    for dx in range(4):
        r.dpart[dx] = through((x + dx) % 4, x % 2)

    for n in range(2):
        part = r.wout.at[(x + 1) % 2, n, :, :, k]
        arrived(part, r.xq_s.at[n], r.xq_r.at[n], me)
        sends.push(part, part, r.core_s.at[n], r.core_r.at[n], me.sibling())

    @pl.loop(4, 6)
    def _(i):
        attend(r, i, 4)

    for n in range(2):
        arrived(r.wout.at[(x + 1) % 2, n, :, :, 1 - k], r.core_s.at[n], r.core_r.at[n], me)
    for dx in (2, 1, 3, 0):
        px = (x + dx) % 4
        pair = r.dpart[dx] + through(px, (x + 1) % 2)
        r.dsend[2 * px] = pair[:, :HD].astype(BF16)
        r.dsend[2 * px + 1] = pair[:, HD:].astype(BF16)
        for dk in range(2):
            d = 4 * dk + dx
            if d:
                pk = (k + dk) % 2
                sends.push(
                    r.dsend.at[2 * px + pk], r.dmix.at[w], r.dm_s.at[d - 1], r.dm_r.at[d - 1], me.device(k=pk, x=px)
                )
    r.dmix[w] = r.dsend[me.head]

    @pl.loop(6, 8)
    def _(i):
        attend(r, i, 4)

    @pl.loop(0, 2)
    def _(quad):
        for n in range(4):
            attn_stats(r, quad, n)

    for d in range(1, 8):
        pk, px = me.row(d // 4, d % 4)
        sends.push(r.stats_a, r.every_a.at[w], r.sa_s.at[d - 1], r.sa_r.at[d - 1], me.device(k=pk, x=px))
    r.every_a[w] = r.stats_a[...]
    r.comb[...] = jnp.zeros_like(r.comb)
    r.dquery[...] = jnp.zeros_like(r.dquery)
    for d in range(1, 8):
        sk, sx = row_source(d)
        arrived(r.dmix.at[sk * 4 + sx], r.dm_s.at[d - 1], r.dm_r.at[d - 1], me)

    @pl.loop(0, 2)
    def _(quad):
        for n in range(4):
            upstream_stats(r, quad, n)

    for d in range(1, 8):
        pk, px = me.row(d // 4, d % 4)
        sends.push(r.stats_b, r.every_b.at[w], r.sb_s.at[d - 1], r.sb_r.at[d - 1], me.device(k=pk, x=px))
    r.every_b[w] = r.stats_b[...]
    for d in range(1, 8):
        sk, sx = row_source(d)
        arrived(r.every_a.at[sk * 4 + sx], r.sa_s.at[d - 1], r.sa_r.at[d - 1], me)
    for d in range(1, 8):
        sk, sx = row_source(d)
        arrived(r.every_b.at[sk * 4 + sx], r.sb_s.at[d - 1], r.sb_r.at[d - 1], me)

    @pl.loop(0, 2)
    def _(quad):
        for n in range(4):
            gate_rows(r, quad, n)

    r.mixed[me.head] = r.msend[w]
    for d in range(1, 8):
        pk, px = me.row(d // 4, d % 4)
        sends.push(
            r.msend.at[pk * 4 + px], r.mixed.at[me.head], r.mx_s.at[d - 1], r.mx_r.at[d - 1], me.device(k=pk, x=px)
        )

    @pl.loop(0, 4)
    def _(j):
        attend_back(r, j, 4)

    for d in range(1, 8):
        sk, sx = row_source(d)
        arrived(r.mixed.at[2 * sx + sk], r.mx_s.at[d - 1], r.mx_r.at[d - 1], me)

    @pl.loop(0, 4)
    def _(n):
        pair = jnp.concatenate([r.mixed[2 * n], r.mixed[2 * n + 1]], axis=1)
        product = dot(pair, r.cotr[...], ATB).astype(BF16)
        for q in range(4):
            r.ps[q % 2, q // 2, pl.ds(2 * n, 2)] = product[:, q * 256 : (q + 1) * 256].reshape(2, 2, 2, 2, 16, 256)

    sends.push(r.ps.at[:, :, :, :, 1 - k], r.pc, r.pc_s.at[0], r.pc_r.at[0], me.sibling())

    joined = jnp.concatenate([r.mixed[h] for h in range(HEADS)], axis=1)
    for n in range(4):
        cols = pl.ds(n * 256, 256)
        product = dot(joined, r.wout[n % 2, n // 2].reshape(D, 256))
        r.lay[:, cols] = (product + r.tokr[:, cols].astype(F32)).astype(BF16)
    swap_lay = copy(r.lay, layer_out, r.sw_s.at[0], r.sw_r.at[0], me.partner())
    swap_grad = [
        copy(r.grad.at[part], tok_grad.at[part], r.sw_s.at[n], r.sw_r.at[n], me.partner())
        for n, part in ((1, pl.ds(0, 128)), (2, pl.ds(128, 128)))
    ]

    @pl.when(stays)
    def _():
        layer_out[...] = r.lay[...]

    @pl.when(me.moved)
    def _():
        swap_lay.start()

    attend_back(r, 4, 3)
    arrived(r.pc, r.pc_s.at[0], r.pc_r.at[0], me)

    @pl.loop(0, NZ)
    def _(n):
        for q in range(4):
            c, m = q % 2, q // 2
            r.pk_sum[c, m, n] = (r.ps[c, m, n, :, k].astype(F32) + r.pc[c, m, n].astype(F32)).astype(BF16)

    for n, to in ((0, right), (1, left)):
        sends.push(r.pk_sum.at[(x + 1) % 2, n], r.pq.at[n], r.pq_s.at[n], r.pq_r.at[n], to)

    for j in range(5, 8):
        attend_back(r, j, 7 - j)

    @pl.loop(0, 8)
    def _(i):
        r.dhidden[i, :, 256:384] = (r.dquery[i] * HALF_FACTOR * r.slope[i, :, 256:384].astype(F32)).astype(BF16)

    def back_product(block, n):
        return dot(r.dhidden[block], r.win[pl.ds(2 * n, 2)].reshape(256, 512), ABT)

    def partial(dx):
        there = (1 - k) * 4 + (x + dx) % 4
        here = k * 4 + (x + dx) % 4

        @pl.loop(0, 4)
        def _(n):
            cols = pl.ds(pl.multiple_of(n * 256, 256), 256)
            r.es_send[dx, :, cols] = back_product(there, n).astype(BF16)

        sends.push(r.es_send.at[dx], r.es_recv.at[dx], r.sib_s.at[dx], r.sib_r.at[dx], me.sibling())

        @pl.loop(0, 4)
        def _(n):
            cols = pl.ds(pl.multiple_of(n * 256, 256), 256)
            r.esum[dx, :, cols] = back_product(here, n)

    def from_sibling(dx):
        arrived(r.es_recv.at[dx], r.sib_s.at[dx], r.sib_r.at[dx], me)

    def to_neighbour(side, half, extra):
        part = pl.ds(half * 128, 128)
        dx = 1 + 2 * side
        total = r.esum[dx, part] + r.es_recv[dx, part].astype(F32)
        if extra is not None:
            total = total + extra.astype(F32)
        r.nb_send[side, part] = total.astype(BF16)
        sends.push(
            r.nb_send.at[side, part], r.nb_recv.at[side, part],
            r.nb_s.at[side, half], r.nb_r.at[side, half], (right, left)[side],
        )

    partial(2)
    partial(1)
    from_sibling(2)
    r.x2_send[...] = (r.esum[2] + r.es_recv[2].astype(F32)).astype(BF16)
    sends.push(r.x2_send.at[pl.ds(0, 128)], r.rl_recv.at[0], r.rl_s.at[0], r.rl_r.at[0], right)
    sends.push(r.x2_send.at[pl.ds(128, 128)], r.rl_recv.at[1], r.rl_s.at[1], r.rl_r.at[1], left)
    for m in range(2):
        arrived(r.pq.at[m], r.pq_s.at[m], r.pq_r.at[m], me)

    @pl.loop(0, NZ)
    def _(n):
        for m in range(2):
            r.pq_sum[m, n] = (r.pk_sum[x % 2, m, n].astype(F32) + r.pq[m, n].astype(F32)).astype(BF16)

    for d in range(1, 4):
        phi, plo = me.along_y(d)
        sends.push(
            r.pq_sum.at[:, :, plo, phi], r.py.at[d - 1], r.py_s.at[d - 1], r.py_r.at[d - 1], me.device(ylo=plo, yhi=phi)
        )

    partial(3)
    from_sibling(1)
    to_neighbour(0, 1, None)
    from_sibling(3)
    to_neighbour(1, 0, None)

    @pl.loop(0, 4)
    def _(n):
        cols = pl.ds(pl.multiple_of(n * 256, 256), 256)
        product = dot(r.normed[:, :, cols].reshape(8 * ROWS, 256), r.dhidden[...].reshape(8 * ROWS, 512), ATB)
        r.gs[pl.ds(2 * n, 2)] = product.astype(BF16).reshape(2, 2, 2, 2, 16, 512)

    for d in range(1, NZ):
        to = me.along_z(d)
        sends.push(r.gs.at[to, :, 1, :], r.hz.at[d - 1], r.hz_s.at[d - 1], r.hz_r.at[d - 1], me.device(z=to))
    for d in range(1, 4):
        phi, plo = me.along_y(d)
        sends.push(
            r.gs.at[:, plo, 0, phi], r.gy.at[d - 1], r.gy_s.at[d - 1], r.gy_r.at[d - 1], me.device(ylo=plo, yhi=phi)
        )

    for side in range(2):
        arrived(r.rl_recv.at[side], r.rl_s.at[side], r.rl_r.at[side], me)
        to_neighbour(side, side, r.rl_recv[side])
    for d in range(1, 4):
        arrived(r.py.at[d - 1], r.py_s.at[d - 1], r.py_r.at[d - 1], me)

    @pl.loop(0, NZ)
    def _(n):
        for m in range(2):
            total = r.pq_sum[m, n, ylo, yhi].astype(F32)
            for d in range(3):
                total = total + r.py[d, m, n].astype(F32)
            r.pz_send[n, m] = total.astype(BF16)

    for d in range(1, NZ):
        to = me.along_z(d)
        sends.push(r.pz_send.at[to], r.pz.at[d - 1], r.pz_s.at[d - 1], r.pz_r.at[d - 1], me.device(z=to))

    partial(0)

    for d in range(1, 4):
        arrived(r.gy.at[d - 1], r.gy_s.at[d - 1], r.gy_r.at[d - 1], me)

    @pl.loop(0, NZ)
    def _(n):
        total = r.gs[n, ylo, 0, yhi].astype(F32)
        for d in range(3):
            total = total + r.gy[d, n].astype(F32)
        r.gz_send[n] = total.astype(BF16)

    for d in range(1, NZ):
        to = me.along_z(d)
        sends.push(r.gz_send.at[to], r.gz.at[d - 1], r.gz_s.at[d - 1], r.gz_r.at[d - 1], me.device(z=to))
    from_sibling(0)

    def finish(half):
        for side in range(2):
            arrived(r.nb_recv.at[side, pl.ds(half * 128, 128)], r.nb_s.at[side, half], r.nb_r.at[side, half], me)
        for n in range(2):
            part = pl.ds(half * 128 + n * 64, 64)
            upstream = (
                r.esum[0, part]
                + r.es_recv[0, part].astype(F32)
                + r.nb_recv[0, part].astype(F32)
                + r.nb_recv[1, part].astype(F32)
            )
            normal, inverse = normalize(r.tokr[part].astype(F32))
            first = jnp.mean(upstream, axis=-1, keepdims=True)
            second = jnp.mean(upstream * normal, axis=-1, keepdims=True)
            r.grad[part] = (inverse * (upstream - first - normal * second) + r.cotr[part].astype(F32)).astype(BF16)

        @pl.when(me.moved)
        def _():
            swap_grad[half].start()

        @pl.when(stays)
        def _():
            part = pl.ds(half * 128, 128)
            tok_grad[part] = r.grad[part]

    finish(0)
    finish(1)

    for d in range(1, NZ):
        arrived(r.hz.at[d - 1], r.hz_s.at[d - 1], r.hz_r.at[d - 1], me)
    for n in range(2):
        total = r.gs[z, n, 1].astype(F32)
        for d in range(7):
            total = total + r.hz[d, n].astype(F32)
        r.hy_send[n] = total.astype(BF16)
    for d in range(1, 4):
        phi, plo = me.along_y(d)
        sends.push(
            r.hy_send.at[plo, phi], r.hy.at[d - 1], r.hy_s.at[d - 1], r.hy_r.at[d - 1], me.device(ylo=plo, yhi=phi)
        )

    for d in range(1, NZ):
        arrived(r.pz.at[d - 1], r.pz_s.at[d - 1], r.pz_r.at[d - 1], me)
    total = r.pz_send[z].astype(F32)
    for d in range(1, NZ):
        total = total + r.pz[d - 1].astype(F32)
    for px in range(4):
        for b in range(4):
            r.px_f[px, b * 4 : b * 4 + 4, :] = total[b // 2, px * 4 : px * 4 + 4, b % 2 * HD : (b % 2 + 1) * HD]
    r.px_recv[x] = r.px_f[x]
    for d in range(1, 4):
        pk, px = me.row(0, d)
        sends.push(r.px_f.at[px], r.px_recv.at[x], r.px_s.at[d - 1], r.px_r.at[d - 1], me.device(x=px))

    for d in range(1, NZ):
        arrived(r.gz.at[d - 1], r.gz_s.at[d - 1], r.gz_r.at[d - 1], me)
    for d in range(1, 4):
        arrived(r.hy.at[d - 1], r.hy_s.at[d - 1], r.hy_r.at[d - 1], me)
    total = r.gz_send[z].astype(F32)
    for d in range(7):
        total = total + r.gz[d].astype(F32)
    other = r.hy_send[ylo, yhi].astype(F32)
    for d in range(3):
        other = other + r.hy[d].astype(F32)
    for c in range(2):
        for px in range(4):
            for b in range(4):
                r.gx_f[c * 4 + px, b * 4 : b * 4 + 4, :] = (total, other)[c][
                    px * 4 : px * 4 + 4, b * HD : (b + 1) * HD
                ]
    r.gx_recv[w] = r.gx_f[w]
    for d in range(1, 8):
        pk, px = me.row(d // 4, d % 4)
        sends.push(
            r.gx_f.at[pk * 4 + px], r.gx_recv.at[w], r.gx_s.at[d - 1], r.gx_r.at[d - 1], me.device(k=pk, x=px)
        )

    for d in range(1, 4):
        arrived(r.px_recv.at[(x + 4 - d) % 4], r.px_s.at[d - 1], r.px_r.at[d - 1], me)
    for c in range(2):
        total = r.px_recv[c] + r.px_recv[c + 2]
        for n in range(4):
            b = n // 2 * 4 + c * 2 + n % 2
            wo_grad[:, b * HD : (b + 1) * HD] = total[n * 4 : n * 4 + 4]
    for d in range(1, 8):
        sk, sx = row_source(d)
        arrived(r.gx_recv.at[sk * 4 + sx], r.gx_s.at[d - 1], r.gx_r.at[d - 1], me)
    for src in range(8):
        h = 2 * (src % 4) + src // 4
        for b in range(4):
            wi_grad[:, b * D + h * HD : b * D + (h + 1) * HD] = r.gx_recv[src, b * 4 : b * 4 + 4, :]
    sends.drain()
    for one in to_right + to_left + to_sibling + list(relay.values()) + list(relay_sibling.values()):
        one.wait_send()

    @pl.when(me.moved)
    def _():
        for one in swap_tok:
            one.wait_send()
        swap_cot.wait_send()
        swap_lay.wait()
        for one in swap_grad:
            one.wait()


def local(tokens, lengths, in_weight, out_weight, cotangent):
    anywhere = pl.BlockSpec(memory_space=pl.ANY)
    shapes = [((ROWS, D), BF16), ((ROWS, D), BF16), ((4, 4 * D), F32), ((4, D), F32)]
    scratch = [pltpu.VMEM(shape, kind) for shape, kind in BUFFERS.values()]
    for shape in SEMAPHORES.values():
        scratch += [DMA(shape), DMA(shape)]
    return tuple(
        pl.pallas_call(
            kernel,
            out_shape=[jax.ShapeDtypeStruct(s, t) for s, t in shapes],
            in_specs=[anywhere, anywhere, VMEM, VMEM, VMEM],
            out_specs=[VMEM] * 4,
            scratch_shapes=scratch,
            compiler_params=pltpu.CompilerParams(
                collective_id=0, has_side_effects=True, vmem_limit_bytes=60 << 20
            ),
            name="layer",
        )(tokens, cotangent, in_weight, out_weight, lengths)
    )


def solution(mesh):
    both = P(("dp", "seq"), None)
    return jax.shard_map(
        local,
        mesh=mesh,
        in_specs=(both, P("dp", None), both, both, both),
        out_specs=(both, both, both, both),
        check_vma=False,
    )
```

```python
import functools

import jax
import jax.numpy as jnp
from jax import lax
from jax.experimental import pallas as pl
from jax.experimental.pallas import tpu as pltpu
from jax.sharding import PartitionSpec as P

F32 = jnp.float32
BF16 = jnp.bfloat16
MESH = pl.DeviceIdType.MESH
DMA = pltpu.SemaphoreType.DMA

D = 1024
HEADS = 8
HD = 128
ROWS = 256
NZ = 8
epsilon = 1e-05
HALF_FACTOR = 0.5 * HD ** (-0.5)
VMEM = pl.BlockSpec(memory_space=pltpu.VMEM)
ABT = (((1,), (1,)), ((), ()))
ATB = (((0,), (0,)), ((), ()))


def dot(a, b, dims=(((1,), (0,)), ((), ()))):
    return lax.dot_general(a, b, dims, preferred_element_type=F32)


class Place:
    def __init__(self):
        g = lax.axis_index("dp")
        s = lax.axis_index("seq")
        self.z, self.ylo, self.k = g // 4, (g // 2) % 2, g % 2
        self.yhi, self.x = s // 4, s % 4
        self.w = self.k * 4 + self.x
        self.head = 2 * self.x + self.k
        self.moved = self.k != self.yhi

    def device(self, z=None, ylo=None, k=None, yhi=None, x=None):
        z = self.z if z is None else z
        ylo = self.ylo if ylo is None else ylo
        k = self.k if k is None else k
        yhi = self.yhi if yhi is None else yhi
        x = self.x if x is None else x
        return (z * 4 + ylo * 2 + k, yhi * 4 + x)

    def row(self, dk, dx):
        return (self.k + dk) % 2, (self.x + dx) % 4

    def along_z(self, d):
        return (self.z + d) % NZ

    def along_y(self, d):
        y = (self.yhi * 2 + self.ylo + d) % 4
        return y // 2, y % 2

    def partner(self):
        return self.device(k=self.yhi, yhi=self.k)

    def sibling(self):
        return self.device(k=1 - self.k)

    def row_peers(self):
        peers = []
        for d in range(1, 8):
            k, x = self.row(d // 4, d % 4)
            peers.append(self.device(k=k, x=x))
        return peers

    def zy_peers(self):
        peers = [self.device(z=self.along_z(d)) for d in range(1, NZ)]
        for d in range(1, 4):
            yhi, ylo = self.along_y(d)
            peers.append(self.device(ylo=ylo, yhi=yhi))
        return peers


def greet(me, peers, meanwhile):
    barrier = pltpu.get_barrier_semaphore()
    for peer in peers:
        pl.semaphore_signal(barrier, inc=1, device_id=peer, device_id_type=MESH)

    @pl.when(me.moved)
    def _():
        pl.semaphore_signal(barrier, inc=1, device_id=me.partner(), device_id_type=MESH)

    meanwhile()
    pl.semaphore_wait(barrier, len(peers) + me.moved.astype(jnp.int32))


def copy(src, dst, send, recv, to):
    return pltpu.make_async_remote_copy(
        src_ref=src, dst_ref=dst, send_sem=send, recv_sem=recv, device_id=to, device_id_type=MESH
    )


class Sends:
    def __init__(self):
        self.started = []

    def push(self, src, dst, send, recv, to):
        one = copy(src, dst, send, recv, to)
        one.start()
        self.started.append(one)

    def drain(self):
        for one in self.started:
            one.wait_send()


def arrived(ref, send, recv, me):
    copy(ref, ref, send, recv, me.sibling()).wait_recv()


def normalize(values):
    centre = values - jnp.mean(values, axis=-1, keepdims=True)
    inverse = lax.rsqrt(jnp.mean(centre * centre, axis=-1, keepdims=True) + epsilon)
    return centre * inverse, inverse


def first_of(position, lens):
    e0 = lens[0:1, 0:1]
    e1 = e0 + lens[0:1, 1:2]
    e2 = e1 + lens[0:1, 2:3]
    zero = jnp.zeros_like(position)
    start = jnp.where(position >= e0, e0, zero)
    start = jnp.where(position >= e1, e1, start)
    return jnp.where(position >= e2, e2, start)


BUFFERS = {
    "tokr": ((ROWS, D), BF16), "cotr": ((ROWS, D), BF16),
    "len_send": ((8, 128), jnp.int32), "len_recv": ((8, 128), jnp.int32), "lens": ((8, 128), jnp.int32),
    "wi_f": ((8, 16, 128), F32), "wi_send": ((8, 16, 128), BF16), "wi_recv": ((8, 16, 128), BF16),
    "wi_asm": ((2, 16, 512), F32),
    "wo_f": ((2, 16, 128), F32), "wo_send": ((2, 16, 128), BF16), "wo_recv": ((4, 16, 128), BF16),
    "wo_asm": ((2, 16, 256), F32),
    "win": ((NZ, 2, 2, 2, 16, 512), BF16), "wout": ((2, 2, NZ, 2, 2, 2, 16, 256), BF16),
    "normed": ((8, ROWS, D), BF16), "gated": ((8, ROWS, 512), BF16), "slope": ((8, ROWS, 512), BF16),
    "dsend": ((8, ROWS, HD), BF16), "dmix": ((8, ROWS, HD), BF16),
    "attn": ((8, ROWS, HD), BF16), "centre": ((8, ROWS, HD), F32), "dpart": ((4, ROWS, 256), F32),
    "stats_a": ((2, 8, ROWS), F32), "every_a": ((8, 2, 8, ROWS), F32),
    "stats_b": ((2, 8, ROWS), F32), "every_b": ((8, 2, 8, ROWS), F32),
    "comb": ((128, ROWS), F32), "msend": ((8, ROWS, HD), BF16), "mixed": ((8, ROWS, HD), BF16),
    "dattn": ((8, ROWS, HD), BF16), "dhidden": ((8, ROWS, 512), BF16), "dquery": ((8, ROWS, HD), F32),
    "lay": ((ROWS, D), BF16), "grad": ((ROWS, D), BF16),
    "esum": ((4, ROWS, D), F32), "es_send": ((4, ROWS, D), BF16), "es_recv": ((4, ROWS, D), BF16),
    "x2_send": ((ROWS, D), BF16), "rl_recv": ((2, 128, D), BF16),
    "nb_send": ((2, ROWS, D), BF16), "nb_recv": ((2, ROWS, D), BF16),
    "gs": ((NZ, 2, 2, 2, 16, 512), BF16),
    "gy": ((3, NZ, 16, 512), BF16), "gz_send": ((NZ, 16, 512), BF16), "gz": ((7, 16, 512), BF16),
    "hz": ((7, 2, 2, 16, 512), BF16), "hy_send": ((2, 2, 16, 512), BF16), "hy": ((3, 16, 512), BF16),
    "gx_f": ((8, 16, 128), F32), "gx_recv": ((8, 16, 128), F32),
    "ps": ((2, 2, NZ, 2, 2, 2, 16, 256), BF16), "pc": ((2, 2, NZ, 2, 2, 16, 256), BF16),
    "pk_sum": ((2, 2, NZ, 2, 2, 16, 256), BF16), "pq": ((2, NZ, 2, 2, 16, 256), BF16),
    "pq_sum": ((2, NZ, 2, 2, 16, 256), BF16),
    "py": ((3, 2, NZ, 16, 256), BF16), "pz_send": ((NZ, 2, 16, 256), BF16), "pz": ((7, 2, 16, 256), BF16),
    "px_f": ((4, 16, 128), F32), "px_recv": ((4, 16, 128), F32),
}
SEMAPHORES = {
    "load": (2,), "swap": (6,), "xi": (7,), "xo": (3,), "zi": (7,), "zo": (7,), "yi": (3,), "yo": (3,), "xq": (2,), "core": (3,),
    "zj": (7,), "yj": (3,),
    "ag": (8, 4), "fw": (4, 4), "dm": (7,), "sa": (7,), "sb": (7,), "mx": (7,), "sib": (4,), "rl": (2,), "nb": (2, 2),
    "gy": (3,), "gz": (7,), "hy": (3,), "hz": (7,), "gx": (7,),
    "pc": (1,), "pq": (2,), "py": (3,), "pz": (7,), "px": (3,), "sw": (3,),
}


class Refs:
    def __init__(self, buffers, semaphores):
        for name, ref in zip(BUFFERS, buffers):
            setattr(self, name, ref)
        for n, name in enumerate(SEMAPHORES):
            setattr(self, name + "_s", semaphores[2 * n])
            setattr(self, name + "_r", semaphores[2 * n + 1])


def project(r, block):
    left = r.normed[block]
    for n in range(2):
        cols = pl.ds(n * 256, 256)
        hidden = dot(left, r.win[:, :, :, :, :, cols].reshape(D, 256))
        sigma = 0.5 + 0.5 * jnp.tanh(0.5 * hidden)
        value = hidden * sigma
        r.gated[block, :, cols] = value.astype(BF16)
        r.slope[block, :, cols] = (sigma + value * (1.0 - sigma)).astype(BF16)


def attend(r, i, reach):
    query = r.gated[i, :, 256:384]
    pos = i * ROWS + lax.broadcasted_iota(jnp.int32, (ROWS, 1), 0)
    start = first_of(pos, r.lens)
    total = jnp.zeros((ROWS, HD), F32)
    for off in range(reach + 1):
        j = i - off
        half = dot(query, r.gated[j, :, 384:512], ABT) * HALF_FACTOR
        weights = half + half * jnp.tanh(half)
        other = j * ROWS + lax.broadcasted_iota(jnp.int32, (ROWS, ROWS), 1)
        allowed = other >= start
        if off == 0:
            allowed = allowed & (other <= pos)
        weights = jnp.where(allowed, weights, 0.0).astype(BF16)
        total = total + dot(weights, r.gated[j, :, 128:256])
    r.attn[i] = total.astype(BF16)


def two_columns(first, second):
    lane = lax.broadcasted_iota(jnp.int32, (ROWS, HD), 1)
    return jnp.where(lane == 0, first, jnp.where(lane == 1, second, 0.0)).T[0:2]


def attn_stats(r, quad, n):
    i = 4 * quad + n
    value = r.attn[i].astype(F32)
    mean = jnp.mean(value, axis=-1, keepdims=True)
    centre = value - mean
    r.centre[i] = centre
    r.stats_a[quad, 2 * n : 2 * n + 2] = two_columns(mean, jnp.sum(centre * centre, axis=-1, keepdims=True))


def upstream_stats(r, quad, n):
    i = 4 * quad + n
    upstream = r.dmix[i].astype(F32) * r.gated[i, :, 0:128].astype(F32)
    r.stats_b[quad, 2 * n : 2 * n + 2] = two_columns(
        jnp.sum(upstream, axis=-1, keepdims=True), jnp.sum(upstream * r.centre[i], axis=-1, keepdims=True)
    )


def gate_rows(r, quad, n):
    i = 4 * quad + n
    mean, second = (r.every_a[:, quad, 2 * n + m, :] for m in range(2))
    total, cross = (r.every_b[:, quad, 2 * n + m, :] for m in range(2))
    middle = jnp.mean(mean, axis=0, keepdims=True)
    apart = mean - middle
    variance = jnp.sum(second + HD * apart * apart, axis=0, keepdims=True) / D
    inverse = lax.rsqrt(variance + epsilon)
    first = jnp.sum(total, axis=0, keepdims=True) / D
    other = inverse * jnp.sum(cross + apart * total, axis=0, keepdims=True) / D
    r.comb[0:1, :] = middle
    r.comb[1:2, :] = inverse
    r.comb[2:3, :] = first
    r.comb[3:4, :] = other
    turned = r.comb[...].T
    middle, inverse, first, other = (turned[:, n : n + 1] for n in range(4))
    upper = r.gated[i, :, 0:128].astype(F32)
    through = r.dmix[i].astype(F32)
    normal = (r.attn[i].astype(F32) - middle) * inverse
    r.msend[i] = (normal * upper).astype(BF16)
    upstream = through * upper
    r.dattn[i] = (inverse * (upstream - first - normal * other)).astype(BF16)
    r.dhidden[i, :, 0:128] = (through * normal * r.slope[i, :, 0:128].astype(F32)).astype(BF16)


def attend_back(r, j, reach):
    key = r.gated[j, :, 384:512]
    value = r.gated[j, :, 128:256]
    other = j * ROWS + lax.broadcasted_iota(jnp.int32, (ROWS, ROWS), 0)
    dkey = jnp.zeros((ROWS, HD), F32)
    dvalue = jnp.zeros((ROWS, HD), F32)
    for off in range(reach + 1):
        i = j + off
        query = r.gated[i, :, 256:384]
        grad = r.dattn[i]
        half = dot(key, query, ABT) * HALF_FACTOR
        pos = i * ROWS + lax.broadcasted_iota(jnp.int32, (1, ROWS), 1)
        allowed = other >= first_of(pos, r.lens)
        if off == 0:
            allowed = allowed & (other <= pos)
        double = jnp.where(allowed, 1.0 + jnp.tanh(half), 0.0)
        weights = half * double
        bend = double + weights * (2.0 - double)
        dscores = (dot(value, grad, ABT) * bend).astype(BF16)
        dvalue = dvalue + dot(weights.astype(BF16), grad)
        dkey = dkey + dot(dscores, query)
        r.dquery[i] += dot(dscores, key, ATB)
    r.dhidden[j, :, 128:256] = (dvalue * r.slope[j, :, 128:256].astype(F32)).astype(BF16)
    r.dhidden[j, :, 384:512] = (dkey * HALF_FACTOR * r.slope[j, :, 384:512].astype(F32)).astype(BF16)


def kernel(tok, cot, wi, wo, lengths, layer_out, tok_grad, wi_grad, wo_grad, *scratch):
    me = Place()
    z, ylo, k, yhi, x, w = me.z, me.ylo, me.k, me.yhi, me.x, me.w
    r = Refs(scratch[: len(BUFFERS)], scratch[len(BUFFERS) :])
    sends = Sends()
    right, left = me.device(x=(x + 1) % 4), me.device(x=(x + 3) % 4)
    stays = jnp.logical_not(me.moved)

    def row_source(d):
        return (k + 2 - d // 4) % 2, (x + 4 - d % 4) % 4

    load_tok = pltpu.make_async_copy(tok, r.tokr, r.load_r.at[0])
    load_cot = pltpu.make_async_copy(cot, r.cotr, r.load_r.at[1])

    @pl.when(stays)
    def _():
        load_tok.start()
        load_cot.start()

    def prepare():
        wide = wi[...].astype(F32)
        for h in range(HEADS):
            for b in range(4):
                r.wi_f[h, b * 4 : b * 4 + 4, :] = wide[:, b * D + h * HD : b * D + (h + 1) * HD]
        r.wi_send[...] = r.wi_f[...].astype(BF16)
        wide_o = wo[...].astype(F32)
        r.wo_f[...] = jnp.zeros_like(r.wo_f)
        for b in range(8):
            r.wo_f[b // 2 % 2, (b // 4 * 2 + b % 2) * 4 : (b // 4 * 2 + b % 2) * 4 + 4, :] = wide_o[:, b * HD : (b + 1) * HD]
        r.wo_send[...] = r.wo_f[...].astype(BF16)
        r.len_send[...] = jnp.zeros_like(r.len_send)
        r.len_send[0:1, 0:4] = lengths[...]

    greet(me, me.row_peers() + me.zy_peers(), prepare)

    swap_tok = [
        copy(tok.at[part], r.tokr.at[part], r.swap_s.at[n], r.swap_r.at[n], me.partner())
        for n, part in ((n, pl.ds(n * 64, 64)) for n in range(4))
    ]
    swap_cot = copy(cot, r.cotr, r.swap_s.at[4], r.swap_r.at[4], me.partner())

    for d in range(1, 8):
        pk, px = me.row(d // 4, d % 4)
        sends.push(
            r.wi_send.at[2 * px + pk], r.wi_recv.at[w], r.xi_s.at[d - 1], r.xi_r.at[d - 1], me.device(k=pk, x=px)
        )
    r.wi_recv[w] = r.wi_send[me.head]
    for d in range(1, 4):
        pk, px = me.row(0, d)
        sends.push(r.wo_send.at[px % 2], r.wo_recv.at[x], r.xo_s.at[d - 1], r.xo_r.at[d - 1], me.device(x=px))
    r.wo_recv[x] = r.wo_send[x % 2]

    @pl.when(me.moved)
    def _():
        for n in (0, 2, 1, 3):
            swap_tok[n].start()

    sends.push(r.len_send, r.len_recv, r.swap_s.at[5], r.swap_r.at[5], me.sibling())

    def norm_chunk(n):
        part = pl.ds(n * 64, 64)
        r.normed[w, part] = normalize(r.tokr[part].astype(F32))[0].astype(BF16)

    def rows_of(dx, n):
        return r.normed.at[k * 4 + (x + dx) % 4, pl.ds(n * 64, 64)]

    def onward(dx, n, slot, to):
        return copy(rows_of(dx, n), rows_of(dx, n), r.ag_s.at[slot, n], r.ag_r.at[slot, n], to)

    def across(dx, n):
        return copy(rows_of(dx, n), rows_of(dx, n), r.fw_s.at[dx, n], r.ag_r.at[4 + dx, n], me.sibling())

    to_right = [onward(0, n, 3, right) for n in range(4)]
    to_left = [onward(0, n, 1, left) for n in range(4)]
    to_sibling = [across(0, n) for n in range(4)]
    relay = {n: onward(3, n, 2, right) if n < 2 else onward(1, n, 2, left) for n in range(4)}
    relay_sibling = {n: across(3 if n < 2 else 1, n) for n in range(4)}

    def send_chunk(n):
        (to_right if n < 2 else to_left)[n].start()
        to_sibling[n].start()

    def send_rest():
        for n in (2, 3):
            to_right[n].start()
            to_left[n - 2].start()

    def take_first():
        for n in (0, 2, 1, 3):
            slot = 3 if n < 2 else 1
            arrived(rows_of(slot, n), r.ag_s.at[slot, n], r.ag_r.at[slot, n], me)
            relay[n].start()
            relay_sibling[n].start()

    def take(dx, n):
        part = rows_of(dx, n)
        arrived(part, r.ag_s.at[dx, n], r.ag_r.at[dx, n], me)
        sends.push(part, part, r.fw_s.at[dx, n], r.ag_r.at[4 + dx, n], me.sibling())

    @pl.when(stays)
    def _():
        load_tok.wait()
        for n in (0, 2, 1, 3):
            norm_chunk(n)
            send_chunk(n)
        send_rest()

    for d in range(1, 8):
        sk, sx = row_source(d)
        arrived(r.wi_recv.at[sk * 4 + sx], r.xi_s.at[d - 1], r.xi_r.at[d - 1], me)
    for src in range(8):
        piece = r.wi_recv[src].astype(F32)
        for b in range(4):
            r.wi_asm[src // 4, (src % 4) * 4 : (src % 4) * 4 + 4, b * HD : (b + 1) * HD] = piece[b * 4 : b * 4 + 4]
    for c in range(2):
        r.win[z, ylo, c, yhi] = r.wi_asm[c].astype(BF16)
    for d in range(1, 4):
        phi, plo = me.along_y(d)
        part = r.win.at[z, ylo, 1, yhi]
        sends.push(part, part, r.yj_s.at[d - 1], r.yj_r.at[d - 1], me.device(ylo=plo, yhi=phi))
    for d in range(1, NZ):
        part = r.win.at[z, ylo, 0, yhi]
        sends.push(part, part, r.zi_s.at[d - 1], r.zi_r.at[d - 1], me.device(z=me.along_z(d)))

    for d in range(1, 4):
        arrived(r.wo_recv.at[(x + 4 - d) % 4], r.xo_s.at[d - 1], r.xo_r.at[d - 1], me)
    for src in range(4):
        piece = r.wo_recv[src].astype(F32)
        for b in range(4):
            r.wo_asm[b // 2, src * 4 : src * 4 + 4, b % 2 * HD : (b % 2 + 1) * HD] = piece[b * 4 : b * 4 + 4]
    for n in range(2):
        r.wout[x % 2, n, z, ylo, k, yhi] = r.wo_asm[n].astype(BF16)
    for d in range(1, NZ):
        part = r.wout.at[x % 2, :, z, ylo, k, yhi]
        sends.push(part, part, r.zo_s.at[d - 1], r.zo_r.at[d - 1], me.device(z=me.along_z(d)))

    @pl.when(stays)
    def _():
        take_first()

    @pl.when(me.moved)
    def _():
        for n in (0, 2, 1, 3):
            swap_tok[n].wait_recv()
            norm_chunk(n)
            send_chunk(n)
        send_rest()

    for d in range(1, 4):
        shi, slo = me.along_y(4 - d)
        arrived(r.win.at[z, slo, 1, shi], r.yj_s.at[d - 1], r.yj_r.at[d - 1], me)
    for d in range(1, NZ):
        part = r.win.at[z, :, 1, :]
        sends.push(part, part, r.zj_s.at[d - 1], r.zj_r.at[d - 1], me.device(z=me.along_z(d)))

    for d in range(1, NZ):
        arrived(r.win.at[(z + NZ - d) % NZ, ylo, 0, yhi], r.zi_s.at[d - 1], r.zi_r.at[d - 1], me)
    for d in range(1, 4):
        phi, plo = me.along_y(d)
        part = r.win.at[:, ylo, 0, yhi]
        sends.push(part, part, r.yi_s.at[d - 1], r.yi_r.at[d - 1], me.device(ylo=plo, yhi=phi))

    for d in range(1, NZ):
        arrived(r.wout.at[x % 2, :, (z + NZ - d) % NZ, ylo, k, yhi], r.zo_s.at[d - 1], r.zo_r.at[d - 1], me)
    for d in range(1, 4):
        phi, plo = me.along_y(d)
        part = r.wout.at[x % 2, :, :, ylo, k, yhi]
        sends.push(part, part, r.yo_s.at[d - 1], r.yo_r.at[d - 1], me.device(ylo=plo, yhi=phi))

    @pl.when(me.moved)
    def _():
        swap_cot.start()
        take_first()

    for dx, n in ((3, 2), (1, 0), (3, 3), (1, 1), (2, 0), (2, 2), (2, 1), (2, 3)):
        take(dx, n)
    arrived(r.len_recv, r.swap_s.at[5], r.swap_r.at[5], me)
    r.lens[...] = jnp.where(me.moved, r.len_recv[...], r.len_send[...])
    for d in range(1, 4):
        shi, slo = me.along_y(4 - d)
        arrived(r.win.at[:, slo, 0, shi], r.yi_s.at[d - 1], r.yi_r.at[d - 1], me)
    for d in range(1, NZ):
        arrived(r.win.at[(z + NZ - d) % NZ, :, 1, :], r.zj_s.at[d - 1], r.zj_r.at[d - 1], me)

    @pl.loop(0, 4)
    def _(i):
        project(r, k * 4 + i)

    for d in range(1, 4):
        shi, slo = me.along_y(4 - d)
        arrived(r.wout.at[x % 2, :, :, slo, k, shi], r.yo_s.at[d - 1], r.yo_r.at[d - 1], me)
    for n, to in ((0, right), (1, left)):
        part = r.wout.at[x % 2, n, :, :, k]
        sends.push(part, part, r.xq_s.at[n], r.xq_r.at[n], to)
    part = r.wout.at[x % 2, :, :, :, k]
    sends.push(part, part, r.core_s.at[2], r.core_r.at[2], me.sibling())
    for dx in range(4):
        for n in range(4):
            arrived(
                r.normed.at[(1 - k) * 4 + (x + dx) % 4, pl.ds(n * 64, 64)],
                r.fw_s.at[dx, n], r.ag_r.at[4 + dx, n], me,
            )

    @pl.loop(0, 4)
    def _(i):
        project(r, (1 - k) * 4 + i)

    for i in range(4):
        attend(r, i, i)

    @pl.when(me.moved)
    def _():
        swap_cot.wait_recv()

    @pl.when(stays)
    def _():
        load_cot.wait()

    arrived(r.wout.at[x % 2, :, :, :, 1 - k], r.core_s.at[2], r.core_r.at[2], me)
    def through(px, side):
        pair = jnp.zeros((ROWS, 256), F32)
        for m in range(2):
            cols = pl.ds(pl.multiple_of((side + 2 * m) * 256, 256), 256)
            pair = pair + dot(r.cotr[:, cols], r.wout[side, m, pl.ds(2 * px, 2)].reshape(256, 256), ABT)
        return pair

    for dx in range(4):
        r.dpart[dx] = through((x + dx) % 4, x % 2)

    for n in range(2):
        part = r.wout.at[(x + 1) % 2, n, :, :, k]
        arrived(part, r.xq_s.at[n], r.xq_r.at[n], me)
        sends.push(part, part, r.core_s.at[n], r.core_r.at[n], me.sibling())

    @pl.loop(4, 6)
    def _(i):
        attend(r, i, 4)

    for n in range(2):
        arrived(r.wout.at[(x + 1) % 2, n, :, :, 1 - k], r.core_s.at[n], r.core_r.at[n], me)
    for dx in (2, 1, 3, 0):
        px = (x + dx) % 4
        pair = r.dpart[dx] + through(px, (x + 1) % 2)
        r.dsend[2 * px] = pair[:, :HD].astype(BF16)
        r.dsend[2 * px + 1] = pair[:, HD:].astype(BF16)
        for dk in range(2):
            d = 4 * dk + dx
            if d:
                pk = (k + dk) % 2
                sends.push(
                    r.dsend.at[2 * px + pk], r.dmix.at[w], r.dm_s.at[d - 1], r.dm_r.at[d - 1], me.device(k=pk, x=px)
                )
    r.dmix[w] = r.dsend[me.head]

    @pl.loop(6, 8)
    def _(i):
        attend(r, i, 4)

    @pl.loop(0, 2)
    def _(quad):
        for n in range(4):
            attn_stats(r, quad, n)

    for d in range(1, 8):
        pk, px = me.row(d // 4, d % 4)
        sends.push(r.stats_a, r.every_a.at[w], r.sa_s.at[d - 1], r.sa_r.at[d - 1], me.device(k=pk, x=px))
    r.every_a[w] = r.stats_a[...]
    r.comb[...] = jnp.zeros_like(r.comb)
    r.dquery[...] = jnp.zeros_like(r.dquery)
    for d in range(1, 8):
        sk, sx = row_source(d)
        arrived(r.dmix.at[sk * 4 + sx], r.dm_s.at[d - 1], r.dm_r.at[d - 1], me)

    @pl.loop(0, 2)
    def _(quad):
        for n in range(4):
            upstream_stats(r, quad, n)

    for d in range(1, 8):
        pk, px = me.row(d // 4, d % 4)
        sends.push(r.stats_b, r.every_b.at[w], r.sb_s.at[d - 1], r.sb_r.at[d - 1], me.device(k=pk, x=px))
    r.every_b[w] = r.stats_b[...]
    for d in range(1, 8):
        sk, sx = row_source(d)
        arrived(r.every_a.at[sk * 4 + sx], r.sa_s.at[d - 1], r.sa_r.at[d - 1], me)
    for d in range(1, 8):
        sk, sx = row_source(d)
        arrived(r.every_b.at[sk * 4 + sx], r.sb_s.at[d - 1], r.sb_r.at[d - 1], me)

    @pl.loop(0, 2)
    def _(quad):
        for n in range(4):
            gate_rows(r, quad, n)

    r.mixed[me.head] = r.msend[w]
    for d in range(1, 8):
        pk, px = me.row(d // 4, d % 4)
        sends.push(
            r.msend.at[pk * 4 + px], r.mixed.at[me.head], r.mx_s.at[d - 1], r.mx_r.at[d - 1], me.device(k=pk, x=px)
        )

    @pl.loop(0, 4)
    def _(j):
        attend_back(r, j, 4)

    for d in range(1, 8):
        sk, sx = row_source(d)
        arrived(r.mixed.at[2 * sx + sk], r.mx_s.at[d - 1], r.mx_r.at[d - 1], me)

    @pl.loop(0, 4)
    def _(n):
        pair = jnp.concatenate([r.mixed[2 * n], r.mixed[2 * n + 1]], axis=1)
        product = dot(pair, r.cotr[...], ATB).astype(BF16)
        for q in range(4):
            r.ps[q % 2, q // 2, pl.ds(2 * n, 2)] = product[:, q * 256 : (q + 1) * 256].reshape(2, 2, 2, 2, 16, 256)

    sends.push(r.ps.at[:, :, :, :, 1 - k], r.pc, r.pc_s.at[0], r.pc_r.at[0], me.sibling())

    joined = jnp.concatenate([r.mixed[h] for h in range(HEADS)], axis=1)
    for n in range(4):
        cols = pl.ds(n * 256, 256)
        product = dot(joined, r.wout[n % 2, n // 2].reshape(D, 256))
        r.lay[:, cols] = (product + r.tokr[:, cols].astype(F32)).astype(BF16)
    swap_lay = copy(r.lay, layer_out, r.sw_s.at[0], r.sw_r.at[0], me.partner())
    swap_grad = [
        copy(r.grad.at[part], tok_grad.at[part], r.sw_s.at[n], r.sw_r.at[n], me.partner())
        for n, part in ((1, pl.ds(0, 128)), (2, pl.ds(128, 128)))
    ]

    @pl.when(stays)
    def _():
        layer_out[...] = r.lay[...]

    @pl.when(me.moved)
    def _():
        swap_lay.start()

    attend_back(r, 4, 3)
    arrived(r.pc, r.pc_s.at[0], r.pc_r.at[0], me)

    @pl.loop(0, NZ)
    def _(n):
        for q in range(4):
            c, m = q % 2, q // 2
            r.pk_sum[c, m, n] = (r.ps[c, m, n, :, k].astype(F32) + r.pc[c, m, n].astype(F32)).astype(BF16)

    for n, to in ((0, right), (1, left)):
        sends.push(r.pk_sum.at[(x + 1) % 2, n], r.pq.at[n], r.pq_s.at[n], r.pq_r.at[n], to)

    for j in range(5, 8):
        attend_back(r, j, 7 - j)

    @pl.loop(0, 8)
    def _(i):
        r.dhidden[i, :, 256:384] = (r.dquery[i] * HALF_FACTOR * r.slope[i, :, 256:384].astype(F32)).astype(BF16)

    def back_product(block, n):
        return dot(r.dhidden[block], r.win[pl.ds(2 * n, 2)].reshape(256, 512), ABT)

    def partial(dx):
        there = (1 - k) * 4 + (x + dx) % 4
        here = k * 4 + (x + dx) % 4

        @pl.loop(0, 4)
        def _(n):
            cols = pl.ds(pl.multiple_of(n * 256, 256), 256)
            r.es_send[dx, :, cols] = back_product(there, n).astype(BF16)

        sends.push(r.es_send.at[dx], r.es_recv.at[dx], r.sib_s.at[dx], r.sib_r.at[dx], me.sibling())

        @pl.loop(0, 4)
        def _(n):
            cols = pl.ds(pl.multiple_of(n * 256, 256), 256)
            r.esum[dx, :, cols] = back_product(here, n)

    def from_sibling(dx):
        arrived(r.es_recv.at[dx], r.sib_s.at[dx], r.sib_r.at[dx], me)

    def to_neighbour(side, half, extra):
        part = pl.ds(half * 128, 128)
        dx = 1 + 2 * side
        total = r.esum[dx, part] + r.es_recv[dx, part].astype(F32)
        if extra is not None:
            total = total + extra.astype(F32)
        r.nb_send[side, part] = total.astype(BF16)
        sends.push(
            r.nb_send.at[side, part], r.nb_recv.at[side, part],
            r.nb_s.at[side, half], r.nb_r.at[side, half], (right, left)[side],
        )

    partial(2)
    partial(1)
    from_sibling(2)
    r.x2_send[...] = (r.esum[2] + r.es_recv[2].astype(F32)).astype(BF16)
    sends.push(r.x2_send.at[pl.ds(0, 128)], r.rl_recv.at[0], r.rl_s.at[0], r.rl_r.at[0], right)
    sends.push(r.x2_send.at[pl.ds(128, 128)], r.rl_recv.at[1], r.rl_s.at[1], r.rl_r.at[1], left)
    for m in range(2):
        arrived(r.pq.at[m], r.pq_s.at[m], r.pq_r.at[m], me)

    @pl.loop(0, NZ)
    def _(n):
        for m in range(2):
            r.pq_sum[m, n] = (r.pk_sum[x % 2, m, n].astype(F32) + r.pq[m, n].astype(F32)).astype(BF16)

    for d in range(1, 4):
        phi, plo = me.along_y(d)
        sends.push(
            r.pq_sum.at[:, :, plo, phi], r.py.at[d - 1], r.py_s.at[d - 1], r.py_r.at[d - 1], me.device(ylo=plo, yhi=phi)
        )

    partial(3)
    from_sibling(1)
    to_neighbour(0, 1, None)
    from_sibling(3)
    to_neighbour(1, 0, None)

    @pl.loop(0, 4)
    def _(n):
        cols = pl.ds(pl.multiple_of(n * 256, 256), 256)
        product = dot(r.normed[:, :, cols].reshape(8 * ROWS, 256), r.dhidden[...].reshape(8 * ROWS, 512), ATB)
        r.gs[pl.ds(2 * n, 2)] = product.astype(BF16).reshape(2, 2, 2, 2, 16, 512)

    for d in range(1, NZ):
        to = me.along_z(d)
        sends.push(r.gs.at[to, :, 1, :], r.hz.at[d - 1], r.hz_s.at[d - 1], r.hz_r.at[d - 1], me.device(z=to))
    for d in range(1, 4):
        phi, plo = me.along_y(d)
        sends.push(
            r.gs.at[:, plo, 0, phi], r.gy.at[d - 1], r.gy_s.at[d - 1], r.gy_r.at[d - 1], me.device(ylo=plo, yhi=phi)
        )

    for side in range(2):
        arrived(r.rl_recv.at[side], r.rl_s.at[side], r.rl_r.at[side], me)
        to_neighbour(side, side, r.rl_recv[side])
    for d in range(1, 4):
        arrived(r.py.at[d - 1], r.py_s.at[d - 1], r.py_r.at[d - 1], me)

    @pl.loop(0, NZ)
    def _(n):
        for m in range(2):
            total = r.pq_sum[m, n, ylo, yhi].astype(F32)
            for d in range(3):
                total = total + r.py[d, m, n].astype(F32)
            r.pz_send[n, m] = total.astype(BF16)

    for d in range(1, NZ):
        to = me.along_z(d)
        sends.push(r.pz_send.at[to], r.pz.at[d - 1], r.pz_s.at[d - 1], r.pz_r.at[d - 1], me.device(z=to))

    partial(0)

    for d in range(1, 4):
        arrived(r.gy.at[d - 1], r.gy_s.at[d - 1], r.gy_r.at[d - 1], me)

    @pl.loop(0, NZ)
    def _(n):
        total = r.gs[n, ylo, 0, yhi].astype(F32)
        for d in range(3):
            total = total + r.gy[d, n].astype(F32)
        r.gz_send[n] = total.astype(BF16)

    for d in range(1, NZ):
        to = me.along_z(d)
        sends.push(r.gz_send.at[to], r.gz.at[d - 1], r.gz_s.at[d - 1], r.gz_r.at[d - 1], me.device(z=to))
    from_sibling(0)

    def finish(half):
        for side in range(2):
            arrived(r.nb_recv.at[side, pl.ds(half * 128, 128)], r.nb_s.at[side, half], r.nb_r.at[side, half], me)
        for n in range(2):
            part = pl.ds(half * 128 + n * 64, 64)
            upstream = (
                r.esum[0, part]
                + r.es_recv[0, part].astype(F32)
                + r.nb_recv[0, part].astype(F32)
                + r.nb_recv[1, part].astype(F32)
            )
            normal, inverse = normalize(r.tokr[part].astype(F32))
            first = jnp.mean(upstream, axis=-1, keepdims=True)
            second = jnp.mean(upstream * normal, axis=-1, keepdims=True)
            r.grad[part] = (inverse * (upstream - first - normal * second) + r.cotr[part].astype(F32)).astype(BF16)

        @pl.when(me.moved)
        def _():
            swap_grad[half].start()

        @pl.when(stays)
        def _():
            part = pl.ds(half * 128, 128)
            tok_grad[part] = r.grad[part]

    finish(0)
    finish(1)

    for d in range(1, NZ):
        arrived(r.hz.at[d - 1], r.hz_s.at[d - 1], r.hz_r.at[d - 1], me)
    for n in range(2):
        total = r.gs[z, n, 1].astype(F32)
        for d in range(7):
            total = total + r.hz[d, n].astype(F32)
        r.hy_send[n] = total.astype(BF16)
    for d in range(1, 4):
        phi, plo = me.along_y(d)
        sends.push(
            r.hy_send.at[plo, phi], r.hy.at[d - 1], r.hy_s.at[d - 1], r.hy_r.at[d - 1], me.device(ylo=plo, yhi=phi)
        )

    for d in range(1, NZ):
        arrived(r.pz.at[d - 1], r.pz_s.at[d - 1], r.pz_r.at[d - 1], me)
    total = r.pz_send[z].astype(F32)
    for d in range(1, NZ):
        total = total + r.pz[d - 1].astype(F32)
    for px in range(4):
        for b in range(4):
            r.px_f[px, b * 4 : b * 4 + 4, :] = total[b // 2, px * 4 : px * 4 + 4, b % 2 * HD : (b % 2 + 1) * HD]
    r.px_recv[x] = r.px_f[x]
    for d in range(1, 4):
        pk, px = me.row(0, d)
        sends.push(r.px_f.at[px], r.px_recv.at[x], r.px_s.at[d - 1], r.px_r.at[d - 1], me.device(x=px))

    for d in range(1, NZ):
        arrived(r.gz.at[d - 1], r.gz_s.at[d - 1], r.gz_r.at[d - 1], me)
    for d in range(1, 4):
        arrived(r.hy.at[d - 1], r.hy_s.at[d - 1], r.hy_r.at[d - 1], me)
    total = r.gz_send[z].astype(F32)
    for d in range(7):
        total = total + r.gz[d].astype(F32)
    other = r.hy_send[ylo, yhi].astype(F32)
    for d in range(3):
        other = other + r.hy[d].astype(F32)
    for c in range(2):
        for px in range(4):
            for b in range(4):
                r.gx_f[c * 4 + px, b * 4 : b * 4 + 4, :] = (total, other)[c][
                    px * 4 : px * 4 + 4, b * HD : (b + 1) * HD
                ]
    r.gx_recv[w] = r.gx_f[w]
    for d in range(1, 8):
        pk, px = me.row(d // 4, d % 4)
        sends.push(
            r.gx_f.at[pk * 4 + px], r.gx_recv.at[w], r.gx_s.at[d - 1], r.gx_r.at[d - 1], me.device(k=pk, x=px)
        )

    for d in range(1, 4):
        arrived(r.px_recv.at[(x + 4 - d) % 4], r.px_s.at[d - 1], r.px_r.at[d - 1], me)
    for c in range(2):
        total = r.px_recv[c] + r.px_recv[c + 2]
        for n in range(4):
            b = n // 2 * 4 + c * 2 + n % 2
            wo_grad[:, b * HD : (b + 1) * HD] = total[n * 4 : n * 4 + 4]
    for d in range(1, 8):
        sk, sx = row_source(d)
        arrived(r.gx_recv.at[sk * 4 + sx], r.gx_s.at[d - 1], r.gx_r.at[d - 1], me)
    for src in range(8):
        h = 2 * (src % 4) + src // 4
        for b in range(4):
            wi_grad[:, b * D + h * HD : b * D + (h + 1) * HD] = r.gx_recv[src, b * 4 : b * 4 + 4, :]
    sends.drain()
    for one in to_right + to_left + to_sibling + list(relay.values()) + list(relay_sibling.values()):
        one.wait_send()

    @pl.when(me.moved)
    def _():
        for one in swap_tok:
            one.wait_send()
        swap_cot.wait_send()
        swap_lay.wait()
        for one in swap_grad:
            one.wait()


def hand_on(*refs):
    copies = [pltpu.make_async_copy(refs[n], refs[4 + n], refs[8].at[n]) for n in range(4)]
    for one in copies:
        one.start()
    for one in copies:
        one.wait()


def local(tokens, lengths, in_weight, out_weight, cotangent):
    anywhere = pl.BlockSpec(memory_space=pl.ANY)
    shapes = [((ROWS, D), BF16), ((ROWS, D), BF16), ((4, 4 * D), F32), ((4, D), F32)]
    scratch = [pltpu.VMEM(shape, kind) for shape, kind in BUFFERS.values()]
    for shape in SEMAPHORES.values():
        scratch += [DMA(shape), DMA(shape)]
    shapes = [jax.ShapeDtypeStruct(s, t) for s, t in shapes]
    results = (
        pl.pallas_call(
            kernel,
            out_shape=shapes,
            in_specs=[anywhere, anywhere, VMEM, VMEM, VMEM],
            out_specs=[VMEM] * 4,
            scratch_shapes=scratch,
            compiler_params=pltpu.CompilerParams(
                collective_id=0, has_side_effects=True, vmem_limit_bytes=60 << 20
            ),
            name="layer",
        )(tokens, cotangent, in_weight, out_weight, lengths)
    )
    return tuple(
        pl.pallas_call(
            hand_on,
            out_shape=shapes,
            in_specs=[VMEM] * 4,
            out_specs=[anywhere] * 4,
            scratch_shapes=[DMA((4,))],
            name="hand_on",
        )(*results)
    )


def solution(mesh):
    both = P(("dp", "seq"), None)
    return jax.shard_map(
        local,
        mesh=mesh,
        in_specs=(both, P("dp", None), both, both, both),
        out_specs=(both, both, both, both),
        check_vma=False,
    )
```
